512 devices in a mesh: phase: 64 (over x_lo, z, core), space: 8 (over x_hi, y).
Axes of the slice: x: 4 (x_hi: 2, x_lo: 2; x = x_hi * 2 + x_lo), y: 4, z: 16, core: 2. Of those that a mesh axis runs over, the one named last changes fastest.
Arguments:
- object_field: float32 [2, 64, 272, 2048], P(None, 'phase', None, 'space'), may hold values from -6 to 6
- split_field: float32 [2, 64, 272, 2048], P(None, 'phase', None, 'space'), may hold values from -6 to 6
- scaled_dual: float32 [2, 64, 272, 2048], P(None, 'phase', None, 'space'), may hold values from -4 to 4
- probe: float32 [2, 256, 256], replicated, may hold values from -6 to 6
- amplitudes: float32 [64, 48, 256, 256], P('phase', 'space'), may hold values from 0.1 to 4
- row_offsets: int32 [64, 48], P('phase', 'space'), may hold values from 0 to 16, as said below
- col_offsets: int32 [64, 48], P('phase', 'space'), may hold values from 0 to 255, as said below
Outputs:
- updated_object: float32 [2, 64, 272, 2048], P(None, 'phase', None, 'space')
- updated_split: float32 [2, 64, 272, 2048], P(None, 'phase', None, 'space')
- updated_dual: float32 [2, 64, 272, 2048], P(None, 'phase', None, 'space')
- probe_gradient: float32 [2, 256, 256], replicated
The draws below stay inside these ranges and needn't reach their ends.
Inputs may be any that keep to these rules, and one draw needn't show every extreme that they name: `row_offsets`: A scan position's rows lie inside the band. `col_offsets`: A scan position may reach into the next tile; positions of the last tile end inside it (offset at most 0).
All inputs are finite; a program needn't handle non-finite values.
Results may differ from the reference program's by a relative error of at most 0.0003.
Values sent between devices are 32-bit elements; how exact they have to be, the bound alone decides.
A program may use at most 64 MiB of HBM per device.

```python
import math
import jax
import jax.numpy as jnp
from jax import lax

PATCH = 256
OBJ_ROWS = 272
TILE_W = 256
PATCHES = 6
PHASES = 64
TILES = 8
BAND_W = 2048


def draw_row_offsets(key, part):
    key = jax.random.fold_in(key, 11)
    first, second = jax.random.split(key)
    count = TILES * PATCHES
    values = jax.random.randint(first, (PHASES, count), 0, OBJ_ROWS - PATCH + 1)
    chosen = jax.random.randint(second, (PHASES,), 0, count)
    column = lax.broadcasted_iota(jnp.int32, (PHASES, count), 1)
    values = jnp.where(column == chosen[:, None], OBJ_ROWS - PATCH, values)
    return values.astype(jnp.int32)


def draw_col_offsets(key, part):
    key = jax.random.fold_in(key, 23)
    first, second = jax.random.split(key)
    count = TILES * PATCHES
    values = jax.random.randint(first, (PHASES, count), 0, TILE_W)
    column = lax.broadcasted_iota(jnp.int32, (PHASES, count), 1)
    last_tile = column // PATCHES == TILES - 1
    values = jnp.where(last_tile, values % (TILE_W - PATCH + 1), values)
    chosen = jax.random.randint(second, (PHASES,), 0, (TILES - 1) * PATCHES)
    values = jnp.where(column == chosen[:, None], TILE_W - 1, values)
    return values.astype(jnp.int32)


def block_levels(rng, shape, pieces, least, top_value):
    level = 1.0
    for position, parts in pieces:
        steps = jax.random.uniform(jax.random.fold_in(jax.random.fold_in(rng, 6), position), (parts,), jnp.float32, least / len(pieces), top_value / len(pieces))
        level = level * jnp.repeat(jnp.exp(steps), shape[position] // parts).reshape((-1,) + (1,) * (len(shape) - 1 - position))
    return level


def centred(own_key, extent, deviation, bound, cuts=(), held_as=jnp.bfloat16):
    level = block_levels(own_key, extent, cuts, -0.22, 0.18) if cuts else 1.0
    result = jax.random.normal(own_key, extent, jnp.float32) * deviation * level
    return jnp.minimum(jnp.maximum(result, -bound), bound).astype(held_as)


def setup_inputs(seed: int = 0) -> dict:
    key_list = jax.random.split(jax.random.key(seed), 8)
    return {
        "object_field": centred(key_list[0], (2, PHASES, OBJ_ROWS, BAND_W), 1.0, 6.0, ((1, 64), (3, 8)), jnp.float32),
        "split_field": centred(key_list[1], (2, PHASES, OBJ_ROWS, BAND_W), 1.0, 6.0, ((1, 64), (3, 8)), jnp.float32),
        "scaled_dual": centred(key_list[2], (2, PHASES, OBJ_ROWS, BAND_W), 0.3, 4.0, ((1, 64), (3, 8)), jnp.float32),
        "probe": centred(key_list[3], (2, PATCH, PATCH), 1.0, 6.0, (), jnp.float32),
        "amplitudes": jnp.clip(jnp.exp(math.log(4.0) - 3.6888794 * jax.random.uniform(key_list[4], (PHASES, TILES * PATCHES, PATCH, PATCH), jnp.float32) ** block_levels(key_list[4], (PHASES, TILES * PATCHES, PATCH, PATCH), ((0, 64), (1, 8)), -0.2, 0.2)), 0.1, 4.0),
        "row_offsets": draw_row_offsets(jax.random.fold_in(key_list[7], 71), 0),
        "col_offsets": draw_col_offsets(jax.random.fold_in(key_list[7], 71), 0),
    }


amp_floor = 0.25
ridge = 1.0
tv_step = 0.25
shrink_level = 0.5

def stacked(values):
    return jnp.stack([jnp.real(values), jnp.imag(values)])

def reference(object_field, split_field, scaled_dual, probe, amplitudes, row_offsets, col_offsets):
    probe_c = lax.complex(probe[0], probe[1])
    probe_power = probe[0] * probe[0] + probe[1] * probe[1]

    def one_phase(inputs):
        field, amp_rows, rows_p, cols_p = inputs
        obj = lax.complex(field[0], field[1])

        def patch_step(slot, carry):
            numer, weight, grad = carry
            top = rows_p[slot].astype(jnp.int32)
            left = (slot // PATCHES * TILE_W + cols_p[slot]).astype(jnp.int32)
            piece = lax.dynamic_slice(obj, (top, left), (PATCH, PATCH))
            wave = probe_c * piece
            far = jnp.fft.fft2(wave, norm='ortho')
            magnitude = jnp.abs(far)
            fixed = far * (amp_rows[slot] / jnp.maximum(magnitude, amp_floor))
            change = jnp.fft.ifft2(fixed, norm='ortho') - wave
            current = lax.dynamic_slice(numer, (top, left), (PATCH, PATCH))
            numer = lax.dynamic_update_slice(numer, current + jnp.conj(probe_c) * change, (top, left))
            current_w = lax.dynamic_slice(weight, (top, left), (PATCH, PATCH))
            weight = lax.dynamic_update_slice(weight, current_w + probe_power, (top, left))
            grad = grad + jnp.conj(piece) * change
            return (numer, weight, grad)
        start = (jnp.zeros((OBJ_ROWS, BAND_W), obj.dtype), jnp.zeros((OBJ_ROWS, BAND_W), field.dtype), jnp.zeros((PATCH, PATCH), obj.dtype))
        numer, weight, grad = lax.fori_loop(0, TILES * PATCHES, patch_step, start)
        return (numer / (weight + ridge), grad)
    fields = jnp.moveaxis(object_field, 1, 0)
    data, grads = lax.map(one_phase, (fields, amplitudes, row_offsets, col_offsets))
    current = lax.complex(object_field[0], object_field[1])
    split_c = lax.complex(split_field[0], split_field[1])
    dual_c = lax.complex(scaled_dual[0], scaled_dual[1])
    resid = jnp.roll(current, -1, 0) - current - split_c + dual_c
    updated = current + data - tv_step * (jnp.roll(resid, 1, 0) - resid)
    joint = jnp.roll(updated, -1, 0) - updated + dual_c
    size_abs = jnp.abs(joint)
    new_split = joint * (jnp.maximum(size_abs - shrink_level, 0.0) / jnp.maximum(size_abs, shrink_level))
    new_dual = joint - new_split
    probe_gradient = lax.optimization_barrier(jnp.sum(grads, 0)) / jnp.sqrt(float(PHASES * TILES * PATCHES))
    return (stacked(updated), stacked(new_split), stacked(new_dual), stacked(probe_gradient))
```

```python
import functools
import math

import jax
import jax.numpy as jnp
import ml_dtypes
import numpy as np
from jax import lax
from jax.experimental import pallas as pl
from jax.experimental.pallas import tpu as pltpu
from jax.sharding import PartitionSpec as P

amp_floor = 0.25
ridge = 1.0
tv_step = 0.25
shrink_level = 0.5

SIDE = 256
HALF = 128
BAND = 272
SPILL = BAND - SIDE
CORES, Z_SIZE, X_LO, Y_SIZE, X_SIZE = 2, 16, 2, 4, 4
GRAD_ROWS = 1024
VMEM_BYTES = 50 * 1024 * 1024


def from_behind(block, axis, distance):
    devices = range(lax.axis_size(axis))
    route = [(i - distance, i) for i in devices if i - distance in devices]
    return lax.ppermute(block, axis, route)


def passed_along(value, axis, steps):
    count = lax.axis_size(axis)
    pairs = [(source, (source + steps) % count) for source in range(count)]
    return lax.ppermute(value, axis, pairs)


def two_parts(table):
    high = table.astype(ml_dtypes.bfloat16)
    low = (table - high.astype(np.float64)).astype(ml_dtypes.bfloat16)
    return np.stack([high, low])


def half_tables():
    place = np.arange(HALF)
    tables = []
    for odd in (0, 1):
        turns = ((2 * place[:, None] + odd) * place[None, :]) % SIDE
        angle = -2.0 * np.pi * turns / SIDE
        re = np.cos(angle) / math.sqrt(SIDE)
        im = np.sin(angle) / math.sqrt(SIDE)
        real_form = np.block([[re, -im], [im, re]])
        tables.append(two_parts(real_form))
        tables.append(two_parts(real_form.T))
    order = np.concatenate([np.arange(0, SIDE, 2), np.arange(1, SIDE, 2)])
    sorter = np.zeros((SIDE, SIDE), np.float32)
    sorter[order, np.arange(SIDE)] = 1.0
    return tables, sorter.astype(ml_dtypes.bfloat16)


def put_split(ref, rows, lanes, value):
    high = value.astype(jnp.bfloat16)
    ref[0, rows, lanes] = high
    ref[1, rows, lanes] = (value - high.astype(jnp.float32)).astype(jnp.bfloat16)


def dot(a, b):
    return jnp.dot(a, b, preferred_element_type=jnp.float32)


def table_dot(table, data):
    return dot(table[0], data[0]) + dot(table[1], data[0]) + dot(table[0], data[1])


def dot_table(data, table):
    return dot(data[0], table[0]) + dot(data[1], table[0]) + dot(data[0], table[1])


def rolled_probe(source, target, left):
    step = 64
    for start in range(0, SIDE, step):
        turned = pltpu.roll(source[start : start + step, :], left, 1)
        for side in range(2):
            lanes = slice(side * HALF, (side + 1) * HALF)
            target[side, SPILL + start : SPILL + start + step, :] = turned[:, lanes]
            if start + step == SIDE:
                target[side, 0:SPILL, :] = turned[step - SPILL :, lanes]


def patch_kernel(
    rows_s, cols_s, own, halo, probe, le, let, lo, lot, sorter, amp,
    numer_own, numer_next, grad,
    prow, pc, piece_s, wave_s, grow, xe, xo, ze, zo, amp_s, amp_c,
):
    slot = pl.program_id(0)
    top = rows_s[0, slot]
    left = cols_s[0, slot]

    @pl.when(slot == 0)
    def _():
        numer_own[...] = jnp.zeros_like(numer_own)
        numer_next[...] = jnp.zeros_like(numer_next)
        grad[...] = jnp.zeros_like(grad)

    rolled_probe(probe.at[0], prow.at[0], left)
    rolled_probe(probe.at[1], prow.at[1], left)

    for side in range(2):
        amp_c[side] = amp[0, 0, :, side * HALF : (side + 1) * HALF]
    for odd in range(2):
        part = jnp.concatenate([amp_c[side, pl.ds(odd, HALF, stride=2), :] for side in range(2)], 1)
        high = part.astype(jnp.bfloat16)
        low = (part - high.astype(jnp.float32)).astype(jnp.bfloat16)
        amp_s[odd * HALF : (odd + 1) * HALF, :] = dot(high, sorter[...]) + dot(low, sorter[...])

    step = 16
    row_id = lax.broadcasted_iota(jnp.int32, (step, HALF), 0)
    lane_id = lax.broadcasted_iota(jnp.int32, (step, HALF), 1)
    row_in = row_id >= top
    lane_in = [lane_id + side * HALF >= left for side in range(2)]

    def wave_rows(start, side):
        rows = slice(start, start + step)
        lanes = slice(side * HALF, (side + 1) * HALF)
        p = [prow[c, side, pl.ds(SPILL - top + start, step), :] for c in range(2)]
        piece = []
        for c in range(2):
            here = own[c, rows, lanes]
            there = halo[c, rows, lanes]
            if start == 0:
                here = jnp.where(row_in, here, own[c, SIDE:BAND, lanes])
                there = jnp.where(row_in, there, halo[c, SIDE:BAND, lanes])
            piece.append(jnp.where(lane_in[side], here, there))
            piece_s[c, rows, lanes] = piece[c]
            pc[c, rows, lanes] = p[c]
        wave = [p[0] * piece[0] - p[1] * piece[1], p[0] * piece[1] + p[1] * piece[0]]
        for c in range(2):
            wave_s[c, rows, lanes] = wave[c]
        return wave

    for start in range(0, HALF, step):
        for side in range(2):
            lanes = slice(side * HALF, (side + 1) * HALF)
            upper = wave_rows(start, side)
            lower = wave_rows(start + HALF, side)
            for c in range(2):
                rows = slice(c * HALF + start, c * HALF + start + step)
                put_split(xe, rows, lanes, upper[c] + lower[c])
                put_split(xo, rows, lanes, upper[c] - lower[c])

    re_half, im_half = slice(0, HALF), slice(HALF, SIDE)
    for odd, (table, data) in enumerate(((le, xe), (lo, xo))):
        mid = table_dot(table, data)
        rows = slice(odd * HALF, (odd + 1) * HALF)
        for part in (re_half, im_half):
            first, second = mid[part, re_half], mid[part, im_half]
            put_split(ze, rows, part, first + second)
            put_split(zo, rows, part, first - second)

    for odd, (table, data, kept) in enumerate(((let, ze, xe), (lot, zo, xo))):
        far = dot_table(data, table)
        far_re, far_im = far[:, re_half], far[:, im_half]
        power = far_re * far_re + far_im * far_im
        factor = amp_s[:, odd * HALF : (odd + 1) * HALF] * lax.rsqrt(
            jnp.maximum(power, amp_floor * amp_floor)
        )
        put_split(kept, slice(0, SIDE), re_half, far_re * factor)
        put_split(kept, slice(0, SIDE), im_half, far_im * factor)

    even = dot_table(xe, le)
    odds = dot_table(xo, lo)
    for c, part in enumerate((re_half, im_half)):
        first, second = even[:, part], odds[:, part]
        for side, value in enumerate((first + second, first - second)):
            lanes = slice(side * HALF, (side + 1) * HALF)
            rows = slice(c * HALF, (c + 1) * HALF)
            put_split(ze, rows, lanes, value[:HALF])
            put_split(zo, rows, lanes, value[HALF:])
    even = table_dot(let, ze)
    odds = table_dot(lot, zo)

    for start in range(0, HALF, step):
        for side in range(2):
            lanes = slice(side * HALF, (side + 1) * HALF)
            first = [even[c * HALF + start : c * HALF + start + step, lanes] for c in range(2)]
            second = [odds[c * HALF + start : c * HALF + start + step, lanes] for c in range(2)]
            for lower in range(2):
                begin = start + lower * HALF
                rows = slice(begin, begin + step)
                change = []
                for c in range(2):
                    back = first[c] - second[c] if lower else first[c] + second[c]
                    change.append(back - wave_s[c, rows, lanes])
                p = [pc[c, rows, lanes] for c in range(2)]
                piece = [piece_s[c, rows, lanes] for c in range(2)]
                numer = [
                    p[0] * change[0] + p[1] * change[1],
                    p[0] * change[1] - p[1] * change[0],
                ]
                turned = [
                    piece[0] * change[0] + piece[1] * change[1],
                    piece[0] * change[1] - piece[1] * change[0],
                ]
                for c in range(2):
                    grow[c, side, rows, :] = turned[c]
                    here = jnp.where(lane_in[side], numer[c], 0.0)
                    there = numer[c] - here
                    if begin == 0:
                        grow[c, side, SIDE:BAND, :] = turned[c]
                        for total, value in ((numer_own, here), (numer_next, there)):
                            inside = jnp.where(row_in, value, 0.0)
                            total[c, rows, lanes] += inside
                            total[c, SIDE:BAND, lanes] += value - inside
                    else:
                        numer_own[c, rows, lanes] += here
                        numer_next[c, rows, lanes] += there

    back_left = lax.rem(SIDE - left, SIDE)
    step = 64
    for c in range(2):
        for start in range(0, SIDE, step):
            pair = [grow[c, side, pl.ds(top + start, step), :] for side in range(2)]
            value = pltpu.roll(jnp.concatenate(pair, 1), back_left, 1)
            for side in range(2):
                begin = (2 * c + side) * SIDE + start
                grad[begin : begin + step, :] += value[:, side * HALF : (side + 1) * HALF]


def patch_terms(rows, cols, own, halo, probe, amplitudes):
    count = amplitudes.shape[1]
    tables, sorter = half_tables()
    whole = lambda *shape: pl.BlockSpec(shape, lambda k: (0,) * len(shape))
    scalars = pl.BlockSpec(memory_space=pltpu.SMEM)
    band = whole(2, BAND, SIDE)
    f32, bf16 = jnp.float32, jnp.bfloat16
    split = pltpu.VMEM((2, SIDE, SIDE), bf16)
    return pl.pallas_call(
        patch_kernel,
        grid=(count,),
        in_specs=[scalars, scalars, band, band, whole(2, SIDE, SIDE)]
        + [whole(2, SIDE, SIDE)] * 4
        + [whole(SIDE, SIDE), pl.BlockSpec((1, 1, SIDE, SIDE), lambda k: (0, k, 0, 0))],
        out_specs=[band, band, whole(GRAD_ROWS, HALF)],
        out_shape=[
            jax.ShapeDtypeStruct((2, BAND, SIDE), f32),
            jax.ShapeDtypeStruct((2, BAND, SIDE), f32),
            jax.ShapeDtypeStruct((GRAD_ROWS, HALF), f32),
        ],
        scratch_shapes=[
            pltpu.VMEM((2, 2, BAND, HALF), f32),
            pltpu.VMEM((2, SIDE, SIDE), f32),
            pltpu.VMEM((2, SIDE, SIDE), f32),
            pltpu.VMEM((2, SIDE, SIDE), f32),
            pltpu.VMEM((2, 2, BAND, HALF), f32),
            split, split, split, split,
            pltpu.VMEM((SIDE, SIDE), f32),
            pltpu.VMEM((2, SIDE, HALF), f32),
        ],
        compiler_params=pltpu.CompilerParams(
            dimension_semantics=("arbitrary",), vmem_limit_bytes=VMEM_BYTES
        ),
        cost_estimate=pl.CostEstimate(
            flops=count * 26 * 2 * SIDE**3, bytes_accessed=6 * 2**20, transcendentals=0
        ),
        name="patch_terms",
    )(rows, cols, own, halo, probe, *[jnp.asarray(t) for t in tables], jnp.asarray(sorter), amplitudes)


def weight_kernel(rows_s, cols_s, rows_b, cols_b, probe, out, power, prow):
    count = rows_s.shape[1]
    power[...] = probe[0] * probe[0] + probe[1] * probe[1]
    out[...] = jnp.full_like(out, ridge)
    step = 16
    row_id = lax.broadcasted_iota(jnp.int32, (step, HALF), 0)
    lane_id = lax.broadcasted_iota(jnp.int32, (step, HALF), 1)

    def place(top, left, behind):
        rolled_probe(power, prow, left)
        row_in = row_id >= top
        for side in range(2):
            lanes = slice(side * HALF, (side + 1) * HALF)
            lane_in = lane_id + side * HALF >= left
            if behind:
                lane_in = jnp.logical_not(lane_in)
            for start in range(0, SIDE, step):
                value = prow[side, pl.ds(SPILL - top + start, step), :]
                value = jnp.where(lane_in, value, 0.0)
                if start == 0:
                    inside = jnp.where(row_in, value, 0.0)
                    out[SIDE:BAND, lanes] += value - inside
                    value = inside
                out[start : start + step, lanes] += value

    def body(slot, carry):
        place(rows_s[0, slot], cols_s[0, slot], False)
        place(rows_b[0, slot], cols_b[0, slot], True)
        return carry

    lax.fori_loop(0, count, body, 0)
    out[...] = 1.0 / out[...]


def weight_inverse(rows, cols, rows_behind, cols_behind, probe):
    scalars = pl.BlockSpec(memory_space=pltpu.SMEM)
    vmem = pl.BlockSpec(memory_space=pltpu.VMEM)
    return pl.pallas_call(
        weight_kernel,
        in_specs=[scalars] * 4 + [vmem],
        out_specs=vmem,
        out_shape=jax.ShapeDtypeStruct((BAND, SIDE), jnp.float32),
        scratch_shapes=[
            pltpu.VMEM((SIDE, SIDE), jnp.float32),
            pltpu.VMEM((2, BAND, HALF), jnp.float32),
        ],
        compiler_params=pltpu.CompilerParams(vmem_limit_bytes=VMEM_BYTES),
        cost_estimate=pl.CostEstimate(flops=2**24, bytes_accessed=2**20, transcendentals=0),
        name="weight_inverse",
    )(rows, cols, rows_behind, cols_behind, probe)


def sum_kernel(
    term, out, r1, a1, r2, a2, r3, r4, a4, f2, f1, f0,
    s1, v1, s2, v2, s3, v3, s4, v4, s5, v5, s6, v6, s7, v7,
):
    phase, space = lax.axis_index("phase"), lax.axis_index("space")
    core = lax.rem(phase, CORES)
    z = lax.rem(phase // CORES, Z_SIZE)
    x_lo = phase // (CORES * Z_SIZE)
    y = lax.rem(space, Y_SIZE)
    x_hi = space // Y_SIZE
    x = x_hi * X_LO + x_lo

    def device(core_=core, z_=z, x_=x, y_=y):
        phase_ = (lax.rem(x_, X_LO) * Z_SIZE + z_) * CORES + core_
        return (phase_, (x_ // X_LO) * Y_SIZE + y_)

    def core_peer():
        return device(core_=1 - core)

    def x_peer(k):
        return device(x_=lax.rem(x + k, X_SIZE))

    def y_peer(k):
        return device(y_=lax.rem(y + k, Y_SIZE))

    def z_peer(k):
        return device(z_=lax.rem(z + k, Z_SIZE))

    def send(src, dst, s, v, target):
        return pltpu.make_async_remote_copy(
            src_ref=src, dst_ref=dst, send_sem=s, recv_sem=v,
            device_id=target, device_id_type=pl.DeviceIdType.MESH,
        )

    barrier = pltpu.get_barrier_semaphore()

    def greet(target):
        pl.semaphore_signal(barrier, inc=1, device_id=target, device_id_type=pl.DeviceIdType.MESH)

    greet(core_peer())
    for k in range(1, X_SIZE):
        greet(x_peer(k))
    for k in range(1, Y_SIZE):
        greet(y_peer(k))

    def greet_z(k, carry):
        greet(z_peer(k))
        return carry

    lax.fori_loop(1, Z_SIZE, greet_z, 0)
    pl.semaphore_wait(barrier, 1 + (X_SIZE - 1) + (Y_SIZE - 1) + (Z_SIZE - 1))

    part1 = GRAD_ROWS // CORES
    part2 = part1 // X_SIZE
    part3 = part2 // Z_SIZE

    def span(index, size):
        return pl.ds(pl.multiple_of(index * size, size), size)

    copy = send(term.at[span(1 - core, part1)], r1, s1, v1, core_peer())
    copy.start()
    copy.wait()
    a1[...] = term[span(core, part1), :] + r1[...]

    copies = []
    for k in range(1, X_SIZE):
        target = lax.rem(x + k, X_SIZE)
        copies.append(
            send(a1.at[span(target, part2)], r2.at[k - 1], s2.at[k - 1], v2.at[k - 1], x_peer(k))
        )
    for copy in copies:
        copy.start()
    for copy in copies:
        copy.wait()
    a2[...] = a1[span(x, part2), :] + r2[0] + r2[1] + r2[2]

    def z_sum(k):
        target = lax.rem(z + k, Z_SIZE)
        return send(a2.at[span(target, part3)], r3.at[k - 1], s3.at[k - 1], v3.at[k - 1], z_peer(k))

    def start_z_sum(k, carry):
        z_sum(k).start()
        return carry

    def wait_z_sum(k, carry):
        z_sum(k).wait()
        return carry

    lax.fori_loop(1, Z_SIZE, start_z_sum, 0)
    lax.fori_loop(1, Z_SIZE, wait_z_sum, 0)
    total = a2[span(z, part3), :]
    for k in range(Z_SIZE - 1):
        total = total + r3[k]

    r4[y] = total
    copies = [
        send(r4.at[y], r4.at[y], s4.at[k - 1], v4.at[k - 1], y_peer(k)) for k in range(1, Y_SIZE)
    ]
    for copy in copies:
        copy.start()
    for copy in copies:
        copy.wait()
    a4[...] = ((r4[0] + r4[1]) + (r4[2] + r4[3])) * (
        1.0 / math.sqrt(6 * lax.axis_size("phase") * lax.axis_size("space"))
    )

    f2[span(z, part3), :] = a4[...]

    def z_spread(k):
        return send(a4, f2.at[span(z, part3)], s5.at[k - 1], v5.at[k - 1], z_peer(k))

    def start_z_spread(k, carry):
        z_spread(k).start()
        return carry

    def wait_z_spread(k, carry):
        z_spread(k).wait()
        return carry

    lax.fori_loop(1, Z_SIZE, start_z_spread, 0)
    lax.fori_loop(1, Z_SIZE, wait_z_spread, 0)

    copies = [
        send(f2, f1.at[span(x, part2)], s6.at[k - 1], v6.at[k - 1], x_peer(k))
        for k in range(1, X_SIZE)
    ]
    for copy in copies:
        copy.start()
    f1[span(x, part2), :] = f2[...]
    for copy in copies:
        copy.wait()

    copy = send(f1, f0.at[span(core, part1)], s7, v7, core_peer())
    copy.start()
    f0[span(core, part1), :] = f1[...]
    copy.wait()
    for c in range(2):
        for side in range(2):
            begin = (2 * c + side) * SIDE
            out[c, :, side * HALF : (side + 1) * HALF] = f0[begin : begin + SIDE, :]


def summed_everywhere(term):
    part1 = GRAD_ROWS // CORES
    part2 = part1 // X_SIZE
    part3 = part2 // Z_SIZE
    f32 = jnp.float32
    dma = pltpu.SemaphoreType.DMA
    vmem = pl.BlockSpec(memory_space=pltpu.VMEM)
    sems = []
    for count in (1, X_SIZE - 1, Z_SIZE - 1, Y_SIZE - 1, Z_SIZE - 1, X_SIZE - 1, 1):
        sems += [dma if count == 1 else dma((count,))] * 2
    return pl.pallas_call(
        sum_kernel,
        in_specs=[vmem],
        out_specs=vmem,
        out_shape=jax.ShapeDtypeStruct((2, SIDE, SIDE), f32),
        scratch_shapes=[
            pltpu.VMEM((part1, HALF), f32),
            pltpu.VMEM((part1, HALF), f32),
            pltpu.VMEM((X_SIZE - 1, part2, HALF), f32),
            pltpu.VMEM((part2, HALF), f32),
            pltpu.VMEM((Z_SIZE - 1, part3, HALF), f32),
            pltpu.VMEM((Y_SIZE, part3, HALF), f32),
            pltpu.VMEM((part3, HALF), f32),
            pltpu.VMEM((part2, HALF), f32),
            pltpu.VMEM((part1, HALF), f32),
            pltpu.VMEM((GRAD_ROWS, HALF), f32),
            *sems,
        ],
        compiler_params=pltpu.CompilerParams(
            collective_id=0, has_side_effects=True, vmem_limit_bytes=VMEM_BYTES
        ),
        cost_estimate=pl.CostEstimate(flops=2**20, bytes_accessed=2**24, transcendentals=0),
        name="summed_everywhere",
    )(term)


def shards(object_field, split_field, scaled_dual, probe, amplitudes, row_offsets, col_offsets):
    own = object_field[:, 0]
    split_own = split_field[:, 0]
    dual_own = scaled_dual[:, 0]
    halo = from_behind(own, "space", -1)
    next_object = passed_along(own, "phase", -1)
    start_point = own + split_own - dual_own
    start_prev = passed_along(start_point, "phase", 1)
    offsets_behind = from_behind(jnp.concatenate([row_offsets, col_offsets], 0), "space", 1)
    inverse = weight_inverse(
        row_offsets, col_offsets, offsets_behind[:1], offsets_behind[1:], probe
    )
    numer_own, numer_next, grad = patch_terms(
        row_offsets, col_offsets, own, halo, probe, amplitudes
    )
    incoming = from_behind(numer_next, "space", 1)
    probe_gradient = summed_everywhere(grad)
    steady = own - tv_step * ((own - start_prev) - (next_object - start_point))
    updated = steady + (numer_own + incoming) * inverse[None]
    next_updated = passed_along(updated, "phase", -1)
    joint = next_updated - updated + dual_own
    size_abs = jnp.sqrt(joint[0] * joint[0] + joint[1] * joint[1])
    shrink = jnp.maximum(size_abs - shrink_level, 0.0) / jnp.maximum(size_abs, shrink_level)
    new_split = joint * shrink[None]
    new_dual = joint - new_split
    return (updated[:, None], new_split[:, None], new_dual[:, None], probe_gradient)


def solution(mesh):
    in_specs = (
        P(None, "phase", None, "space"),
        P(None, "phase", None, "space"),
        P(None, "phase", None, "space"),
        P(),
        P("phase", "space", None, None),
        P("phase", "space"),
        P("phase", "space"),
    )
    out_specs = (
        P(None, "phase", None, "space"),
        P(None, "phase", None, "space"),
        P(None, "phase", None, "space"),
        P(),
    )
    return jax.shard_map(shards, mesh=mesh, in_specs=in_specs, out_specs=out_specs, check_vma=False)
```

```python
import math

import jax
import jax.numpy as jnp
import ml_dtypes
import numpy as np
from jax import lax
from jax.experimental import pallas as pl
from jax.experimental.pallas import tpu as pltpu
from jax.sharding import PartitionSpec as P

amp_floor = 0.25
ridge = 1.0
tv_step = 0.25
shrink_level = 0.5

SIDE = 256
HALF = 128
BAND = 272
SPILL = BAND - SIDE
CORES, Z_SIZE, X_LO, Y_SIZE, X_SIZE = 2, 16, 2, 4, 4
GRAD_ROWS = 1024
TILES = X_SIZE // X_LO * Y_SIZE
PATCHES = 6
VMEM_BYTES = 50 * 1024 * 1024


def two_parts(table):
    high = table.astype(ml_dtypes.bfloat16)
    low = (table - high.astype(np.float64)).astype(ml_dtypes.bfloat16)
    return np.stack([high, low])


def half_tables():
    place = np.arange(HALF)
    tables = []
    for odd in (0, 1):
        turns = ((2 * place[:, None] + odd) * place[None, :]) % SIDE
        angle = -2.0 * np.pi * turns / SIDE
        re = np.cos(angle) / math.sqrt(SIDE)
        im = np.sin(angle) / math.sqrt(SIDE)
        real_form = np.block([[re, -im], [im, re]])
        tables.append(two_parts(real_form))
        tables.append(two_parts(real_form.T))
    order = np.concatenate([np.arange(0, SIDE, 2), np.arange(1, SIDE, 2)])
    sorter = np.zeros((SIDE, SIDE), np.float32)
    sorter[order, np.arange(SIDE)] = 1.0
    return tables, sorter.astype(ml_dtypes.bfloat16)


def put_split(ref, rows, lanes, value):
    high = value.astype(jnp.bfloat16)
    ref[0, rows, lanes] = high
    ref[1, rows, lanes] = (value - high.astype(jnp.float32)).astype(jnp.bfloat16)


def dot(a, b):
    return jnp.dot(a, b, preferred_element_type=jnp.float32)


def table_dot(table, data):
    return dot(table[0], data[0]) + dot(table[1], data[0]) + dot(table[0], data[1])


def dot_table(data, table):
    return dot(data[0], table[0]) + dot(data[1], table[0]) + dot(data[0], table[1])


def rolled_probe(source, target, left):
    step = 64
    for start in range(0, SIDE, step):
        turned = pltpu.roll(source[start : start + step, :], left, 1)
        for side in range(2):
            lanes = slice(side * HALF, (side + 1) * HALF)
            target[side, SPILL + start : SPILL + start + step, :] = turned[:, lanes]
            if start + step == SIDE:
                target[side, 0:SPILL, :] = turned[step - SPILL :, lanes]


def patch_kernel(
    rows_s, cols_s, behind, own, halo, probe, le, let, lo, lot, sorter, amp,
    numer_own, numer_next, grad, weight,
    power, brow, prow, pc, piece_s, wave_s, grow, xe, xo, ze, zo, amp_s, amp_c,
):
    slot = pl.program_id(0)
    top = rows_s[0, slot]
    left = cols_s[0, slot]

    @pl.when(slot == 0)
    def _():
        numer_own[...] = jnp.zeros_like(numer_own)
        numer_next[...] = jnp.zeros_like(numer_next)
        grad[...] = jnp.zeros_like(grad)
        weight[...] = jnp.full_like(weight, ridge)
        power[...] = probe[0] * probe[0] + probe[1] * probe[1]

    rolled_probe(probe.at[0], prow.at[0], left)
    rolled_probe(probe.at[1], prow.at[1], left)
    top_b = behind[0, slot]
    left_b = behind[1, slot]
    rolled_probe(power, brow, left_b)

    for side in range(2):
        amp_c[side] = amp[0, 0, :, side * HALF : (side + 1) * HALF]
    for odd in range(2):
        part = jnp.concatenate([amp_c[side, pl.ds(odd, HALF, stride=2), :] for side in range(2)], 1)
        high = part.astype(jnp.bfloat16)
        low = (part - high.astype(jnp.float32)).astype(jnp.bfloat16)
        amp_s[odd * HALF : (odd + 1) * HALF, :] = dot(high, sorter[...]) + dot(low, sorter[...])

    step = 16
    row_id = lax.broadcasted_iota(jnp.int32, (step, HALF), 0)
    lane_id = lax.broadcasted_iota(jnp.int32, (step, HALF), 1)
    row_in = row_id >= top
    lane_in = [lane_id + side * HALF >= left for side in range(2)]
    lane_behind = [lane_id + side * HALF < left_b for side in range(2)]

    def wave_rows(start, side):
        rows = slice(start, start + step)
        lanes = slice(side * HALF, (side + 1) * HALF)
        p = [prow[c, side, pl.ds(SPILL - top + start, step), :] for c in range(2)]
        piece = []
        for c in range(2):
            here = own[c, rows, lanes]
            there = halo[c, rows, lanes]
            if start == 0:
                here = jnp.where(row_in, here, own[c, SIDE:BAND, lanes])
                there = jnp.where(row_in, there, halo[c, SIDE:BAND, lanes])
            piece.append(jnp.where(lane_in[side], here, there))
            piece_s[c, rows, lanes] = piece[c]
            pc[c, rows, lanes] = p[c]
        wave = [p[0] * piece[0] - p[1] * piece[1], p[0] * piece[1] + p[1] * piece[0]]
        for c in range(2):
            wave_s[c, rows, lanes] = wave[c]
        mine = jnp.where(lane_in[side], p[0] * p[0] + p[1] * p[1], 0.0)
        theirs = brow[side, pl.ds(SPILL - top_b + start, step), :]
        theirs = jnp.where(lane_behind[side], theirs, 0.0)
        if start == 0:
            mine_in = jnp.where(row_in, mine, 0.0)
            theirs_in = jnp.where(row_id >= top_b, theirs, 0.0)
            weight[SIDE:BAND, lanes] += (mine - mine_in) + (theirs - theirs_in)
            mine, theirs = mine_in, theirs_in
        weight[rows, lanes] += mine + theirs
        return wave

    for start in range(0, HALF, step):
        for side in range(2):
            lanes = slice(side * HALF, (side + 1) * HALF)
            upper = wave_rows(start, side)
            lower = wave_rows(start + HALF, side)
            for c in range(2):
                rows = slice(c * HALF + start, c * HALF + start + step)
                put_split(xe, rows, lanes, upper[c] + lower[c])
                put_split(xo, rows, lanes, upper[c] - lower[c])

    re_half, im_half = slice(0, HALF), slice(HALF, SIDE)
    for odd, (table, data) in enumerate(((le, xe), (lo, xo))):
        mid = table_dot(table, data)
        rows = slice(odd * HALF, (odd + 1) * HALF)
        for part in (re_half, im_half):
            first, second = mid[part, re_half], mid[part, im_half]
            put_split(ze, rows, part, first + second)
            put_split(zo, rows, part, first - second)

    for odd, (table, data, kept) in enumerate(((let, ze, xe), (lot, zo, xo))):
        far = dot_table(data, table)
        far_re, far_im = far[:, re_half], far[:, im_half]
        power = far_re * far_re + far_im * far_im
        factor = amp_s[:, odd * HALF : (odd + 1) * HALF] * lax.rsqrt(
            jnp.maximum(power, amp_floor * amp_floor)
        )
        put_split(kept, slice(0, SIDE), re_half, far_re * factor)
        put_split(kept, slice(0, SIDE), im_half, far_im * factor)

    even = dot_table(xe, le)
    odds = dot_table(xo, lo)
    for c, part in enumerate((re_half, im_half)):
        first, second = even[:, part], odds[:, part]
        for side, value in enumerate((first + second, first - second)):
            lanes = slice(side * HALF, (side + 1) * HALF)
            rows = slice(c * HALF, (c + 1) * HALF)
            put_split(ze, rows, lanes, value[:HALF])
            put_split(zo, rows, lanes, value[HALF:])
    even = table_dot(let, ze)
    odds = table_dot(lot, zo)

    for start in range(0, HALF, step):
        for side in range(2):
            lanes = slice(side * HALF, (side + 1) * HALF)
            first = [even[c * HALF + start : c * HALF + start + step, lanes] for c in range(2)]
            second = [odds[c * HALF + start : c * HALF + start + step, lanes] for c in range(2)]
            for lower in range(2):
                begin = start + lower * HALF
                rows = slice(begin, begin + step)
                change = []
                for c in range(2):
                    back = first[c] - second[c] if lower else first[c] + second[c]
                    change.append(back - wave_s[c, rows, lanes])
                p = [pc[c, rows, lanes] for c in range(2)]
                piece = [piece_s[c, rows, lanes] for c in range(2)]
                numer = [
                    p[0] * change[0] + p[1] * change[1],
                    p[0] * change[1] - p[1] * change[0],
                ]
                turned = [
                    piece[0] * change[0] + piece[1] * change[1],
                    piece[0] * change[1] - piece[1] * change[0],
                ]
                for c in range(2):
                    grow[c, side, rows, :] = turned[c]
                    here = jnp.where(lane_in[side], numer[c], 0.0)
                    there = numer[c] - here
                    if begin == 0:
                        grow[c, side, SIDE:BAND, :] = turned[c]
                        for total, value in ((numer_own, here), (numer_next, there)):
                            inside = jnp.where(row_in, value, 0.0)
                            total[c, rows, lanes] += inside
                            total[c, SIDE:BAND, lanes] += value - inside
                    else:
                        numer_own[c, rows, lanes] += here
                        numer_next[c, rows, lanes] += there

    back_left = lax.rem(SIDE - left, SIDE)
    step = 64
    for c in range(2):
        for start in range(0, SIDE, step):
            pair = [grow[c, side, pl.ds(top + start, step), :] for side in range(2)]
            value = pltpu.roll(jnp.concatenate(pair, 1), back_left, 1)
            for side in range(2):
                begin = (2 * c + side) * SIDE + start
                grad[begin : begin + step, :] += value[:, side * HALF : (side + 1) * HALF]

    @pl.when(slot == pl.num_programs(0) - 1)
    def _():
        weight[...] = 1.0 / weight[...]


def patch_terms(rows, cols, behind, own, halo, probe, amplitudes):
    count = amplitudes.shape[1]
    tables, sorter = half_tables()
    whole = lambda *shape: pl.BlockSpec(shape, lambda k: (0,) * len(shape))
    scalars = pl.BlockSpec(memory_space=pltpu.SMEM)
    band = whole(2, BAND, SIDE)
    f32, bf16 = jnp.float32, jnp.bfloat16
    split = pltpu.VMEM((2, SIDE, SIDE), bf16)
    return pl.pallas_call(
        patch_kernel,
        grid=(count,),
        in_specs=[scalars, scalars, scalars, band, band, whole(2, SIDE, SIDE)]
        + [whole(2, SIDE, SIDE)] * 4
        + [whole(SIDE, SIDE), pl.BlockSpec((1, 1, SIDE, SIDE), lambda k: (0, k, 0, 0))],
        out_specs=[band, band, whole(GRAD_ROWS, HALF), whole(BAND, SIDE)],
        out_shape=[
            jax.ShapeDtypeStruct((2, BAND, SIDE), f32),
            jax.ShapeDtypeStruct((2, BAND, SIDE), f32),
            jax.ShapeDtypeStruct((GRAD_ROWS, HALF), f32),
            jax.ShapeDtypeStruct((BAND, SIDE), f32),
        ],
        scratch_shapes=[
            pltpu.VMEM((SIDE, SIDE), f32),
            pltpu.VMEM((2, BAND, HALF), f32),
            pltpu.VMEM((2, 2, BAND, HALF), f32),
            pltpu.VMEM((2, SIDE, SIDE), f32),
            pltpu.VMEM((2, SIDE, SIDE), f32),
            pltpu.VMEM((2, SIDE, SIDE), f32),
            pltpu.VMEM((2, 2, BAND, HALF), f32),
            split, split, split, split,
            pltpu.VMEM((SIDE, SIDE), f32),
            pltpu.VMEM((2, SIDE, HALF), f32),
        ],
        compiler_params=pltpu.CompilerParams(
            dimension_semantics=("arbitrary",), vmem_limit_bytes=VMEM_BYTES
        ),
        cost_estimate=pl.CostEstimate(
            flops=count * 26 * 2 * SIDE**3, bytes_accessed=6 * 2**20, transcendentals=0
        ),
        name="patch_terms",
    )(rows, cols, behind, own, halo, probe, *[jnp.asarray(t) for t in tables], jnp.asarray(sorter), amplitudes)


class Place:
    def __init__(self):
        self.phase, self.space = lax.axis_index("phase"), lax.axis_index("space")
        self.core = lax.rem(self.phase, CORES)
        self.z = lax.rem(self.phase // CORES, Z_SIZE)
        x_lo = self.phase // (CORES * Z_SIZE)
        self.y = lax.rem(self.space, Y_SIZE)
        self.x_hi = self.space // Y_SIZE
        self.x = self.x_hi * X_LO + x_lo

    def device(self, core, z, x, y):
        phase = (lax.rem(x, X_LO) * Z_SIZE + z) * CORES + core
        return (phase, (x // X_LO) * Y_SIZE + y)

    def core_peer(self):
        return self.device(1 - self.core, self.z, self.x, self.y)

    def x_peer(self, k):
        return self.device(self.core, self.z, lax.rem(self.x + k, X_SIZE), self.y)

    def y_peer(self, k):
        return self.device(self.core, self.z, self.x, lax.rem(self.y + k, Y_SIZE))

    def z_peer(self, k):
        return self.device(self.core, lax.rem(self.z + k, Z_SIZE), self.x, self.y)

    def bin_at(self, k):
        count = lax.axis_size("phase")
        return (lax.rem(self.phase + k + count, count), self.space)

    def tile_at(self, k):
        count = lax.axis_size("space")
        return (self.phase, lax.rem(self.space + k + count, count))


def remote(src, dst, s, v, target):
    return pltpu.make_async_remote_copy(
        src_ref=src, dst_ref=dst, send_sem=s, recv_sem=v,
        device_id=target, device_id_type=pl.DeviceIdType.MESH,
    )


def greet(target):
    pl.semaphore_signal(
        pltpu.get_barrier_semaphore(), inc=1, device_id=target, device_id_type=pl.DeviceIdType.MESH
    )


CHUNKS = 4
CHUNK_ROWS = BAND // 2


def chunk_of(ref, index):
    return ref.at[index // 2, pl.ds((index % 2) * CHUNK_ROWS, CHUNK_ROWS), :]


def opening_kernel(
    own, split, dual, rows, cols,
    halo, steady, behind,
    start_point, following, preceding, offsets,
    hs, hv, rs, ns, nv, ps, pv, os, ov,
):
    me = Place()
    last = TILES - 1
    for target in (me.tile_at(1), me.tile_at(-1), me.tile_at(TILES // 2), me.bin_at(1), me.bin_at(-1)):
        greet(target)
    greet(me.device(me.core, me.z, me.x, Y_SIZE - 1 - me.y))
    start_point[...] = own[...] + split[...] - dual[...]
    offsets[...] = jnp.zeros_like(offsets)
    offsets[0:1, 0 : rows.shape[1]] = rows[...]
    offsets[1:2, 0 : cols.shape[1]] = cols[...]

    @pl.when(me.space == 0)
    def _():
        behind[...] = jnp.zeros_like(behind)

    pl.semaphore_wait(pltpu.get_barrier_semaphore(), 6)

    def halo_copy(index):
        target = me.tile_at(-1) if index < CHUNKS // 2 else me.y_peer(Y_SIZE - 1)
        return remote(chunk_of(own, index), chunk_of(halo, index), hs.at[index], hv.at[index], target)

    def relay(index):
        place = chunk_of(halo, index)
        return remote(place, place, rs.at[index - CHUNKS // 2], hv.at[index], me.tile_at(TILES // 2))

    order = (2, 0, 3, 1)

    @pl.when(me.space > 0)
    def _():
        for index in order:
            halo_copy(index).start()

    to_preceding = remote(own, following, ns, nv, me.bin_at(-1))
    to_following = remote(start_point, preceding, ps, pv, me.bin_at(1))
    offsets_on = remote(offsets, behind, os, ov, me.tile_at(1))
    to_preceding.start()
    to_following.start()

    @pl.when(me.space < last)
    def _():
        offsets_on.start()

    @pl.when(me.space == last)
    def _():
        for index in (2, 3):
            halo_copy(index).wait_recv()
            relay(index).start()

    to_preceding.wait()
    to_following.wait()
    steady[...] = own[...] - tv_step * (
        (own[...] - preceding[...]) - (following[...] - start_point[...])
    )

    @pl.when(me.space > 0)
    def _():
        offsets_on.wait_recv()
        for index in order:
            halo_copy(index).wait_send()

    @pl.when(me.space < last)
    def _():
        offsets_on.wait_send()
        for index in order:
            halo_copy(index).wait_recv()

    @pl.when(me.space == last)
    def _():
        for index in (2, 3):
            relay(index).wait_send()


def opening(own, split, dual, rows, cols):
    f32, i32 = jnp.float32, jnp.int32
    dma = pltpu.SemaphoreType.DMA
    vmem = pl.BlockSpec(memory_space=pltpu.VMEM)
    band = jax.ShapeDtypeStruct((2, BAND, SIDE), f32)
    return pl.pallas_call(
        opening_kernel,
        in_specs=[vmem] * 5,
        out_specs=[vmem] * 3,
        out_shape=[band, band, jax.ShapeDtypeStruct((8, HALF), i32)],
        scratch_shapes=[
            pltpu.VMEM((2, BAND, SIDE), f32),
            pltpu.VMEM((2, BAND, SIDE), f32),
            pltpu.VMEM((2, BAND, SIDE), f32),
            pltpu.VMEM((8, HALF), i32),
            dma((CHUNKS,)), dma((CHUNKS,)), dma((CHUNKS // 2,)),
            dma, dma, dma, dma, dma, dma,
        ],
        compiler_params=pltpu.CompilerParams(
            collective_id=0, has_side_effects=True, vmem_limit_bytes=VMEM_BYTES
        ),
        cost_estimate=pl.CostEstimate(flops=2**20, bytes_accessed=2**24, transcendentals=0),
        name="opening",
    )(own, split, dual, rows, cols)


def tail_kernel(
    numer_own, numer_next, inverse, steady, term,
    updated, next_updated, out,
    inc, r1, a1, r2, a2, r3, r4, a4, f2, f1, f0,
    cs, cv, rs, us, uv,
    s1, v1, s2, v2, s3, v3, s4, v4, s5, v5, s6, v6, s7, v7,
):
    me = Place()
    core, x, y, z = me.core, me.x, me.y, me.z
    last = TILES - 1

    greet(me.core_peer())
    for k in range(1, X_SIZE):
        greet(me.x_peer(k))
    for k in range(1, Y_SIZE):
        greet(me.y_peer(k))
    for target in (me.tile_at(1), me.tile_at(-1), me.bin_at(1), me.bin_at(-1)):
        greet(target)

    def greet_z(k, carry):
        greet(me.z_peer(k))
        return carry

    lax.fori_loop(1, Z_SIZE, greet_z, 0)
    pl.semaphore_wait(
        pltpu.get_barrier_semaphore(), 1 + (X_SIZE - 1) + (Y_SIZE - 1) + 4 + (Z_SIZE - 1)
    )

    def correction(index):
        target = me.tile_at(1) if index < CHUNKS // 2 else me.y_peer(1)
        return remote(
            chunk_of(numer_next, index), chunk_of(inc, index), cs.at[index], cv.at[index], target
        )

    def relay(index):
        place = chunk_of(inc, index)
        return remote(place, place, rs.at[index - CHUNKS // 2], cv.at[index], me.tile_at(TILES // 2))

    def updated_copy(index):
        return remote(
            chunk_of(updated, index), chunk_of(next_updated, index), us.at[index], uv.at[index],
            me.bin_at(-1),
        )

    order = (2, 0, 3, 1)

    @pl.when(me.space < last)
    def _():
        for index in order:
            correction(index).start()

    def relay_on(index):
        @pl.when(me.space == 0)
        def _():
            correction(index).wait_recv()
            relay(index).start()

    part1 = GRAD_ROWS // CORES
    part2 = part1 // X_SIZE
    part3 = part2 // Z_SIZE

    def span(index, size):
        return pl.ds(pl.multiple_of(index * size, size), size)

    copy = remote(term.at[span(1 - core, part1)], r1, s1, v1, me.core_peer())
    copy.start()
    copy.wait()
    a1[...] = term[span(core, part1), :] + r1[...]

    copies = []
    for k in range(1, X_SIZE):
        target = lax.rem(x + k, X_SIZE)
        copies.append(
            remote(a1.at[span(target, part2)], r2.at[k - 1], s2.at[k - 1], v2.at[k - 1], me.x_peer(k))
        )
    for copy in copies:
        copy.start()
    relay_on(2)
    for copy in copies:
        copy.wait()
    a2[...] = a1[span(x, part2), :] + r2[0] + r2[1] + r2[2]

    def z_sum(k):
        target = lax.rem(z + k, Z_SIZE)
        return remote(a2.at[span(target, part3)], r3.at[k - 1], s3.at[k - 1], v3.at[k - 1], me.z_peer(k))

    def start_z_sum(k, carry):
        z_sum(k).start()
        return carry

    def wait_z_sum(k, carry):
        z_sum(k).wait()
        return carry

    lax.fori_loop(1, Z_SIZE, start_z_sum, 0)
    relay_on(3)
    lax.fori_loop(1, Z_SIZE, wait_z_sum, 0)
    total = a2[span(z, part3), :]
    for k in range(Z_SIZE - 1):
        total = total + r3[k]

    r4[y] = total
    copies = [
        remote(r4.at[y], r4.at[y], s4.at[k - 1], v4.at[k - 1], me.y_peer(k)) for k in range(1, Y_SIZE)
    ]
    for copy in copies:
        copy.start()
    for copy in copies:
        copy.wait()
    count = PATCHES * lax.axis_size("phase") * lax.axis_size("space")
    a4[...] = ((r4[0] + r4[1]) + (r4[2] + r4[3])) * (1.0 / math.sqrt(count))

    f2[span(z, part3), :] = a4[...]

    def z_spread(k):
        return remote(a4, f2.at[span(z, part3)], s5.at[k - 1], v5.at[k - 1], me.z_peer(k))

    def start_z_spread(k, carry):
        z_spread(k).start()
        return carry

    def wait_z_spread(k, carry):
        z_spread(k).wait()
        return carry

    lax.fori_loop(1, Z_SIZE, start_z_spread, 0)

    for index in order:
        part, rows = index // 2, pl.ds((index % 2) * CHUNK_ROWS, CHUNK_ROWS)

        @pl.when(me.space > 0)
        def _():
            correction(index).wait_recv()
            numer = numer_own[part, rows, :] + inc[part, rows, :]
            updated[part, rows, :] = steady[part, rows, :] + numer * inverse[rows, :]

        @pl.when(me.space == 0)
        def _():
            updated[part, rows, :] = steady[part, rows, :] + numer_own[part, rows, :] * inverse[rows, :]

        updated_copy(index).start()

    lax.fori_loop(1, Z_SIZE, wait_z_spread, 0)

    copies = [
        remote(f2, f1.at[span(x, part2)], s6.at[k - 1], v6.at[k - 1], me.x_peer(k))
        for k in range(1, X_SIZE)
    ]
    for copy in copies:
        copy.start()
    f1[span(x, part2), :] = f2[...]
    for copy in copies:
        copy.wait()

    copy = remote(f1, f0.at[span(core, part1)], s7, v7, me.core_peer())
    copy.start()
    f0[span(core, part1), :] = f1[...]
    copy.wait()
    for c in range(2):
        for side in range(2):
            begin = (2 * c + side) * SIDE
            out[c, :, side * HALF : (side + 1) * HALF] = f0[begin : begin + SIDE, :]

    for index in order:
        updated_copy(index).wait()

    @pl.when(me.space < last)
    def _():
        for index in order:
            correction(index).wait_send()

    @pl.when(me.space == 0)
    def _():
        for index in (2, 3):
            relay(index).wait_send()


def tail(numer_own, numer_next, inverse, steady, term):
    part1 = GRAD_ROWS // CORES
    part2 = part1 // X_SIZE
    part3 = part2 // Z_SIZE
    f32 = jnp.float32
    dma = pltpu.SemaphoreType.DMA
    vmem = pl.BlockSpec(memory_space=pltpu.VMEM)
    band = jax.ShapeDtypeStruct((2, BAND, SIDE), f32)
    sems = []
    for count in (1, X_SIZE - 1, Z_SIZE - 1, Y_SIZE - 1, Z_SIZE - 1, X_SIZE - 1, 1):
        sems += [dma if count == 1 else dma((count,))] * 2
    return pl.pallas_call(
        tail_kernel,
        in_specs=[vmem] * 5,
        out_specs=[vmem] * 3,
        out_shape=[band, band, jax.ShapeDtypeStruct((2, SIDE, SIDE), f32)],
        scratch_shapes=[
            pltpu.VMEM((2, BAND, SIDE), f32),
            pltpu.VMEM((part1, HALF), f32),
            pltpu.VMEM((part1, HALF), f32),
            pltpu.VMEM((X_SIZE - 1, part2, HALF), f32),
            pltpu.VMEM((part2, HALF), f32),
            pltpu.VMEM((Z_SIZE - 1, part3, HALF), f32),
            pltpu.VMEM((Y_SIZE, part3, HALF), f32),
            pltpu.VMEM((part3, HALF), f32),
            pltpu.VMEM((part2, HALF), f32),
            pltpu.VMEM((part1, HALF), f32),
            pltpu.VMEM((GRAD_ROWS, HALF), f32),
            dma((CHUNKS,)), dma((CHUNKS,)), dma((CHUNKS // 2,)), dma((CHUNKS,)), dma((CHUNKS,)),
            *sems,
        ],
        compiler_params=pltpu.CompilerParams(
            collective_id=1, has_side_effects=True, vmem_limit_bytes=VMEM_BYTES
        ),
        cost_estimate=pl.CostEstimate(flops=2**20, bytes_accessed=2**24, transcendentals=0),
        name="tail",
    )(numer_own, numer_next, inverse, steady, term)


def finish_kernel(updated, next_updated, dual, summed, out_object, out_split, out_dual, out_sum):
    out_object[...] = updated[...]
    out_sum[...] = summed[...]
    joint = [next_updated[c] - updated[c] + dual[c] for c in range(2)]
    size_abs = jnp.sqrt(joint[0] * joint[0] + joint[1] * joint[1])
    shrink = jnp.maximum(size_abs - shrink_level, 0.0) / jnp.maximum(size_abs, shrink_level)
    for c in range(2):
        new_split = joint[c] * shrink
        out_split[c] = new_split
        out_dual[c] = joint[c] - new_split


def finish(updated, next_updated, dual, summed):
    steps = 2
    f32 = jnp.float32
    band = pl.BlockSpec((2, BAND // steps, SIDE), lambda i: (0, i, 0))
    grad = pl.BlockSpec((2, SIDE // steps, SIDE), lambda i: (0, i, 0))
    band_shape = jax.ShapeDtypeStruct((2, BAND, SIDE), f32)
    return pl.pallas_call(
        finish_kernel,
        grid=(steps,),
        in_specs=[band, band, band, grad],
        out_specs=[band, band, band, grad],
        out_shape=[band_shape] * 3 + [jax.ShapeDtypeStruct((2, SIDE, SIDE), f32)],
        compiler_params=pltpu.CompilerParams(
            dimension_semantics=("arbitrary",), vmem_limit_bytes=VMEM_BYTES
        ),
        cost_estimate=pl.CostEstimate(flops=2**20, bytes_accessed=2**22, transcendentals=0),
        name="finish",
    )(updated, next_updated, dual, summed)


def shards(object_field, split_field, scaled_dual, probe, amplitudes, row_offsets, col_offsets):
    own = object_field[:, 0]
    split_own = split_field[:, 0]
    dual_own = scaled_dual[:, 0]
    halo, steady, behind = opening(own, split_own, dual_own, row_offsets, col_offsets)
    numer_own, numer_next, grad, inverse = patch_terms(
        row_offsets, col_offsets, behind, own, halo, probe, amplitudes
    )
    updated, next_updated, summed = tail(numer_own, numer_next, inverse, steady, grad)
    updated, new_split, new_dual, probe_gradient = finish(updated, next_updated, dual_own, summed)
    return (updated[:, None], new_split[:, None], new_dual[:, None], probe_gradient)


def solution(mesh):
    in_specs = (
        P(None, "phase", None, "space"),
        P(None, "phase", None, "space"),
        P(None, "phase", None, "space"),
        P(),
        P("phase", "space", None, None),
        P("phase", "space"),
        P("phase", "space"),
    )
    out_specs = (
        P(None, "phase", None, "space"),
        P(None, "phase", None, "space"),
        P(None, "phase", None, "space"),
        P(),
    )
    return jax.shard_map(shards, mesh=mesh, in_specs=in_specs, out_specs=out_specs, check_vma=False)
```

```python
import math

import jax
import jax.numpy as jnp
import ml_dtypes
import numpy as np
from jax import lax
from jax.experimental import pallas as pl
from jax.experimental.pallas import tpu as pltpu
from jax.sharding import PartitionSpec as P

amp_floor = 0.25
ridge = 1.0
tv_step = 0.25
shrink_level = 0.5

SIDE = 256
HALF = 128
BAND = 272
SPILL = BAND - SIDE
CORES, Z_SIZE, X_LO, Y_SIZE, X_SIZE = 2, 16, 2, 4, 4
GRAD_ROWS = 1024
TILES = X_SIZE // X_LO * Y_SIZE
PATCHES = 6
VMEM_BYTES = 50 * 1024 * 1024
PATCH_VMEM_BYTES = 36 * 1024 * 1024
GROUP = 2


def two_parts(table):
    high = table.astype(ml_dtypes.bfloat16)
    low = (table - high.astype(np.float64)).astype(ml_dtypes.bfloat16)
    return np.stack([high, low])


def half_tables():
    place = np.arange(HALF)
    tables = []
    for odd in (0, 1):
        turns = ((2 * place[:, None] + odd) * place[None, :]) % SIDE
        angle = -2.0 * np.pi * turns / SIDE
        re = np.cos(angle) / math.sqrt(SIDE)
        im = np.sin(angle) / math.sqrt(SIDE)
        real_form = np.block([[re, -im], [im, re]])
        tables.append(two_parts(real_form))
        tables.append(two_parts(real_form.T))
    return tables


def put_split(ref, rows, lanes, value):
    high = value.astype(jnp.bfloat16)
    ref[0, rows, lanes] = high
    ref[1, rows, lanes] = (value - high.astype(jnp.float32)).astype(jnp.bfloat16)


def dot(a, b):
    return jnp.dot(a, b, preferred_element_type=jnp.float32)


def table_dot(table, data):
    high, low = table[0], table[1]
    return dot(
        jnp.concatenate([high, high, low], 1),
        jnp.concatenate([data[0], data[1], data[0]], 0),
    )


def dot_table(data, table):
    high, low = table[0], table[1]
    return dot(
        jnp.concatenate([data[0], data[1], data[0]], 1),
        jnp.concatenate([high, high, low], 0),
    )


def rolled_probe(source, target, left):
    step = 64
    for start in range(0, SIDE, step):
        turned = pltpu.roll(source[start : start + step, :], left, 1)
        for side in range(2):
            lanes = slice(side * HALF, (side + 1) * HALF)
            target[side, SPILL + start : SPILL + start + step, :] = turned[:, lanes]
            if start + step == SIDE:
                target[side, 0:SPILL, :] = turned[step - SPILL :, lanes]


def patch_kernel(
    rows_s, cols_s, behind, own, halo, probe, le, let, lo, lot, amp,
    numer_own, numer_next, grad, weight,
    power, sorter, *scratch,
):
    first_slot = pl.program_id(0) * GROUP
    step = 16
    row_id = lax.broadcasted_iota(jnp.int32, (step, HALF), 0)
    lane_id = lax.broadcasted_iota(jnp.int32, (step, HALF), 1)
    re_half, im_half = slice(0, HALF), slice(HALF, SIDE)

    @pl.when(pl.program_id(0) == 0)
    def _():
        numer_own[...] = jnp.zeros_like(numer_own)
        numer_next[...] = jnp.zeros_like(numer_next)
        grad[...] = jnp.zeros_like(grad)
        weight[...] = jnp.full_like(weight, ridge)
        power[...] = probe[0] * probe[0] + probe[1] * probe[1]
        place = lax.broadcasted_iota(jnp.int32, (SIDE, SIDE), 0)
        target = lax.broadcasted_iota(jnp.int32, (SIDE, SIDE), 1)
        source = jnp.where(target < HALF, 2 * target, 2 * (target - HALF) + 1)
        sorter[...] = jnp.where(place == source, 1.0, 0.0).astype(jnp.bfloat16)

    def stages(member):
        brow, prow, pc, piece_s, wave_s, grow, xe, xo, ze, zo, amp_s, amp_c = scratch[
            member * 12 : member * 12 + 12
        ]
        slot = first_slot + member
        top, left = rows_s[0, slot], cols_s[0, slot]
        top_b, left_b = behind[0, slot], behind[1, slot]
        row_in = row_id >= top
        lane_in = [lane_id + side * HALF >= left for side in range(2)]
        lane_behind = [lane_id + side * HALF < left_b for side in range(2)]
        kept = {}

        def turn_probe():
            rolled_probe(probe.at[0], prow.at[0], left)
            rolled_probe(probe.at[1], prow.at[1], left)
            rolled_probe(power, brow, left_b)

        def sort_amplitudes():
            for side in range(2):
                amp_c[side] = amp[0, member, :, side * HALF : (side + 1) * HALF]
            for odd in range(2):
                part = jnp.concatenate(
                    [amp_c[side, pl.ds(odd, HALF, stride=2), :] for side in range(2)], 1
                )
                high = part.astype(jnp.bfloat16)
                low = (part - high.astype(jnp.float32)).astype(jnp.bfloat16)
                amp_s[odd * HALF : (odd + 1) * HALF, :] = dot(high, sorter[...]) + dot(low, sorter[...])

        def wave_rows(start, side):
            rows = slice(start, start + step)
            lanes = slice(side * HALF, (side + 1) * HALF)
            p = [prow[c, side, pl.ds(SPILL - top + start, step), :] for c in range(2)]
            piece = []
            for c in range(2):
                here = own[c, rows, lanes]
                there = halo[c, rows, lanes]
                if start == 0:
                    here = jnp.where(row_in, here, own[c, SIDE:BAND, lanes])
                    there = jnp.where(row_in, there, halo[c, SIDE:BAND, lanes])
                piece.append(jnp.where(lane_in[side], here, there))
                piece_s[c, rows, lanes] = piece[c]
                pc[c, rows, lanes] = p[c]
            wave = [p[0] * piece[0] - p[1] * piece[1], p[0] * piece[1] + p[1] * piece[0]]
            for c in range(2):
                wave_s[c, rows, lanes] = wave[c]
            mine = jnp.where(lane_in[side], p[0] * p[0] + p[1] * p[1], 0.0)
            theirs = brow[side, pl.ds(SPILL - top_b + start, step), :]
            theirs = jnp.where(lane_behind[side], theirs, 0.0)
            if start == 0:
                mine_in = jnp.where(row_in, mine, 0.0)
                theirs_in = jnp.where(row_id >= top_b, theirs, 0.0)
                weight[SIDE:BAND, lanes] += (mine - mine_in) + (theirs - theirs_in)
                mine, theirs = mine_in, theirs_in
            weight[rows, lanes] += mine + theirs
            return wave

        def waves():
            for start in range(0, HALF, step):
                for side in range(2):
                    lanes = slice(side * HALF, (side + 1) * HALF)
                    upper = wave_rows(start, side)
                    lower = wave_rows(start + HALF, side)
                    for c in range(2):
                        rows = slice(c * HALF + start, c * HALF + start + step)
                        put_split(xe, rows, lanes, upper[c] + lower[c])
                        put_split(xo, rows, lanes, upper[c] - lower[c])

        def over_rows(odd):
            mid = table_dot((le, lo)[odd], (xe, xo)[odd])
            rows = slice(odd * HALF, (odd + 1) * HALF)
            for part in (re_half, im_half):
                first, second = mid[part, re_half], mid[part, im_half]
                put_split(ze, rows, part, first + second)
                put_split(zo, rows, part, first - second)

        def over_columns(odd):
            far = dot_table((ze, zo)[odd], (let, lot)[odd])
            far_re, far_im = far[:, re_half], far[:, im_half]
            square = far_re * far_re + far_im * far_im
            factor = amp_s[:, odd * HALF : (odd + 1) * HALF] * lax.rsqrt(
                jnp.maximum(square, amp_floor * amp_floor)
            )
            put_split((xe, xo)[odd], slice(0, SIDE), re_half, far_re * factor)
            put_split((xe, xo)[odd], slice(0, SIDE), im_half, far_im * factor)

        def back_columns():
            even = dot_table(xe, le)
            odds = dot_table(xo, lo)
            for c, part in enumerate((re_half, im_half)):
                first, second = even[:, part], odds[:, part]
                for side, value in enumerate((first + second, first - second)):
                    lanes = slice(side * HALF, (side + 1) * HALF)
                    rows = slice(c * HALF, (c + 1) * HALF)
                    put_split(ze, rows, lanes, value[:HALF])
                    put_split(zo, rows, lanes, value[HALF:])

        def back_rows():
            kept["even"] = table_dot(let, ze)
            kept["odds"] = table_dot(lot, zo)

        def changes():
            even, odds = kept["even"], kept["odds"]
            for start in range(0, HALF, step):
                for side in range(2):
                    lanes = slice(side * HALF, (side + 1) * HALF)
                    spans = [slice(c * HALF + start, c * HALF + start + step) for c in range(2)]
                    first = [even[spans[c], lanes] for c in range(2)]
                    second = [odds[spans[c], lanes] for c in range(2)]
                    for lower in range(2):
                        begin = start + lower * HALF
                        rows = slice(begin, begin + step)
                        change = []
                        for c in range(2):
                            back = first[c] - second[c] if lower else first[c] + second[c]
                            change.append(back - wave_s[c, rows, lanes])
                        p = [pc[c, rows, lanes] for c in range(2)]
                        piece = [piece_s[c, rows, lanes] for c in range(2)]
                        numer = [
                            p[0] * change[0] + p[1] * change[1],
                            p[0] * change[1] - p[1] * change[0],
                        ]
                        turned = [
                            piece[0] * change[0] + piece[1] * change[1],
                            piece[0] * change[1] - piece[1] * change[0],
                        ]
                        for c in range(2):
                            grow[c, side, rows, :] = turned[c]
                            here = jnp.where(lane_in[side], numer[c], 0.0)
                            there = numer[c] - here
                            if begin == 0:
                                grow[c, side, SIDE:BAND, :] = turned[c]
                                for total, value in ((numer_own, here), (numer_next, there)):
                                    inside = jnp.where(row_in, value, 0.0)
                                    total[c, rows, lanes] += inside
                                    total[c, SIDE:BAND, lanes] += value - inside
                            else:
                                numer_own[c, rows, lanes] += here
                                numer_next[c, rows, lanes] += there

        def gradient():
            back_left = lax.rem(SIDE - left, SIDE)
            tall = 64
            for c in range(2):
                for start in range(0, SIDE, tall):
                    pair = [grow[c, side, pl.ds(top + start, tall), :] for side in range(2)]
                    value = pltpu.roll(jnp.concatenate(pair, 1), back_left, 1)
                    for side in range(2):
                        begin = (2 * c + side) * SIDE + start
                        grad[begin : begin + tall, :] += value[:, side * HALF : (side + 1) * HALF]

        return [
            turn_probe,
            waves,
            lambda: (over_rows(0), sort_amplitudes(), over_rows(1)),
            lambda: (over_columns(0), over_columns(1)),
            back_columns,
            back_rows,
            changes,
            gradient,
        ]

    ahead, after = stages(0), stages(1)
    lag = 3
    for turn in range(len(ahead) + lag):
        if turn < len(ahead):
            ahead[turn]()
        if turn >= lag:
            after[turn - lag]()

    @pl.when(pl.program_id(0) == pl.num_programs(0) - 1)
    def _():
        weight[...] = 1.0 / weight[...]


def patch_terms(rows, cols, behind, own, halo, probe, amplitudes):
    count = amplitudes.shape[1]
    tables = half_tables()
    whole = lambda *shape: pl.BlockSpec(shape, lambda k: (0,) * len(shape))
    scalars = pl.BlockSpec(memory_space=pltpu.SMEM)
    band = whole(2, BAND, SIDE)
    f32, bf16 = jnp.float32, jnp.bfloat16
    split = pltpu.VMEM((2, SIDE, SIDE), bf16)
    square = pltpu.VMEM((2, SIDE, SIDE), f32)
    member = [
        pltpu.VMEM((2, BAND, HALF), f32),
        pltpu.VMEM((2, 2, BAND, HALF), f32),
        square, square, square,
        pltpu.VMEM((2, 2, BAND, HALF), f32),
        split, split, split, split,
        pltpu.VMEM((SIDE, SIDE), f32),
        pltpu.VMEM((2, SIDE, HALF), f32),
    ]
    return pl.pallas_call(
        patch_kernel,
        grid=(count // GROUP,),
        in_specs=[scalars, scalars, scalars, band, band, whole(2, SIDE, SIDE)]
        + [whole(2, SIDE, SIDE)] * 4
        + [pl.BlockSpec((1, GROUP, SIDE, SIDE), lambda k: (0, k, 0, 0))],
        out_specs=[band, band, whole(GRAD_ROWS, HALF), whole(BAND, SIDE)],
        out_shape=[
            jax.ShapeDtypeStruct((2, BAND, SIDE), f32),
            jax.ShapeDtypeStruct((2, BAND, SIDE), f32),
            jax.ShapeDtypeStruct((GRAD_ROWS, HALF), f32),
            jax.ShapeDtypeStruct((BAND, SIDE), f32),
        ],
        scratch_shapes=[pltpu.VMEM((SIDE, SIDE), f32), pltpu.VMEM((SIDE, SIDE), bf16)]
        + member * GROUP,
        compiler_params=pltpu.CompilerParams(
            dimension_semantics=("arbitrary",), vmem_limit_bytes=PATCH_VMEM_BYTES
        ),
        cost_estimate=pl.CostEstimate(
            flops=count * 26 * 2 * SIDE**3, bytes_accessed=6 * 2**20, transcendentals=0
        ),
        name="patch_terms",
    )(rows, cols, behind, own, halo, probe, *[jnp.asarray(t) for t in tables], amplitudes)


class Place:
    def __init__(self):
        self.phase, self.space = lax.axis_index("phase"), lax.axis_index("space")
        self.core = lax.rem(self.phase, CORES)
        self.z = lax.rem(self.phase // CORES, Z_SIZE)
        x_lo = self.phase // (CORES * Z_SIZE)
        self.y = lax.rem(self.space, Y_SIZE)
        self.x_hi = self.space // Y_SIZE
        self.x = self.x_hi * X_LO + x_lo

    def device(self, core, z, x, y):
        phase = (lax.rem(x, X_LO) * Z_SIZE + z) * CORES + core
        return (phase, (x // X_LO) * Y_SIZE + y)

    def core_peer(self):
        return self.device(1 - self.core, self.z, self.x, self.y)

    def x_peer(self, k):
        return self.device(self.core, self.z, lax.rem(self.x + k, X_SIZE), self.y)

    def y_peer(self, k):
        return self.device(self.core, self.z, self.x, lax.rem(self.y + k, Y_SIZE))

    def z_peer(self, k):
        return self.device(self.core, lax.rem(self.z + k, Z_SIZE), self.x, self.y)

    def over_cut(self):
        return self.device(self.core, self.z, X_SIZE - 1 - self.x, self.y)

    def beside(self, k):
        other = self.x + 1 - 2 * lax.rem(self.x, X_LO)
        return self.device(self.core, self.z, other, lax.rem(self.y + k, Y_SIZE))

    def bin_at(self, k):
        count = lax.axis_size("phase")
        return (lax.rem(self.phase + k + count, count), self.space)

    def tile_at(self, k):
        count = lax.axis_size("space")
        return (self.phase, lax.rem(self.space + k + count, count))


def remote(src, dst, s, v, target):
    return pltpu.make_async_remote_copy(
        src_ref=src, dst_ref=dst, send_sem=s, recv_sem=v,
        device_id=target, device_id_type=pl.DeviceIdType.MESH,
    )


def greet(target):
    pl.semaphore_signal(
        pltpu.get_barrier_semaphore(), inc=1, device_id=target, device_id_type=pl.DeviceIdType.MESH
    )


ROW_CUTS = (0, 72, 136, 208, 272)
CHUNKS = tuple(
    (part, slice(ROW_CUTS[i], ROW_CUTS[i + 1])) for i in range(len(ROW_CUTS) - 1) for part in range(2)
)
EDGE = Y_SIZE


def chunk_of(ref, index):
    part, rows = CHUNKS[index]
    return ref.at[part, pl.ds(rows.start, rows.stop - rows.start), :]


def opening_kernel(
    own_h, split_h, dual_h, rows_h, cols_h,
    halo, steady, behind,
    own, split, dual, rows, cols, start_point, following, preceding, offsets, via,
    ls, hs, hv, rs, rv, ns, nv, ps, pv, os, ov,
):
    me = Place()
    last = TILES - 1
    count = range(len(CHUNKS))
    loads = [
        pltpu.make_async_copy(src, dst, ls.at[i])
        for i, (src, dst) in enumerate(
            ((own_h, own), (split_h, split), (dual_h, dual), (rows_h, rows), (cols_h, cols))
        )
    ]
    for load in loads:
        load.start()
    for target in (me.tile_at(1), me.tile_at(-1), me.bin_at(1), me.bin_at(-1)):
        greet(target)
    greet(me.over_cut())
    greet(me.beside(1))
    greet(me.beside(Y_SIZE - 1))

    @pl.when(me.space == 0)
    def _():
        behind[...] = jnp.zeros_like(behind)

    loads[0].wait()
    pl.semaphore_wait(pltpu.get_barrier_semaphore(), 7)

    def halo_copy(index):
        return remote(
            chunk_of(own, index), chunk_of(halo, index), hs.at[index], hv.at[index], me.tile_at(-1)
        )

    def cut_copy(index):
        return remote(
            chunk_of(own, index), chunk_of(via, index), hs.at[index], rv.at[index], me.over_cut()
        )

    def relay(index):
        return remote(
            chunk_of(via, index), chunk_of(halo, index), rs.at[index], hv.at[index],
            me.beside(Y_SIZE - 1),
        )

    @pl.when(me.space == EDGE)
    def _():
        for index in count:
            cut_copy(index).start()

    @pl.when(jnp.logical_and(me.space > 0, me.space != EDGE))
    def _():
        for index in count:
            halo_copy(index).start()

    to_preceding = remote(own, following, ns, nv, me.bin_at(-1))
    to_following = remote(start_point, preceding, ps, pv, me.bin_at(1))
    offsets_on = remote(offsets, behind, os, ov, me.tile_at(1))
    to_preceding.start()
    for load in loads[1:]:
        load.wait()
    offsets[...] = jnp.zeros_like(offsets)
    offsets[0:1, 0 : rows.shape[1]] = rows[...]
    offsets[1:2, 0 : cols.shape[1]] = cols[...]

    @pl.when(me.space < last)
    def _():
        offsets_on.start()

    start_point[...] = own[...] + split[...] - dual[...]
    to_following.start()

    @pl.when(me.space == 0)
    def _():
        for index in count:
            cut_copy(index).wait_recv()
            relay(index).start()

    to_preceding.wait()
    to_following.wait()
    steady[...] = own[...] - tv_step * (
        (own[...] - preceding[...]) - (following[...] - start_point[...])
    )

    @pl.when(me.space > 0)
    def _():
        offsets_on.wait_recv()
        for index in count:
            halo_copy(index).wait_send()

    @pl.when(me.space < last)
    def _():
        offsets_on.wait_send()
        for index in count:
            halo_copy(index).wait_recv()

    @pl.when(me.space == 0)
    def _():
        for index in count:
            relay(index).wait_send()


def opening(own, split, dual, rows, cols):
    f32, i32 = jnp.float32, jnp.int32
    dma = pltpu.SemaphoreType.DMA
    vmem = pl.BlockSpec(memory_space=pltpu.VMEM)
    room = pltpu.VMEM((2, BAND, SIDE), f32)
    many = dma((len(CHUNKS),))
    band = jax.ShapeDtypeStruct((2, BAND, SIDE), f32)
    return pl.pallas_call(
        opening_kernel,
        in_specs=[pl.BlockSpec(memory_space=pl.ANY)] * 5,
        out_specs=[vmem] * 3,
        out_shape=[band, band, jax.ShapeDtypeStruct((8, HALF), i32)],
        scratch_shapes=[
            room, room, room, pltpu.VMEM(rows.shape, i32), pltpu.VMEM(cols.shape, i32),
            room, room, room, pltpu.VMEM((8, HALF), i32), room,
            dma((5,)), many, many, many, many,
            dma, dma, dma, dma, dma, dma,
        ],
        compiler_params=pltpu.CompilerParams(
            collective_id=0, has_side_effects=True, vmem_limit_bytes=VMEM_BYTES
        ),
        cost_estimate=pl.CostEstimate(flops=2**20, bytes_accessed=2**24, transcendentals=0),
        name="opening",
    )(own, split, dual, rows, cols)


def tail_kernel(
    numer_own, numer_next, inverse, steady, term,
    updated, next_updated, out,
    inc, via, r1, a1, r2, a2, r3, r4, a4, f2, f1, f0,
    cs, cv, rs, rv, us, uv,
    s1, v1, s2, v2, s3, v3, s4, v4, s5, v5, s6, v6, s7, v7,
):
    me = Place()
    core, x, y, z = me.core, me.x, me.y, me.z
    last = TILES - 1

    greet(me.core_peer())
    for k in range(1, X_SIZE):
        greet(me.x_peer(k))
    for k in range(1, Y_SIZE):
        greet(me.y_peer(k))
    for target in (me.tile_at(1), me.tile_at(-1), me.bin_at(1), me.bin_at(-1)):
        greet(target)
    greet(me.over_cut())
    greet(me.beside(1))
    greet(me.beside(Y_SIZE - 1))

    def greet_z(k, carry):
        greet(me.z_peer(k))
        return carry

    lax.fori_loop(1, Z_SIZE, greet_z, 0)
    pl.semaphore_wait(
        pltpu.get_barrier_semaphore(), 1 + (X_SIZE - 1) + (Y_SIZE - 1) + 7 + (Z_SIZE - 1)
    )

    count = range(len(CHUNKS))

    def correction(index):
        return remote(
            chunk_of(numer_next, index), chunk_of(inc, index), cs.at[index], cv.at[index], me.tile_at(1)
        )

    def cut_copy(index):
        return remote(
            chunk_of(numer_next, index), chunk_of(via, index), cs.at[index], rv.at[index], me.over_cut()
        )

    def relay(index):
        return remote(
            chunk_of(via, index), chunk_of(inc, index), rs.at[index], cv.at[index], me.beside(1)
        )

    def relay_on(index):
        @pl.when(me.space == last)
        def _():
            cut_copy(index).wait_recv()
            relay(index).start()

    def updated_copy(index):
        return remote(
            chunk_of(updated, index), chunk_of(next_updated, index), us.at[index], uv.at[index],
            me.bin_at(-1),
        )

    @pl.when(jnp.logical_and(me.space < last, me.space != EDGE - 1))
    def _():
        for index in count:
            correction(index).start()

    part1 = GRAD_ROWS // CORES
    part2 = part1 // X_SIZE
    part3 = part2 // Z_SIZE

    def span(index, size):
        return pl.ds(pl.multiple_of(index * size, size), size)

    copy = remote(term.at[span(1 - core, part1)], r1, s1, v1, me.core_peer())
    copy.start()
    copy.wait()
    a1[...] = term[span(core, part1), :] + r1[...]

    copies = []
    for k in range(1, X_SIZE):
        target = lax.rem(x + k, X_SIZE)
        copies.append(
            remote(a1.at[span(target, part2)], r2.at[k - 1], s2.at[k - 1], v2.at[k - 1], me.x_peer(k))
        )
    for copy in copies:
        copy.start()
    for copy in copies:
        copy.wait()
    @pl.when(me.space == EDGE - 1)
    def _():
        for index in count:
            cut_copy(index).start()

    a2[...] = a1[span(x, part2), :] + r2[0] + r2[1] + r2[2]

    def z_sum(k):
        target = lax.rem(z + k, Z_SIZE)
        return remote(a2.at[span(target, part3)], r3.at[k - 1], s3.at[k - 1], v3.at[k - 1], me.z_peer(k))

    def start_z_sum(k, carry):
        z_sum(k).start()
        return carry

    def wait_z_sum(k, carry):
        z_sum(k).wait()
        return carry

    lax.fori_loop(1, Z_SIZE, start_z_sum, 0)
    lax.fori_loop(1, Z_SIZE, wait_z_sum, 0)
    relay_on(0)
    relay_on(1)
    total = a2[span(z, part3), :]
    for k in range(Z_SIZE - 1):
        total = total + r3[k]

    r4[y] = total
    copies = [
        remote(r4.at[y], r4.at[y], s4.at[k - 1], v4.at[k - 1], me.y_peer(k)) for k in range(1, Y_SIZE)
    ]
    for copy in copies:
        copy.start()
    relay_on(2)
    for copy in copies:
        copy.wait()
    terms = PATCHES * lax.axis_size("phase") * lax.axis_size("space")
    a4[...] = ((r4[0] + r4[1]) + (r4[2] + r4[3])) * (1.0 / math.sqrt(terms))

    f2[span(z, part3), :] = a4[...]

    def z_spread(k):
        return remote(a4, f2.at[span(z, part3)], s5.at[k - 1], v5.at[k - 1], me.z_peer(k))

    def start_z_spread(k, carry):
        z_spread(k).start()
        return carry

    def wait_z_spread(k, carry):
        z_spread(k).wait()
        return carry

    lax.fori_loop(1, Z_SIZE, start_z_spread, 0)

    for index in count:
        part, rows = CHUNKS[index]
        if index + 3 < len(CHUNKS):
            relay_on(index + 3)

        @pl.when(me.space > 0)
        def _():
            correction(index).wait_recv()
            numer = numer_own[part, rows, :] + inc[part, rows, :]
            updated[part, rows, :] = steady[part, rows, :] + numer * inverse[rows, :]

        @pl.when(me.space == 0)
        def _():
            updated[part, rows, :] = steady[part, rows, :] + numer_own[part, rows, :] * inverse[rows, :]

        updated_copy(index).start()

    lax.fori_loop(1, Z_SIZE, wait_z_spread, 0)

    copies = [
        remote(f2, f1.at[span(x, part2)], s6.at[k - 1], v6.at[k - 1], me.x_peer(k))
        for k in range(1, X_SIZE)
    ]
    for copy in copies:
        copy.start()
    f1[span(x, part2), :] = f2[...]
    for copy in copies:
        copy.wait()

    copy = remote(f1, f0.at[span(core, part1)], s7, v7, me.core_peer())
    copy.start()
    f0[span(core, part1), :] = f1[...]
    copy.wait()
    for c in range(2):
        for side in range(2):
            begin = (2 * c + side) * SIDE
            out[c, :, side * HALF : (side + 1) * HALF] = f0[begin : begin + SIDE, :]

    for index in count:
        updated_copy(index).wait()

    @pl.when(me.space < last)
    def _():
        for index in count:
            correction(index).wait_send()

    @pl.when(me.space == last)
    def _():
        for index in count:
            relay(index).wait_send()


def tail(numer_own, numer_next, inverse, steady, term):
    part1 = GRAD_ROWS // CORES
    part2 = part1 // X_SIZE
    part3 = part2 // Z_SIZE
    f32 = jnp.float32
    dma = pltpu.SemaphoreType.DMA
    vmem = pl.BlockSpec(memory_space=pltpu.VMEM)
    room = pltpu.VMEM((2, BAND, SIDE), f32)
    many = dma((len(CHUNKS),))
    band = jax.ShapeDtypeStruct((2, BAND, SIDE), f32)
    sems = []
    for count in (1, X_SIZE - 1, Z_SIZE - 1, Y_SIZE - 1, Z_SIZE - 1, X_SIZE - 1, 1):
        sems += [dma if count == 1 else dma((count,))] * 2
    return pl.pallas_call(
        tail_kernel,
        in_specs=[vmem] * 5,
        out_specs=[vmem] * 3,
        out_shape=[band, band, jax.ShapeDtypeStruct((2, SIDE, SIDE), f32)],
        scratch_shapes=[
            room, room,
            pltpu.VMEM((part1, HALF), f32),
            pltpu.VMEM((part1, HALF), f32),
            pltpu.VMEM((X_SIZE - 1, part2, HALF), f32),
            pltpu.VMEM((part2, HALF), f32),
            pltpu.VMEM((Z_SIZE - 1, part3, HALF), f32),
            pltpu.VMEM((Y_SIZE, part3, HALF), f32),
            pltpu.VMEM((part3, HALF), f32),
            pltpu.VMEM((part2, HALF), f32),
            pltpu.VMEM((part1, HALF), f32),
            pltpu.VMEM((GRAD_ROWS, HALF), f32),
            many, many, many, many, many, many,
            *sems,
        ],
        compiler_params=pltpu.CompilerParams(
            collective_id=1, has_side_effects=True, vmem_limit_bytes=VMEM_BYTES
        ),
        cost_estimate=pl.CostEstimate(flops=2**20, bytes_accessed=2**24, transcendentals=0),
        name="tail",
    )(numer_own, numer_next, inverse, steady, term)


def finish_kernel(updated, next_updated, dual, summed, out_object, out_split, out_dual, out_sum):
    out_object[...] = updated[...]
    out_sum[...] = summed[...]
    joint = [next_updated[c] - updated[c] + dual[c] for c in range(2)]
    size_abs = jnp.sqrt(joint[0] * joint[0] + joint[1] * joint[1])
    shrink = jnp.maximum(size_abs - shrink_level, 0.0) / jnp.maximum(size_abs, shrink_level)
    for c in range(2):
        new_split = joint[c] * shrink
        out_split[c] = new_split
        out_dual[c] = joint[c] - new_split


def finish(updated, next_updated, dual, summed):
    steps = 2
    f32 = jnp.float32
    band = pl.BlockSpec((2, BAND // steps, SIDE), lambda i: (0, i, 0))
    grad = pl.BlockSpec((2, SIDE // steps, SIDE), lambda i: (0, i, 0))
    band_shape = jax.ShapeDtypeStruct((2, BAND, SIDE), f32)
    return pl.pallas_call(
        finish_kernel,
        grid=(steps,),
        in_specs=[band, band, band, grad],
        out_specs=[band, band, band, grad],
        out_shape=[band_shape] * 3 + [jax.ShapeDtypeStruct((2, SIDE, SIDE), f32)],
        compiler_params=pltpu.CompilerParams(
            dimension_semantics=("arbitrary",), vmem_limit_bytes=VMEM_BYTES
        ),
        cost_estimate=pl.CostEstimate(flops=2**20, bytes_accessed=2**22, transcendentals=0),
        name="finish",
    )(updated, next_updated, dual, summed)


def shards(object_field, split_field, scaled_dual, probe, amplitudes, row_offsets, col_offsets):
    own = object_field[:, 0]
    split_own = split_field[:, 0]
    dual_own = scaled_dual[:, 0]
    halo, steady, behind = opening(own, split_own, dual_own, row_offsets, col_offsets)
    numer_own, numer_next, grad, inverse = patch_terms(
        row_offsets, col_offsets, behind, own, halo, probe, amplitudes
    )
    updated, next_updated, summed = tail(numer_own, numer_next, inverse, steady, grad)
    updated, new_split, new_dual, probe_gradient = finish(updated, next_updated, dual_own, summed)
    return (updated[:, None], new_split[:, None], new_dual[:, None], probe_gradient)


def solution(mesh):
    in_specs = (
        P(None, "phase", None, "space"),
        P(None, "phase", None, "space"),
        P(None, "phase", None, "space"),
        P(),
        P("phase", "space", None, None),
        P("phase", "space"),
        P("phase", "space"),
    )
    out_specs = (
        P(None, "phase", None, "space"),
        P(None, "phase", None, "space"),
        P(None, "phase", None, "space"),
        P(),
    )
    return jax.shard_map(shards, mesh=mesh, in_specs=in_specs, out_specs=out_specs, check_vma=False)
```

```python
import math

import jax
import jax.numpy as jnp
import ml_dtypes
import numpy as np
from jax import lax
from jax.experimental import pallas as pl
from jax.experimental.pallas import tpu as pltpu
from jax.sharding import PartitionSpec as P

amp_floor = 0.25
ridge = 1.0
tv_step = 0.25
shrink_level = 0.5

SIDE = 256
HALF = 128
BAND = 272
SPILL = BAND - SIDE
CORES, Z_SIZE, X_LO, Y_SIZE, X_SIZE = 2, 16, 2, 4, 4
GRAD_ROWS = 1024
TILES = X_SIZE // X_LO * Y_SIZE
PATCHES = 6
VMEM_BYTES = 58 * 1024 * 1024
GROUP = 2


def two_parts(table):
    high = table.astype(ml_dtypes.bfloat16)
    low = (table - high.astype(np.float64)).astype(ml_dtypes.bfloat16)
    return np.stack([high, low])


def half_tables():
    place = np.arange(HALF)
    tables = []
    for odd in (0, 1):
        turns = ((2 * place[:, None] + odd) * place[None, :]) % SIDE
        angle = -2.0 * np.pi * turns / SIDE
        re = np.cos(angle) / math.sqrt(SIDE)
        im = np.sin(angle) / math.sqrt(SIDE)
        real_form = np.block([[re, -im], [im, re]])
        tables.append(two_parts(real_form))
        tables.append(two_parts(real_form.T))
    return tables


def put_split(ref, rows, lanes, value):
    high = value.astype(jnp.bfloat16)
    ref[0, rows, lanes] = high
    ref[1, rows, lanes] = (value - high.astype(jnp.float32)).astype(jnp.bfloat16)


def dot(a, b):
    return jnp.dot(a, b, preferred_element_type=jnp.float32)


def table_dot(table, data):
    high, low = table[0], table[1]
    return dot(
        jnp.concatenate([high, high, low], 1),
        jnp.concatenate([data[0], data[1], data[0]], 0),
    )


def dot_table(data, table):
    high, low = table[0], table[1]
    return dot(
        jnp.concatenate([data[0], data[1], data[0]], 1),
        jnp.concatenate([high, high, low], 0),
    )


def rolled_probe(source, target, left):
    step = 64
    for start in range(0, SIDE, step):
        turned = pltpu.roll(source[start : start + step, :], left, 1)
        for side in range(2):
            lanes = slice(side * HALF, (side + 1) * HALF)
            target[side, SPILL + start : SPILL + start + step, :] = turned[:, lanes]
            if start + step == SIDE:
                target[side, 0:SPILL, :] = turned[step - SPILL :, lanes]


def patch_kernel(
    rows_s, cols_s, behind, own, halo, probe, le_h, let_h, lo_h, lot_h, amp_h,
    numer_own, numer_next, grad, weight,
    power, sorter, le, let, lo, lot, amp, table_sems, amp_sems, *scratch,
):
    group = pl.program_id(0)
    groups = amp.shape[0] // GROUP
    tables = [
        pltpu.make_async_copy(src, dst, table_sems.at[i])
        for i, (src, dst) in enumerate(((le_h, le), (let_h, let), (lo_h, lo), (lot_h, lot)))
    ]

    def amp_load(index):
        rows = pl.ds(index * GROUP, GROUP)
        return pltpu.make_async_copy(amp_h.at[0, rows], amp.at[rows], amp_sems.at[index])

    first_slot = pl.program_id(0) * GROUP
    step = 16
    row_id = lax.broadcasted_iota(jnp.int32, (step, HALF), 0)
    lane_id = lax.broadcasted_iota(jnp.int32, (step, HALF), 1)
    re_half, im_half = slice(0, HALF), slice(HALF, SIDE)

    @pl.when(group == 0)
    def _():
        for load in tables:
            load.start()
        for index in range(groups):
            amp_load(index).start()
        numer_own[...] = jnp.zeros_like(numer_own)
        numer_next[...] = jnp.zeros_like(numer_next)
        grad[...] = jnp.zeros_like(grad)
        weight[...] = jnp.full_like(weight, ridge)
        power[...] = probe[0] * probe[0] + probe[1] * probe[1]
        place = lax.broadcasted_iota(jnp.int32, (SIDE, SIDE), 0)
        target = lax.broadcasted_iota(jnp.int32, (SIDE, SIDE), 1)
        source = jnp.where(target < HALF, 2 * target, 2 * (target - HALF) + 1)
        sorter[...] = jnp.where(place == source, 1.0, 0.0).astype(jnp.bfloat16)
        for load in tables:
            load.wait()

    amp_load(group).wait()

    def stages(member):
        brow, prow, pc, piece_s, wave_s, grow, xe, xo, ze, zo, amp_s, amp_c = scratch[
            member * 12 : member * 12 + 12
        ]
        slot = first_slot + member
        top, left = rows_s[0, slot], cols_s[0, slot]
        top_b, left_b = behind[0, slot], behind[1, slot]
        row_in = row_id >= top
        lane_in = [lane_id + side * HALF >= left for side in range(2)]
        lane_behind = [lane_id + side * HALF < left_b for side in range(2)]
        kept = {}

        def turn_probe():
            rolled_probe(probe.at[0], prow.at[0], left)
            rolled_probe(probe.at[1], prow.at[1], left)
            rolled_probe(power, brow, left_b)

        def sort_amplitudes():
            for side in range(2):
                amp_c[side] = amp[slot, :, side * HALF : (side + 1) * HALF]
            for odd in range(2):
                part = jnp.concatenate(
                    [amp_c[side, pl.ds(odd, HALF, stride=2), :] for side in range(2)], 1
                )
                high = part.astype(jnp.bfloat16)
                low = (part - high.astype(jnp.float32)).astype(jnp.bfloat16)
                amp_s[odd * HALF : (odd + 1) * HALF, :] = dot(high, sorter[...]) + dot(low, sorter[...])

        def wave_rows(start, side):
            rows = slice(start, start + step)
            lanes = slice(side * HALF, (side + 1) * HALF)
            p = [prow[c, side, pl.ds(SPILL - top + start, step), :] for c in range(2)]
            piece = []
            for c in range(2):
                here = own[c, rows, lanes]
                there = halo[c, rows, lanes]
                if start == 0:
                    here = jnp.where(row_in, here, own[c, SIDE:BAND, lanes])
                    there = jnp.where(row_in, there, halo[c, SIDE:BAND, lanes])
                piece.append(jnp.where(lane_in[side], here, there))
                piece_s[c, rows, lanes] = piece[c]
                pc[c, rows, lanes] = p[c]
            wave = [p[0] * piece[0] - p[1] * piece[1], p[0] * piece[1] + p[1] * piece[0]]
            for c in range(2):
                wave_s[c, rows, lanes] = wave[c]
            mine = jnp.where(lane_in[side], p[0] * p[0] + p[1] * p[1], 0.0)
            theirs = brow[side, pl.ds(SPILL - top_b + start, step), :]
            theirs = jnp.where(lane_behind[side], theirs, 0.0)
            if start == 0:
                mine_in = jnp.where(row_in, mine, 0.0)
                theirs_in = jnp.where(row_id >= top_b, theirs, 0.0)
                weight[SIDE:BAND, lanes] += (mine - mine_in) + (theirs - theirs_in)
                mine, theirs = mine_in, theirs_in
            weight[rows, lanes] += mine + theirs
            return wave

        def waves():
            for start in range(0, HALF, step):
                for side in range(2):
                    lanes = slice(side * HALF, (side + 1) * HALF)
                    upper = wave_rows(start, side)
                    lower = wave_rows(start + HALF, side)
                    for c in range(2):
                        rows = slice(c * HALF + start, c * HALF + start + step)
                        put_split(xe, rows, lanes, upper[c] + lower[c])
                        put_split(xo, rows, lanes, upper[c] - lower[c])

        def over_rows(odd):
            mid = table_dot((le, lo)[odd], (xe, xo)[odd])
            rows = slice(odd * HALF, (odd + 1) * HALF)
            for part in (re_half, im_half):
                first, second = mid[part, re_half], mid[part, im_half]
                put_split(ze, rows, part, first + second)
                put_split(zo, rows, part, first - second)

        def over_columns(odd):
            far = dot_table((ze, zo)[odd], (let, lot)[odd])
            far_re, far_im = far[:, re_half], far[:, im_half]
            square = far_re * far_re + far_im * far_im
            factor = amp_s[:, odd * HALF : (odd + 1) * HALF] * lax.rsqrt(
                jnp.maximum(square, amp_floor * amp_floor)
            )
            put_split((xe, xo)[odd], slice(0, SIDE), re_half, far_re * factor)
            put_split((xe, xo)[odd], slice(0, SIDE), im_half, far_im * factor)

        def back_columns():
            even = dot_table(xe, le)
            odds = dot_table(xo, lo)
            for c, part in enumerate((re_half, im_half)):
                first, second = even[:, part], odds[:, part]
                for side, value in enumerate((first + second, first - second)):
                    lanes = slice(side * HALF, (side + 1) * HALF)
                    rows = slice(c * HALF, (c + 1) * HALF)
                    put_split(ze, rows, lanes, value[:HALF])
                    put_split(zo, rows, lanes, value[HALF:])

        def back_rows():
            kept["even"] = table_dot(let, ze)
            kept["odds"] = table_dot(lot, zo)

        def changes():
            even, odds = kept["even"], kept["odds"]
            for start in range(0, HALF, step):
                for side in range(2):
                    lanes = slice(side * HALF, (side + 1) * HALF)
                    spans = [slice(c * HALF + start, c * HALF + start + step) for c in range(2)]
                    first = [even[spans[c], lanes] for c in range(2)]
                    second = [odds[spans[c], lanes] for c in range(2)]
                    for lower in range(2):
                        begin = start + lower * HALF
                        rows = slice(begin, begin + step)
                        change = []
                        for c in range(2):
                            back = first[c] - second[c] if lower else first[c] + second[c]
                            change.append(back - wave_s[c, rows, lanes])
                        p = [pc[c, rows, lanes] for c in range(2)]
                        piece = [piece_s[c, rows, lanes] for c in range(2)]
                        numer = [
                            p[0] * change[0] + p[1] * change[1],
                            p[0] * change[1] - p[1] * change[0],
                        ]
                        turned = [
                            piece[0] * change[0] + piece[1] * change[1],
                            piece[0] * change[1] - piece[1] * change[0],
                        ]
                        for c in range(2):
                            grow[c, side, rows, :] = turned[c]
                            here = jnp.where(lane_in[side], numer[c], 0.0)
                            there = numer[c] - here
                            if begin == 0:
                                grow[c, side, SIDE:BAND, :] = turned[c]
                                for total, value in ((numer_own, here), (numer_next, there)):
                                    inside = jnp.where(row_in, value, 0.0)
                                    total[c, rows, lanes] += inside
                                    total[c, SIDE:BAND, lanes] += value - inside
                            else:
                                numer_own[c, rows, lanes] += here
                                numer_next[c, rows, lanes] += there

        def gradient():
            back_left = lax.rem(SIDE - left, SIDE)
            tall = 64
            for c in range(2):
                for start in range(0, SIDE, tall):
                    pair = [grow[c, side, pl.ds(top + start, tall), :] for side in range(2)]
                    value = pltpu.roll(jnp.concatenate(pair, 1), back_left, 1)
                    for side in range(2):
                        begin = (2 * c + side) * SIDE + start
                        grad[begin : begin + tall, :] += value[:, side * HALF : (side + 1) * HALF]

        return [
            turn_probe,
            waves,
            lambda: (over_rows(0), sort_amplitudes(), over_rows(1)),
            lambda: (over_columns(0), over_columns(1)),
            back_columns,
            back_rows,
            changes,
            gradient,
        ]

    ahead, after = stages(0), stages(1)
    lag = 3
    for turn in range(len(ahead) + lag):
        if turn < len(ahead):
            ahead[turn]()
        if turn >= lag:
            after[turn - lag]()

    @pl.when(pl.program_id(0) == pl.num_programs(0) - 1)
    def _():
        weight[...] = 1.0 / weight[...]


def patch_terms(rows, cols, behind, own, halo, probe, amplitudes):
    count = amplitudes.shape[1]
    tables = half_tables()
    whole = lambda *shape: pl.BlockSpec(shape, lambda k: (0,) * len(shape))
    scalars = pl.BlockSpec(memory_space=pltpu.SMEM)
    band = whole(2, BAND, SIDE)
    f32, bf16 = jnp.float32, jnp.bfloat16
    split = pltpu.VMEM((2, SIDE, SIDE), bf16)
    square = pltpu.VMEM((2, SIDE, SIDE), f32)
    member = [
        pltpu.VMEM((2, BAND, HALF), f32),
        pltpu.VMEM((2, 2, BAND, HALF), f32),
        square, square, square,
        pltpu.VMEM((2, 2, BAND, HALF), f32),
        split, split, split, split,
        pltpu.VMEM((SIDE, SIDE), f32),
        pltpu.VMEM((2, SIDE, HALF), f32),
    ]
    return pl.pallas_call(
        patch_kernel,
        grid=(count // GROUP,),
        in_specs=[scalars, scalars, scalars, band, band, whole(2, SIDE, SIDE)]
        + [pl.BlockSpec(memory_space=pltpu.HBM)] * 5,
        out_specs=[band, band, whole(GRAD_ROWS, HALF), whole(BAND, SIDE)],
        out_shape=[
            jax.ShapeDtypeStruct((2, BAND, SIDE), f32),
            jax.ShapeDtypeStruct((2, BAND, SIDE), f32),
            jax.ShapeDtypeStruct((GRAD_ROWS, HALF), f32),
            jax.ShapeDtypeStruct((BAND, SIDE), f32),
        ],
        scratch_shapes=[pltpu.VMEM((SIDE, SIDE), f32), pltpu.VMEM((SIDE, SIDE), bf16)]
        + [split] * 4
        + [
            pltpu.VMEM((count, SIDE, SIDE), f32),
            pltpu.SemaphoreType.DMA((4,)),
            pltpu.SemaphoreType.DMA((count // GROUP,)),
        ]
        + member * GROUP,
        compiler_params=pltpu.CompilerParams(
            dimension_semantics=("arbitrary",), vmem_limit_bytes=VMEM_BYTES
        ),
        cost_estimate=pl.CostEstimate(
            flops=count * 26 * 2 * SIDE**3, bytes_accessed=6 * 2**20, transcendentals=0
        ),
        name="patch_terms",
    )(rows, cols, behind, own, halo, probe, *[jnp.asarray(t) for t in tables], amplitudes)


class Place:
    def __init__(self):
        self.phase, self.space = lax.axis_index("phase"), lax.axis_index("space")
        self.core = lax.rem(self.phase, CORES)
        self.z = lax.rem(self.phase // CORES, Z_SIZE)
        x_lo = self.phase // (CORES * Z_SIZE)
        self.y = lax.rem(self.space, Y_SIZE)
        self.x_hi = self.space // Y_SIZE
        self.x = self.x_hi * X_LO + x_lo

    def device(self, core, z, x, y):
        phase = (lax.rem(x, X_LO) * Z_SIZE + z) * CORES + core
        return (phase, (x // X_LO) * Y_SIZE + y)

    def core_peer(self):
        return self.device(1 - self.core, self.z, self.x, self.y)

    def x_peer(self, k):
        return self.device(self.core, self.z, lax.rem(self.x + k, X_SIZE), self.y)

    def y_peer(self, k):
        return self.device(self.core, self.z, self.x, lax.rem(self.y + k, Y_SIZE))

    def z_peer(self, k):
        return self.device(self.core, lax.rem(self.z + k, Z_SIZE), self.x, self.y)

    def over_cut(self):
        return self.device(self.core, self.z, X_SIZE - 1 - self.x, self.y)

    def beside(self, k):
        other = self.x + 1 - 2 * lax.rem(self.x, X_LO)
        return self.device(self.core, self.z, other, lax.rem(self.y + k, Y_SIZE))

    def bin_at(self, k):
        count = lax.axis_size("phase")
        return (lax.rem(self.phase + k + count, count), self.space)

    def tile_at(self, k):
        count = lax.axis_size("space")
        return (self.phase, lax.rem(self.space + k + count, count))


def remote(src, dst, s, v, target):
    return pltpu.make_async_remote_copy(
        src_ref=src, dst_ref=dst, send_sem=s, recv_sem=v,
        device_id=target, device_id_type=pl.DeviceIdType.MESH,
    )


def greet(target):
    pl.semaphore_signal(
        pltpu.get_barrier_semaphore(), inc=1, device_id=target, device_id_type=pl.DeviceIdType.MESH
    )


ROW_CUTS = (0, 72, 136, 208, 272)
CHUNKS = tuple(
    (part, slice(ROW_CUTS[i], ROW_CUTS[i + 1])) for i in range(len(ROW_CUTS) - 1) for part in range(2)
)
EDGE = Y_SIZE


def chunk_of(ref, index):
    part, rows = CHUNKS[index]
    return ref.at[part, pl.ds(rows.start, rows.stop - rows.start), :]


def opening_kernel(
    own, rows_h, cols_h,
    halo, behind,
    rows, cols, offsets, via,
    ls, hs, hv, rs, rv, os, ov,
):
    me = Place()
    last = TILES - 1
    count = range(len(CHUNKS))
    loads = [
        pltpu.make_async_copy(rows_h, rows, ls.at[0]),
        pltpu.make_async_copy(cols_h, cols, ls.at[1]),
    ]
    for load in loads:
        load.start()
    for target in (me.tile_at(1), me.tile_at(-1), me.over_cut(), me.beside(1), me.beside(Y_SIZE - 1)):
        greet(target)

    @pl.when(me.space == 0)
    def _():
        behind[...] = jnp.zeros_like(behind)

    pl.semaphore_wait(pltpu.get_barrier_semaphore(), 5)

    def halo_copy(index):
        return remote(
            chunk_of(own, index), chunk_of(halo, index), hs.at[index], hv.at[index], me.tile_at(-1)
        )

    def cut_copy(index):
        return remote(
            chunk_of(own, index), chunk_of(via, index), hs.at[index], rv.at[index], me.over_cut()
        )

    def relay(index):
        return remote(
            chunk_of(via, index), chunk_of(halo, index), rs.at[index], hv.at[index],
            me.beside(Y_SIZE - 1),
        )

    @pl.when(me.space == EDGE)
    def _():
        for index in count:
            cut_copy(index).start()

    @pl.when(jnp.logical_and(me.space > 0, me.space != EDGE))
    def _():
        for index in count:
            halo_copy(index).start()

    for load in loads:
        load.wait()
    offsets[...] = jnp.zeros_like(offsets)
    offsets[0:1, 0 : rows.shape[1]] = rows[...]
    offsets[1:2, 0 : cols.shape[1]] = cols[...]
    offsets_on = remote(offsets, behind, os, ov, me.tile_at(1))

    @pl.when(me.space < last)
    def _():
        offsets_on.start()

    @pl.when(me.space == 0)
    def _():
        for index in count:
            cut_copy(index).wait_recv()
            relay(index).start()

    @pl.when(me.space > 0)
    def _():
        offsets_on.wait_recv()
        for index in count:
            halo_copy(index).wait_send()

    @pl.when(me.space < last)
    def _():
        offsets_on.wait_send()
        for index in count:
            halo_copy(index).wait_recv()

    @pl.when(me.space == 0)
    def _():
        for index in count:
            relay(index).wait_send()


def opening(own, rows, cols):
    f32, i32 = jnp.float32, jnp.int32
    dma = pltpu.SemaphoreType.DMA
    many = dma((len(CHUNKS),))
    return pl.pallas_call(
        opening_kernel,
        in_specs=[pl.BlockSpec(memory_space=pltpu.HBM)] * 3,
        out_specs=[
            pl.BlockSpec(memory_space=pltpu.HBM),
            pl.BlockSpec(memory_space=pltpu.VMEM),
        ],
        out_shape=[
            jax.ShapeDtypeStruct((2, BAND, SIDE), f32),
            jax.ShapeDtypeStruct((8, HALF), i32),
        ],
        scratch_shapes=[
            pltpu.VMEM(rows.shape, i32), pltpu.VMEM(cols.shape, i32), pltpu.VMEM((8, HALF), i32),
            pltpu.VMEM((2, BAND, SIDE), f32),
            dma((2,)), many, many, many, many, dma, dma,
        ],
        compiler_params=pltpu.CompilerParams(
            collective_id=0, has_side_effects=True, vmem_limit_bytes=VMEM_BYTES
        ),
        cost_estimate=pl.CostEstimate(flops=2**20, bytes_accessed=2**24, transcendentals=0),
        name="opening",
    )(own, rows, cols)


def tail_kernel(
    numer_own, numer_next, inverse, term, own_h, split_h, dual_h,
    updated, next_updated, out,
    own, split, dual, start_point, following, preceding, inc, via, r1, a1, r2, a2, r3, r4, a4, f2, f1, f0,
    ls, ns, nv, ps, pv, cs, cv, rs, rv, us, uv,
    s1, v1, s2, v2, s3, v3, s4, v4, s5, v5, s6, v6, s7, v7,
):
    me = Place()
    core, x, y, z = me.core, me.x, me.y, me.z
    last = TILES - 1

    loads = [
        pltpu.make_async_copy(src, dst, ls.at[i])
        for i, (src, dst) in enumerate(((own_h, own), (split_h, split), (dual_h, dual)))
    ]
    for load in loads:
        load.start()
    greet(me.core_peer())
    for k in range(1, X_SIZE):
        greet(me.x_peer(k))
    for k in range(1, Y_SIZE):
        greet(me.y_peer(k))
    for target in (me.bin_at(1), me.bin_at(-1), me.beside(1), me.beside(Y_SIZE - 1)):
        greet(target)

    def greet_z(k, carry):
        greet(me.z_peer(k))
        return carry

    lax.fori_loop(1, Z_SIZE, greet_z, 0)
    pl.semaphore_wait(
        pltpu.get_barrier_semaphore(), 1 + (X_SIZE - 1) + (Y_SIZE - 1) + 4 + (Z_SIZE - 1)
    )
    for load in loads:
        load.wait()
    start_point[...] = own[...] + split[...] - dual[...]
    to_preceding = remote(own, following, ns, nv, me.bin_at(-1))
    to_following = remote(start_point, preceding, ps, pv, me.bin_at(1))
    first_end = jnp.logical_and(z == 0, core == 0)
    last_end = jnp.logical_and(z == Z_SIZE - 1, core == CORES - 1)

    count = range(len(CHUNKS))

    def correction(index):
        return remote(
            chunk_of(numer_next, index), chunk_of(inc, index), cs.at[index], cv.at[index], me.y_peer(1)
        )

    def cut_copy(index):
        return remote(
            chunk_of(numer_next, index), chunk_of(via, index), cs.at[index], rv.at[index], me.over_cut()
        )

    def relay(index):
        return remote(
            chunk_of(via, index), chunk_of(inc, index), rs.at[index], cv.at[index], me.beside(1)
        )

    def relay_on(index):
        @pl.when(me.space == last)
        def _():
            cut_copy(index).wait_recv()
            relay(index).start()

    def updated_copy(index):
        return remote(
            chunk_of(updated, index), chunk_of(next_updated, index), us.at[index], uv.at[index],
            me.bin_at(-1),
        )

    @pl.when(jnp.logical_and(me.space < last, me.space != EDGE - 1))
    def _():
        for index in count:
            correction(index).start()

    part1 = GRAD_ROWS // CORES
    part2 = part1 // X_SIZE
    part3 = part2 // Z_SIZE

    def span(index, size):
        return pl.ds(pl.multiple_of(index * size, size), size)

    copy = remote(term.at[span(1 - core, part1)], r1, s1, v1, me.core_peer())
    copy.start()

    @pl.when(jnp.logical_not(first_end))
    def _():
        to_preceding.start()

    @pl.when(jnp.logical_not(last_end))
    def _():
        to_following.start()

    copy.wait()
    a1[...] = term[span(core, part1), :] + r1[...]

    copies = []
    for k in range(1, X_SIZE):
        target = lax.rem(x + k, X_SIZE)
        copies.append(
            remote(a1.at[span(target, part2)], r2.at[k - 1], s2.at[k - 1], v2.at[k - 1], me.x_peer(k))
        )
    for copy in copies:
        copy.start()
    for copy in copies:
        copy.wait()
    @pl.when(me.space == EDGE - 1)
    def _():
        for index in count:
            cut_copy(index).start()

    @pl.when(first_end)
    def _():
        to_preceding.start()

    @pl.when(last_end)
    def _():
        to_following.start()

    a2[...] = a1[span(x, part2), :] + r2[0] + r2[1] + r2[2]

    def z_sum(k):
        target = lax.rem(z + k, Z_SIZE)
        return remote(a2.at[span(target, part3)], r3.at[k - 1], s3.at[k - 1], v3.at[k - 1], me.z_peer(k))

    def start_z_sum(k, carry):
        z_sum(k).start()
        return carry

    def wait_z_sum(k, carry):
        z_sum(k).wait()
        return carry

    lax.fori_loop(1, Z_SIZE, start_z_sum, 0)
    lax.fori_loop(1, Z_SIZE, wait_z_sum, 0)
    relay_on(0)
    relay_on(1)
    total = a2[span(z, part3), :]
    for k in range(Z_SIZE - 1):
        total = total + r3[k]

    r4[y] = total
    copies = [
        remote(r4.at[y], r4.at[y], s4.at[k - 1], v4.at[k - 1], me.y_peer(k)) for k in range(1, Y_SIZE)
    ]
    for copy in copies:
        copy.start()
    relay_on(2)

    def send_updated(index, corrected):
        part, rows = CHUNKS[index]
        numer = numer_own[part, rows, :]
        if corrected:
            correction(index).wait_recv()
            numer = numer + inc[part, rows, :]
        here = own[part, rows, :]
        resid = following[part, rows, :] - start_point[part, rows, :]
        steady = here - tv_step * ((here - preceding[part, rows, :]) - resid)
        updated[part, rows, :] = steady + numer * inverse[rows, :]
        updated_copy(index).start()

    to_preceding.wait_recv()
    to_following.wait_recv()

    @pl.when(me.space == 0)
    def _():
        for index in count:
            send_updated(index, False)

    @pl.when(jnp.logical_and(me.space > 0, me.space != EDGE))
    def _():
        for index in count:
            send_updated(index, True)

    relay_on(3)
    for copy in copies:
        copy.wait()
    terms = PATCHES * lax.axis_size("phase") * lax.axis_size("space")
    a4[...] = ((r4[0] + r4[1]) + (r4[2] + r4[3])) * (1.0 / math.sqrt(terms))

    f2[span(z, part3), :] = a4[...]

    def z_spread(k):
        return remote(a4, f2.at[span(z, part3)], s5.at[k - 1], v5.at[k - 1], me.z_peer(k))

    def start_z_spread(k, carry):
        z_spread(k).start()
        return carry

    def wait_z_spread(k, carry):
        z_spread(k).wait()
        return carry

    lax.fori_loop(1, Z_SIZE, start_z_spread, 0)

    for index in range(4, len(CHUNKS)):
        relay_on(index)
    lax.fori_loop(1, Z_SIZE, wait_z_spread, 0)

    copies = [
        remote(f2, f1.at[span(x, part2)], s6.at[k - 1], v6.at[k - 1], me.x_peer(k))
        for k in range(1, X_SIZE)
    ]
    for copy in copies:
        copy.start()
    f1[span(x, part2), :] = f2[...]

    @pl.when(me.space == EDGE)
    def _():
        for index in count:
            send_updated(index, True)

    for copy in copies:
        copy.wait()

    copy = remote(f1, f0.at[span(core, part1)], s7, v7, me.core_peer())
    copy.start()
    f0[span(core, part1), :] = f1[...]
    copy.wait()
    for c in range(2):
        for side in range(2):
            begin = (2 * c + side) * SIDE
            out[c, :, side * HALF : (side + 1) * HALF] = f0[begin : begin + SIDE, :]

    for index in count:
        updated_copy(index).wait()
    to_preceding.wait_send()
    to_following.wait_send()

    @pl.when(me.space < last)
    def _():
        for index in count:
            correction(index).wait_send()

    @pl.when(me.space == last)
    def _():
        for index in count:
            relay(index).wait_send()


def tail(numer_own, numer_next, inverse, term, own, split, dual):
    part1 = GRAD_ROWS // CORES
    part2 = part1 // X_SIZE
    part3 = part2 // Z_SIZE
    f32 = jnp.float32
    dma = pltpu.SemaphoreType.DMA
    vmem = pl.BlockSpec(memory_space=pltpu.VMEM)
    hbm = pl.BlockSpec(memory_space=pltpu.HBM)
    room = pltpu.VMEM((2, BAND, SIDE), f32)
    many = dma((len(CHUNKS),))
    band = jax.ShapeDtypeStruct((2, BAND, SIDE), f32)
    sems = []
    for count in (1, X_SIZE - 1, Z_SIZE - 1, Y_SIZE - 1, Z_SIZE - 1, X_SIZE - 1, 1):
        sems += [dma if count == 1 else dma((count,))] * 2
    return pl.pallas_call(
        tail_kernel,
        in_specs=[vmem, hbm, vmem, vmem, hbm, hbm, hbm],
        out_specs=[vmem] * 3,
        out_shape=[band, band, jax.ShapeDtypeStruct((2, SIDE, SIDE), f32)],
        scratch_shapes=[
            room, room, room, room, room, room, room, room,
            pltpu.VMEM((part1, HALF), f32),
            pltpu.VMEM((part1, HALF), f32),
            pltpu.VMEM((X_SIZE - 1, part2, HALF), f32),
            pltpu.VMEM((part2, HALF), f32),
            pltpu.VMEM((Z_SIZE - 1, part3, HALF), f32),
            pltpu.VMEM((Y_SIZE, part3, HALF), f32),
            pltpu.VMEM((part3, HALF), f32),
            pltpu.VMEM((part2, HALF), f32),
            pltpu.VMEM((part1, HALF), f32),
            pltpu.VMEM((GRAD_ROWS, HALF), f32),
            dma((3,)), dma, dma, dma, dma, many, many, many, many, many, many,
            *sems,
        ],
        compiler_params=pltpu.CompilerParams(
            collective_id=1, has_side_effects=True, vmem_limit_bytes=VMEM_BYTES
        ),
        cost_estimate=pl.CostEstimate(flops=2**20, bytes_accessed=2**24, transcendentals=0),
        name="tail",
    )(numer_own, numer_next, inverse, term, own, split, dual)


def finish_kernel(updated, next_updated, dual, summed, out_object, out_split, out_dual, out_sum):
    out_object[...] = updated[...]
    out_sum[...] = summed[...]
    joint = [next_updated[c] - updated[c] + dual[c] for c in range(2)]
    size_abs = jnp.sqrt(joint[0] * joint[0] + joint[1] * joint[1])
    shrink = jnp.maximum(size_abs - shrink_level, 0.0) / jnp.maximum(size_abs, shrink_level)
    for c in range(2):
        new_split = joint[c] * shrink
        out_split[c] = new_split
        out_dual[c] = joint[c] - new_split


def finish(updated, next_updated, dual, summed):
    steps = 2
    f32 = jnp.float32
    band = pl.BlockSpec((2, BAND // steps, SIDE), lambda i: (0, i, 0))
    grad = pl.BlockSpec((2, SIDE // steps, SIDE), lambda i: (0, i, 0))
    band_shape = jax.ShapeDtypeStruct((2, BAND, SIDE), f32)
    return pl.pallas_call(
        finish_kernel,
        grid=(steps,),
        in_specs=[band, band, band, grad],
        out_specs=[band, band, band, grad],
        out_shape=[band_shape] * 3 + [jax.ShapeDtypeStruct((2, SIDE, SIDE), f32)],
        compiler_params=pltpu.CompilerParams(
            dimension_semantics=("arbitrary",), vmem_limit_bytes=VMEM_BYTES
        ),
        cost_estimate=pl.CostEstimate(flops=2**20, bytes_accessed=2**22, transcendentals=0),
        name="finish",
    )(updated, next_updated, dual, summed)


def shards(object_field, split_field, scaled_dual, probe, amplitudes, row_offsets, col_offsets):
    own = object_field[:, 0]
    split_own = split_field[:, 0]
    dual_own = scaled_dual[:, 0]
    halo, behind = opening(own, row_offsets, col_offsets)
    numer_own, numer_next, grad, inverse = patch_terms(
        row_offsets, col_offsets, behind, own, halo, probe, amplitudes
    )
    updated, next_updated, summed = tail(
        numer_own, numer_next, inverse, grad, own, split_own, dual_own
    )
    updated, new_split, new_dual, probe_gradient = finish(updated, next_updated, dual_own, summed)
    return (updated[:, None], new_split[:, None], new_dual[:, None], probe_gradient)


def solution(mesh):
    in_specs = (
        P(None, "phase", None, "space"),
        P(None, "phase", None, "space"),
        P(None, "phase", None, "space"),
        P(),
        P("phase", "space", None, None),
        P("phase", "space"),
        P("phase", "space"),
    )
    out_specs = (
        P(None, "phase", None, "space"),
        P(None, "phase", None, "space"),
        P(None, "phase", None, "space"),
        P(),
    )
    return jax.shard_map(shards, mesh=mesh, in_specs=in_specs, out_specs=out_specs, check_vma=False)
```

```python
import math

import jax
import jax.numpy as jnp
import ml_dtypes
import numpy as np
from jax import lax
from jax.experimental import pallas as pl
from jax.experimental.pallas import tpu as pltpu
from jax.sharding import PartitionSpec as P

amp_floor = 0.25
ridge = 1.0
tv_step = 0.25
shrink_level = 0.5

SIDE = 256
HALF = 128
BAND = 272
SPILL = BAND - SIDE
CORES, Z_SIZE, X_LO, Y_SIZE, X_SIZE = 2, 16, 2, 4, 4
GRAD_ROWS = 1024
TILES = X_SIZE // X_LO * Y_SIZE
PATCHES = 6
VMEM_BYTES = 58 * 1024 * 1024
GROUP = 2


def passed_along(value, axis, steps):
    count = lax.axis_size(axis)
    pairs = [(source, (source + steps) % count) for source in range(count)]
    return lax.ppermute(value, axis, pairs)


def two_parts(table):
    high = table.astype(ml_dtypes.bfloat16)
    low = (table - high.astype(np.float64)).astype(ml_dtypes.bfloat16)
    return np.stack([high, low])


def half_tables():
    place = np.arange(HALF)
    tables = []
    for odd in (0, 1):
        turns = ((2 * place[:, None] + odd) * place[None, :]) % SIDE
        angle = -2.0 * np.pi * turns / SIDE
        re = np.cos(angle) / math.sqrt(SIDE)
        im = np.sin(angle) / math.sqrt(SIDE)
        real_form = np.block([[re, -im], [im, re]])
        tables.append(two_parts(real_form))
        tables.append(two_parts(real_form.T))
    return tables


def put_split(ref, rows, lanes, value):
    high = value.astype(jnp.bfloat16)
    ref[0, rows, lanes] = high
    ref[1, rows, lanes] = (value - high.astype(jnp.float32)).astype(jnp.bfloat16)


def dot(a, b):
    return jnp.dot(a, b, preferred_element_type=jnp.float32)


def table_dot(table, data):
    high, low = table[0], table[1]
    return dot(
        jnp.concatenate([high, high, low], 1),
        jnp.concatenate([data[0], data[1], data[0]], 0),
    )


def dot_table(data, table):
    high, low = table[0], table[1]
    return dot(
        jnp.concatenate([data[0], data[1], data[0]], 1),
        jnp.concatenate([high, high, low], 0),
    )


def rolled_probe(source, target, left):
    step = 64
    for start in range(0, SIDE, step):
        turned = pltpu.roll(source[start : start + step, :], left, 1)
        for side in range(2):
            lanes = slice(side * HALF, (side + 1) * HALF)
            target[side, SPILL + start : SPILL + start + step, :] = turned[:, lanes]
            if start + step == SIDE:
                target[side, 0:SPILL, :] = turned[step - SPILL :, lanes]


def patch_kernel(
    rows_s, cols_s, behind, own, halo, probe, le_h, let_h, lo_h, lot_h, amp_h,
    numer_own, numer_next, grad, weight,
    power, sorter, le, let, lo, lot, amp, table_sems, amp_sems, *scratch,
):
    group = pl.program_id(0)
    groups = amp.shape[0] // GROUP
    tables = [
        pltpu.make_async_copy(src, dst, table_sems.at[i])
        for i, (src, dst) in enumerate(((le_h, le), (let_h, let), (lo_h, lo), (lot_h, lot)))
    ]

    def amp_load(index):
        rows = pl.ds(index * GROUP, GROUP)
        return pltpu.make_async_copy(amp_h.at[0, rows], amp.at[rows], amp_sems.at[index])

    first_slot = pl.program_id(0) * GROUP
    step = 16
    row_id = lax.broadcasted_iota(jnp.int32, (step, HALF), 0)
    lane_id = lax.broadcasted_iota(jnp.int32, (step, HALF), 1)
    re_half, im_half = slice(0, HALF), slice(HALF, SIDE)

    @pl.when(group == 0)
    def _():
        for load in tables:
            load.start()
        for index in range(groups):
            amp_load(index).start()
        numer_own[...] = jnp.zeros_like(numer_own)
        numer_next[...] = jnp.zeros_like(numer_next)
        grad[...] = jnp.zeros_like(grad)
        weight[...] = jnp.full_like(weight, ridge)
        power[...] = probe[0] * probe[0] + probe[1] * probe[1]
        place = lax.broadcasted_iota(jnp.int32, (SIDE, SIDE), 0)
        target = lax.broadcasted_iota(jnp.int32, (SIDE, SIDE), 1)
        source = jnp.where(target < HALF, 2 * target, 2 * (target - HALF) + 1)
        sorter[...] = jnp.where(place == source, 1.0, 0.0).astype(jnp.bfloat16)
        for load in tables:
            load.wait()

    amp_load(group).wait()

    def stages(member):
        brow, prow, pc, piece_s, wave_s, grow, xe, xo, ze, zo, amp_s, amp_c = scratch[
            member * 12 : member * 12 + 12
        ]
        slot = first_slot + member
        top, left = rows_s[0, slot], cols_s[0, slot]
        top_b, left_b = behind[0, slot], behind[1, slot]
        row_in = row_id >= top
        lane_in = [lane_id + side * HALF >= left for side in range(2)]
        lane_behind = [lane_id + side * HALF < left_b for side in range(2)]
        kept = {}

        def turn_probe():
            rolled_probe(probe.at[0], prow.at[0], left)
            rolled_probe(probe.at[1], prow.at[1], left)
            rolled_probe(power, brow, left_b)

        def sort_amplitudes():
            for side in range(2):
                amp_c[side] = amp[slot, :, side * HALF : (side + 1) * HALF]
            for odd in range(2):
                part = jnp.concatenate(
                    [amp_c[side, pl.ds(odd, HALF, stride=2), :] for side in range(2)], 1
                )
                high = part.astype(jnp.bfloat16)
                low = (part - high.astype(jnp.float32)).astype(jnp.bfloat16)
                amp_s[odd * HALF : (odd + 1) * HALF, :] = dot(high, sorter[...]) + dot(low, sorter[...])

        def wave_rows(start, side):
            rows = slice(start, start + step)
            lanes = slice(side * HALF, (side + 1) * HALF)
            p = [prow[c, side, pl.ds(SPILL - top + start, step), :] for c in range(2)]
            piece = []
            for c in range(2):
                here = own[c, rows, lanes]
                there = halo[c, rows, lanes]
                if start == 0:
                    here = jnp.where(row_in, here, own[c, SIDE:BAND, lanes])
                    there = jnp.where(row_in, there, halo[c, SIDE:BAND, lanes])
                piece.append(jnp.where(lane_in[side], here, there))
                piece_s[c, rows, lanes] = piece[c]
                pc[c, rows, lanes] = p[c]
            wave = [p[0] * piece[0] - p[1] * piece[1], p[0] * piece[1] + p[1] * piece[0]]
            for c in range(2):
                wave_s[c, rows, lanes] = wave[c]
            mine = jnp.where(lane_in[side], p[0] * p[0] + p[1] * p[1], 0.0)
            theirs = brow[side, pl.ds(SPILL - top_b + start, step), :]
            theirs = jnp.where(lane_behind[side], theirs, 0.0)
            if start == 0:
                mine_in = jnp.where(row_in, mine, 0.0)
                theirs_in = jnp.where(row_id >= top_b, theirs, 0.0)
                weight[SIDE:BAND, lanes] += (mine - mine_in) + (theirs - theirs_in)
                mine, theirs = mine_in, theirs_in
            weight[rows, lanes] += mine + theirs
            return wave

        def waves():
            for start in range(0, HALF, step):
                for side in range(2):
                    lanes = slice(side * HALF, (side + 1) * HALF)
                    upper = wave_rows(start, side)
                    lower = wave_rows(start + HALF, side)
                    for c in range(2):
                        rows = slice(c * HALF + start, c * HALF + start + step)
                        put_split(xe, rows, lanes, upper[c] + lower[c])
                        put_split(xo, rows, lanes, upper[c] - lower[c])

        def over_rows(odd):
            mid = table_dot((le, lo)[odd], (xe, xo)[odd])
            rows = slice(odd * HALF, (odd + 1) * HALF)
            for part in (re_half, im_half):
                first, second = mid[part, re_half], mid[part, im_half]
                put_split(ze, rows, part, first + second)
                put_split(zo, rows, part, first - second)

        def over_columns(odd):
            far = dot_table((ze, zo)[odd], (let, lot)[odd])
            far_re, far_im = far[:, re_half], far[:, im_half]
            square = far_re * far_re + far_im * far_im
            factor = amp_s[:, odd * HALF : (odd + 1) * HALF] * lax.rsqrt(
                jnp.maximum(square, amp_floor * amp_floor)
            )
            put_split((xe, xo)[odd], slice(0, SIDE), re_half, far_re * factor)
            put_split((xe, xo)[odd], slice(0, SIDE), im_half, far_im * factor)

        def back_columns():
            even = dot_table(xe, le)
            odds = dot_table(xo, lo)
            for c, part in enumerate((re_half, im_half)):
                first, second = even[:, part], odds[:, part]
                for side, value in enumerate((first + second, first - second)):
                    lanes = slice(side * HALF, (side + 1) * HALF)
                    rows = slice(c * HALF, (c + 1) * HALF)
                    put_split(ze, rows, lanes, value[:HALF])
                    put_split(zo, rows, lanes, value[HALF:])

        def back_rows():
            kept["even"] = table_dot(let, ze)
            kept["odds"] = table_dot(lot, zo)

        def changes():
            even, odds = kept["even"], kept["odds"]
            for start in range(0, HALF, step):
                for side in range(2):
                    lanes = slice(side * HALF, (side + 1) * HALF)
                    spans = [slice(c * HALF + start, c * HALF + start + step) for c in range(2)]
                    first = [even[spans[c], lanes] for c in range(2)]
                    second = [odds[spans[c], lanes] for c in range(2)]
                    for lower in range(2):
                        begin = start + lower * HALF
                        rows = slice(begin, begin + step)
                        change = []
                        for c in range(2):
                            back = first[c] - second[c] if lower else first[c] + second[c]
                            change.append(back - wave_s[c, rows, lanes])
                        p = [pc[c, rows, lanes] for c in range(2)]
                        piece = [piece_s[c, rows, lanes] for c in range(2)]
                        numer = [
                            p[0] * change[0] + p[1] * change[1],
                            p[0] * change[1] - p[1] * change[0],
                        ]
                        turned = [
                            piece[0] * change[0] + piece[1] * change[1],
                            piece[0] * change[1] - piece[1] * change[0],
                        ]
                        for c in range(2):
                            grow[c, side, rows, :] = turned[c]
                            here = jnp.where(lane_in[side], numer[c], 0.0)
                            there = numer[c] - here
                            if begin == 0:
                                grow[c, side, SIDE:BAND, :] = turned[c]
                                for total, value in ((numer_own, here), (numer_next, there)):
                                    inside = jnp.where(row_in, value, 0.0)
                                    total[c, rows, lanes] += inside
                                    total[c, SIDE:BAND, lanes] += value - inside
                            else:
                                numer_own[c, rows, lanes] += here
                                numer_next[c, rows, lanes] += there

        def gradient():
            back_left = lax.rem(SIDE - left, SIDE)
            tall = 64
            for c in range(2):
                for start in range(0, SIDE, tall):
                    pair = [grow[c, side, pl.ds(top + start, tall), :] for side in range(2)]
                    value = pltpu.roll(jnp.concatenate(pair, 1), back_left, 1)
                    for side in range(2):
                        begin = (2 * c + side) * SIDE + start
                        grad[begin : begin + tall, :] += value[:, side * HALF : (side + 1) * HALF]

        return [
            turn_probe,
            waves,
            lambda: (over_rows(0), sort_amplitudes(), over_rows(1)),
            lambda: (over_columns(0), over_columns(1)),
            back_columns,
            back_rows,
            changes,
            gradient,
        ]

    ahead, after = stages(0), stages(1)
    lag = 3
    for turn in range(len(ahead) + lag):
        if turn < len(ahead):
            ahead[turn]()
        if turn >= lag:
            after[turn - lag]()

    @pl.when(pl.program_id(0) == pl.num_programs(0) - 1)
    def _():
        weight[...] = 1.0 / weight[...]


def patch_terms(rows, cols, behind, own, halo, probe, amplitudes):
    count = amplitudes.shape[1]
    tables = half_tables()
    whole = lambda *shape: pl.BlockSpec(shape, lambda k: (0,) * len(shape))
    scalars = pl.BlockSpec(memory_space=pltpu.SMEM)
    band = whole(2, BAND, SIDE)
    f32, bf16 = jnp.float32, jnp.bfloat16
    split = pltpu.VMEM((2, SIDE, SIDE), bf16)
    square = pltpu.VMEM((2, SIDE, SIDE), f32)
    member = [
        pltpu.VMEM((2, BAND, HALF), f32),
        pltpu.VMEM((2, 2, BAND, HALF), f32),
        square, square, square,
        pltpu.VMEM((2, 2, BAND, HALF), f32),
        split, split, split, split,
        pltpu.VMEM((SIDE, SIDE), f32),
        pltpu.VMEM((2, SIDE, HALF), f32),
    ]
    return pl.pallas_call(
        patch_kernel,
        grid=(count // GROUP,),
        in_specs=[scalars, scalars, scalars, band, band, whole(2, SIDE, SIDE)]
        + [pl.BlockSpec(memory_space=pltpu.HBM)] * 5,
        out_specs=[band, band, whole(GRAD_ROWS, HALF), whole(BAND, SIDE)],
        out_shape=[
            jax.ShapeDtypeStruct((2, BAND, SIDE), f32),
            jax.ShapeDtypeStruct((2, BAND, SIDE), f32),
            jax.ShapeDtypeStruct((GRAD_ROWS, HALF), f32),
            jax.ShapeDtypeStruct((BAND, SIDE), f32),
        ],
        scratch_shapes=[pltpu.VMEM((SIDE, SIDE), f32), pltpu.VMEM((SIDE, SIDE), bf16)]
        + [split] * 4
        + [
            pltpu.VMEM((count, SIDE, SIDE), f32),
            pltpu.SemaphoreType.DMA((4,)),
            pltpu.SemaphoreType.DMA((count // GROUP,)),
        ]
        + member * GROUP,
        compiler_params=pltpu.CompilerParams(
            dimension_semantics=("arbitrary",), vmem_limit_bytes=VMEM_BYTES
        ),
        cost_estimate=pl.CostEstimate(
            flops=count * 26 * 2 * SIDE**3, bytes_accessed=6 * 2**20, transcendentals=0
        ),
        name="patch_terms",
    )(rows, cols, behind, own, halo, probe, *[jnp.asarray(t) for t in tables], amplitudes)


class Place:
    def __init__(self):
        self.phase, self.space = lax.axis_index("phase"), lax.axis_index("space")
        self.core = lax.rem(self.phase, CORES)
        self.z = lax.rem(self.phase // CORES, Z_SIZE)
        x_lo = self.phase // (CORES * Z_SIZE)
        self.y = lax.rem(self.space, Y_SIZE)
        self.x_hi = self.space // Y_SIZE
        self.x = self.x_hi * X_LO + x_lo

    def device(self, core, z, x, y):
        phase = (lax.rem(x, X_LO) * Z_SIZE + z) * CORES + core
        return (phase, (x // X_LO) * Y_SIZE + y)

    def core_peer(self):
        return self.device(1 - self.core, self.z, self.x, self.y)

    def x_peer(self, k):
        return self.device(self.core, self.z, lax.rem(self.x + k, X_SIZE), self.y)

    def y_peer(self, k):
        return self.device(self.core, self.z, self.x, lax.rem(self.y + k, Y_SIZE))

    def z_peer(self, k):
        return self.device(self.core, lax.rem(self.z + k, Z_SIZE), self.x, self.y)

    def y_mirror(self):
        return self.device(self.core, self.z, self.x, Y_SIZE - 1 - self.y)

    def bin_at(self, k):
        count = lax.axis_size("phase")
        return (lax.rem(self.phase + k + count, count), self.space)

    def tile_at(self, k):
        count = lax.axis_size("space")
        return (self.phase, lax.rem(self.space + k + count, count))


def remote(src, dst, s, v, target):
    return pltpu.make_async_remote_copy(
        src_ref=src, dst_ref=dst, send_sem=s, recv_sem=v,
        device_id=target, device_id_type=pl.DeviceIdType.MESH,
    )


def greet(target):
    pl.semaphore_signal(
        pltpu.get_barrier_semaphore(), inc=1, device_id=target, device_id_type=pl.DeviceIdType.MESH
    )


ROW_CUTS = (0, 72, 136, 208, 272)
CHUNKS = tuple(
    (part, slice(ROW_CUTS[i], ROW_CUTS[i + 1])) for i in range(len(ROW_CUTS) - 1) for part in range(2)
)
EDGE = Y_SIZE


def chunk_of(ref, index):
    part, rows = CHUNKS[index]
    return ref.at[part, pl.ds(rows.start, rows.stop - rows.start), :]


def by_ring(index):
    return CHUNKS[index][0] == 1


def opening_kernel(
    own, split_h, dual_h, rows_h, cols_h,
    halo, start_point, behind,
    here, split, dual, rows, cols, offsets,
    ls, hs, hv, rs, os, ov,
):
    me = Place()
    last = TILES - 1
    count = range(len(CHUNKS))
    loads = [
        pltpu.make_async_copy(src, dst, ls.at[i])
        for i, (src, dst) in enumerate(
            ((rows_h, rows), (cols_h, cols), (own, here), (split_h, split), (dual_h, dual))
        )
    ]
    for load in loads:
        load.start()
    for target in (me.tile_at(1), me.tile_at(-1), me.tile_at(TILES // 2), me.y_mirror()):
        greet(target)

    @pl.when(me.space == 0)
    def _():
        behind[...] = jnp.zeros_like(behind)

    pl.semaphore_wait(pltpu.get_barrier_semaphore(), 4)

    def halo_copy(index):
        target = me.y_peer(Y_SIZE - 1) if by_ring(index) else me.tile_at(-1)
        return remote(chunk_of(own, index), chunk_of(halo, index), hs.at[index], hv.at[index], target)

    def relay(index):
        place = chunk_of(halo, index)
        return remote(place, place, rs.at[index], hv.at[index], me.tile_at(TILES // 2))

    @pl.when(me.space > 0)
    def _():
        for index in count:
            halo_copy(index).start()

    loads[0].wait()
    loads[1].wait()
    offsets[...] = jnp.zeros_like(offsets)
    offsets[0:1, 0 : rows.shape[1]] = rows[...]
    offsets[1:2, 0 : cols.shape[1]] = cols[...]
    offsets_on = remote(offsets, behind, os, ov, me.tile_at(1))

    @pl.when(me.space < last)
    def _():
        offsets_on.start()

    for load in loads[2:]:
        load.wait()
    start_point[...] = here[...] + split[...] - dual[...]

    @pl.when(me.space == last)
    def _():
        for index in count:
            if by_ring(index):
                halo_copy(index).wait_recv()
                relay(index).start()

    @pl.when(me.space > 0)
    def _():
        offsets_on.wait_recv()
        for index in count:
            halo_copy(index).wait_send()

    @pl.when(me.space < last)
    def _():
        offsets_on.wait_send()
        for index in count:
            halo_copy(index).wait_recv()

    @pl.when(me.space == last)
    def _():
        for index in count:
            if by_ring(index):
                relay(index).wait_send()


def opening(own, split, dual, rows, cols):
    f32, i32 = jnp.float32, jnp.int32
    dma = pltpu.SemaphoreType.DMA
    room = pltpu.VMEM((2, BAND, SIDE), f32)
    many = dma((len(CHUNKS),))
    return pl.pallas_call(
        opening_kernel,
        in_specs=[pl.BlockSpec(memory_space=pltpu.HBM)] * 5,
        out_specs=[
            pl.BlockSpec(memory_space=pltpu.HBM),
            pl.BlockSpec(memory_space=pltpu.VMEM),
            pl.BlockSpec(memory_space=pltpu.VMEM),
        ],
        out_shape=[
            jax.ShapeDtypeStruct((2, BAND, SIDE), f32),
            jax.ShapeDtypeStruct((2, BAND, SIDE), f32),
            jax.ShapeDtypeStruct((8, HALF), i32),
        ],
        scratch_shapes=[
            room, room, room,
            pltpu.VMEM(rows.shape, i32), pltpu.VMEM(cols.shape, i32), pltpu.VMEM((8, HALF), i32),
            dma((5,)), many, many, many, dma, dma,
        ],
        compiler_params=pltpu.CompilerParams(
            collective_id=0, has_side_effects=True, vmem_limit_bytes=VMEM_BYTES
        ),
        cost_estimate=pl.CostEstimate(flops=2**20, bytes_accessed=2**24, transcendentals=0),
        name="opening",
    )(own, split, dual, rows, cols)


def tail_kernel(
    numer_own, numer_next, inverse, term, own_h, start_h, following_h, preceding_h,
    updated, next_updated, out,
    own, start_point, following, preceding, inc, r1, a1, r2, a2, r3, r4, a4, f2, f1, f0,
    ls, cs, cv, rs, us, uv,
    s1, v1, s2, v2, s3, v3, s4, v4, s5, v5, s6, v6, s7, v7,
):
    me = Place()
    core, x, y, z = me.core, me.x, me.y, me.z
    last = TILES - 1

    loads = [
        pltpu.make_async_copy(src, dst, ls.at[i])
        for i, (src, dst) in enumerate(
            (
                (own_h, own),
                (start_h, start_point),
                (following_h, following),
                (preceding_h, preceding),
            )
        )
    ]
    for load in loads:
        load.start()
    greet(me.core_peer())
    for k in range(1, X_SIZE):
        greet(me.x_peer(k))
    for k in range(1, Y_SIZE):
        greet(me.y_peer(k))
    for target in (me.bin_at(1), me.bin_at(-1), me.tile_at(1), me.tile_at(-1)):
        greet(target)

    def greet_z(k, carry):
        greet(me.z_peer(k))
        return carry

    lax.fori_loop(1, Z_SIZE, greet_z, 0)
    pl.semaphore_wait(
        pltpu.get_barrier_semaphore(), 1 + (X_SIZE - 1) + (Y_SIZE - 1) + 4 + (Z_SIZE - 1)
    )
    count = range(len(CHUNKS))

    def correction(index):
        target = me.y_peer(1) if by_ring(index) else me.tile_at(1)
        return remote(
            chunk_of(numer_next, index), chunk_of(inc, index), cs.at[index], cv.at[index], target
        )

    def relay(index):
        place = chunk_of(inc, index)
        return remote(place, place, rs.at[index], cv.at[index], me.tile_at(TILES // 2))

    def updated_copy(index):
        return remote(
            chunk_of(updated, index), chunk_of(next_updated, index), us.at[index], uv.at[index],
            me.bin_at(-1),
        )

    for index in count:
        early = last if by_ring(index) else EDGE - 1

        @pl.when(jnp.logical_or(me.space < early, jnp.logical_and(me.space > EDGE - 1, me.space < last)))
        def _():
            correction(index).start()

    part1 = GRAD_ROWS // CORES
    part2 = part1 // X_SIZE
    part3 = part2 // Z_SIZE

    def span(index, size):
        return pl.ds(pl.multiple_of(index * size, size), size)

    copy = remote(term.at[span(1 - core, part1)], r1, s1, v1, me.core_peer())
    copy.start()
    copy.wait()
    a1[...] = term[span(core, part1), :] + r1[...]

    copies = []
    for k in range(1, X_SIZE):
        target = lax.rem(x + k, X_SIZE)
        copies.append(
            remote(a1.at[span(target, part2)], r2.at[k - 1], s2.at[k - 1], v2.at[k - 1], me.x_peer(k))
        )
    for copy in copies:
        copy.start()
    for copy in copies:
        copy.wait()
    @pl.when(me.space == EDGE - 1)
    def _():
        for index in count:
            if not by_ring(index):
                correction(index).start()

    a2[...] = a1[span(x, part2), :] + r2[0] + r2[1] + r2[2]

    def z_sum(k):
        target = lax.rem(z + k, Z_SIZE)
        return remote(a2.at[span(target, part3)], r3.at[k - 1], s3.at[k - 1], v3.at[k - 1], me.z_peer(k))

    def start_z_sum(k, carry):
        z_sum(k).start()
        return carry

    def wait_z_sum(k, carry):
        z_sum(k).wait()
        return carry

    lax.fori_loop(1, Z_SIZE, start_z_sum, 0)

    @pl.when(me.space == 0)
    def _():
        for index in count:
            if by_ring(index):
                correction(index).wait_recv()
                relay(index).start()

    lax.fori_loop(1, Z_SIZE, wait_z_sum, 0)
    total = a2[span(z, part3), :]
    for k in range(Z_SIZE - 1):
        total = total + r3[k]

    r4[y] = total
    copies = [
        remote(r4.at[y], r4.at[y], s4.at[k - 1], v4.at[k - 1], me.y_peer(k)) for k in range(1, Y_SIZE)
    ]
    for copy in copies:
        copy.start()
    for copy in copies:
        copy.wait()
    terms = PATCHES * lax.axis_size("phase") * lax.axis_size("space")
    a4[...] = ((r4[0] + r4[1]) + (r4[2] + r4[3])) * (1.0 / math.sqrt(terms))

    f2[span(z, part3), :] = a4[...]

    def z_spread(k):
        return remote(a4, f2.at[span(z, part3)], s5.at[k - 1], v5.at[k - 1], me.z_peer(k))

    def start_z_spread(k, carry):
        z_spread(k).start()
        return carry

    def wait_z_spread(k, carry):
        z_spread(k).wait()
        return carry

    lax.fori_loop(1, Z_SIZE, start_z_spread, 0)
    lax.fori_loop(1, Z_SIZE, wait_z_spread, 0)

    copies = [
        remote(f2, f1.at[span(x, part2)], s6.at[k - 1], v6.at[k - 1], me.x_peer(k))
        for k in range(1, X_SIZE)
    ]
    for copy in copies:
        copy.start()
    f1[span(x, part2), :] = f2[...]

    def send_updated(index, corrected):
        part, rows = CHUNKS[index]
        numer = numer_own[part, rows, :]
        if corrected:
            correction(index).wait_recv()
            numer = numer + inc[part, rows, :]
        here = own[part, rows, :]
        resid = following[part, rows, :] - start_point[part, rows, :]
        steady = here - tv_step * ((here - preceding[part, rows, :]) - resid)
        updated[part, rows, :] = steady + numer * inverse[rows, :]
        updated_copy(index).start()

    for load in loads:
        load.wait()

    @pl.when(me.space == 0)
    def _():
        for index in count:
            send_updated(index, False)

    @pl.when(me.space > 0)
    def _():
        for index in count:
            send_updated(index, True)

    for copy in copies:
        copy.wait()

    copy = remote(f1, f0.at[span(core, part1)], s7, v7, me.core_peer())
    copy.start()
    f0[span(core, part1), :] = f1[...]
    copy.wait()
    for c in range(2):
        for side in range(2):
            begin = (2 * c + side) * SIDE
            out[c, :, side * HALF : (side + 1) * HALF] = f0[begin : begin + SIDE, :]

    for index in count:
        updated_copy(index).wait()

    @pl.when(me.space < last)
    def _():
        for index in count:
            correction(index).wait_send()

    @pl.when(me.space == 0)
    def _():
        for index in count:
            if by_ring(index):
                relay(index).wait_send()


def tail(numer_own, numer_next, inverse, term, own, start_point, following, preceding):
    part1 = GRAD_ROWS // CORES
    part2 = part1 // X_SIZE
    part3 = part2 // Z_SIZE
    f32 = jnp.float32
    dma = pltpu.SemaphoreType.DMA
    vmem = pl.BlockSpec(memory_space=pltpu.VMEM)
    hbm = pl.BlockSpec(memory_space=pltpu.HBM)
    place = pl.BlockSpec(memory_space=pl.ANY)
    room = pltpu.VMEM((2, BAND, SIDE), f32)
    many = dma((len(CHUNKS),))
    band = jax.ShapeDtypeStruct((2, BAND, SIDE), f32)
    sems = []
    for count in (1, X_SIZE - 1, Z_SIZE - 1, Y_SIZE - 1, Z_SIZE - 1, X_SIZE - 1, 1):
        sems += [dma if count == 1 else dma((count,))] * 2
    return pl.pallas_call(
        tail_kernel,
        in_specs=[vmem, hbm, vmem, vmem, place, place, place, place],
        out_specs=[vmem] * 3,
        out_shape=[band, band, jax.ShapeDtypeStruct((2, SIDE, SIDE), f32)],
        scratch_shapes=[
            room, room, room, room, room,
            pltpu.VMEM((part1, HALF), f32),
            pltpu.VMEM((part1, HALF), f32),
            pltpu.VMEM((X_SIZE - 1, part2, HALF), f32),
            pltpu.VMEM((part2, HALF), f32),
            pltpu.VMEM((Z_SIZE - 1, part3, HALF), f32),
            pltpu.VMEM((Y_SIZE, part3, HALF), f32),
            pltpu.VMEM((part3, HALF), f32),
            pltpu.VMEM((part2, HALF), f32),
            pltpu.VMEM((part1, HALF), f32),
            pltpu.VMEM((GRAD_ROWS, HALF), f32),
            dma((4,)), many, many, many, many, many,
            *sems,
        ],
        compiler_params=pltpu.CompilerParams(
            collective_id=1, has_side_effects=True, vmem_limit_bytes=VMEM_BYTES
        ),
        cost_estimate=pl.CostEstimate(flops=2**20, bytes_accessed=2**24, transcendentals=0),
        name="tail",
    )(numer_own, numer_next, inverse, term, own, start_point, following, preceding)


def finish_kernel(updated, next_updated, dual, summed, out_object, out_split, out_dual, out_sum):
    out_object[...] = updated[...]
    out_sum[...] = summed[...]
    joint = [next_updated[c] - updated[c] + dual[c] for c in range(2)]
    size_abs = jnp.sqrt(joint[0] * joint[0] + joint[1] * joint[1])
    shrink = jnp.maximum(size_abs - shrink_level, 0.0) / jnp.maximum(size_abs, shrink_level)
    for c in range(2):
        new_split = joint[c] * shrink
        out_split[c] = new_split
        out_dual[c] = joint[c] - new_split


def finish(updated, next_updated, dual, summed):
    steps = 2
    f32 = jnp.float32
    band = pl.BlockSpec((2, BAND // steps, SIDE), lambda i: (0, i, 0))
    grad = pl.BlockSpec((2, SIDE // steps, SIDE), lambda i: (0, i, 0))
    band_shape = jax.ShapeDtypeStruct((2, BAND, SIDE), f32)
    return pl.pallas_call(
        finish_kernel,
        grid=(steps,),
        in_specs=[band, band, band, grad],
        out_specs=[band, band, band, grad],
        out_shape=[band_shape] * 3 + [jax.ShapeDtypeStruct((2, SIDE, SIDE), f32)],
        compiler_params=pltpu.CompilerParams(
            dimension_semantics=("arbitrary",), vmem_limit_bytes=VMEM_BYTES
        ),
        cost_estimate=pl.CostEstimate(flops=2**20, bytes_accessed=2**22, transcendentals=0),
        name="finish",
    )(updated, next_updated, dual, summed)


def shards(object_field, split_field, scaled_dual, probe, amplitudes, row_offsets, col_offsets):
    own = object_field[:, 0]
    split_own = split_field[:, 0]
    dual_own = scaled_dual[:, 0]
    halo, start_point, behind = opening(own, split_own, dual_own, row_offsets, col_offsets)
    sent, halo = lax.optimization_barrier((own, halo))
    following = passed_along(sent, "phase", -1)
    preceding = passed_along(start_point, "phase", 1)
    numer_own, numer_next, grad, inverse = patch_terms(
        row_offsets, col_offsets, behind, own, halo, probe, amplitudes
    )
    updated, next_updated, summed = tail(
        numer_own, numer_next, inverse, grad, own, start_point, following, preceding
    )
    updated, new_split, new_dual, probe_gradient = finish(updated, next_updated, dual_own, summed)
    return (updated[:, None], new_split[:, None], new_dual[:, None], probe_gradient)


def solution(mesh):
    in_specs = (
        P(None, "phase", None, "space"),
        P(None, "phase", None, "space"),
        P(None, "phase", None, "space"),
        P(),
        P("phase", "space", None, None),
        P("phase", "space"),
        P("phase", "space"),
    )
    out_specs = (
        P(None, "phase", None, "space"),
        P(None, "phase", None, "space"),
        P(None, "phase", None, "space"),
        P(),
    )
    return jax.shard_map(shards, mesh=mesh, in_specs=in_specs, out_specs=out_specs, check_vma=False)
```

```python
import math

import jax
import jax.numpy as jnp
import ml_dtypes
import numpy as np
from jax import lax
from jax.experimental import pallas as pl
from jax.experimental.pallas import tpu as pltpu
from jax.sharding import PartitionSpec as P

amp_floor = 0.25
ridge = 1.0
tv_step = 0.25
shrink_level = 0.5

SIDE = 256
HALF = 128
BAND = 272
SPILL = BAND - SIDE
CORES, Z_SIZE, X_LO, Y_SIZE, X_SIZE = 2, 16, 2, 4, 4
NEAR = 4
GRAD_ROWS = 1024
TILES = X_SIZE // X_LO * Y_SIZE
PATCHES = 6
VMEM_BYTES = 58 * 1024 * 1024
GROUP = 2


def two_parts(table):
    high = table.astype(ml_dtypes.bfloat16)
    low = (table - high.astype(np.float64)).astype(ml_dtypes.bfloat16)
    return np.stack([high, low])


def half_tables():
    place = np.arange(HALF)
    tables = []
    for odd in (0, 1):
        turns = ((2 * place[:, None] + odd) * place[None, :]) % SIDE
        angle = -2.0 * np.pi * turns / SIDE
        re = np.cos(angle) / math.sqrt(SIDE)
        im = np.sin(angle) / math.sqrt(SIDE)
        real_form = np.block([[re, -im], [im, re]])
        tables.append(two_parts(real_form))
        tables.append(two_parts(real_form.T))
    return tables


def put_split(ref, rows, lanes, value):
    high = value.astype(jnp.bfloat16)
    ref[0, rows, lanes] = high
    ref[1, rows, lanes] = (value - high.astype(jnp.float32)).astype(jnp.bfloat16)


def dot(a, b):
    return jnp.dot(a, b, preferred_element_type=jnp.float32)


def table_dot(table, data):
    high, low = table[0], table[1]
    return dot(
        jnp.concatenate([high, high, low], 1),
        jnp.concatenate([data[0], data[1], data[0]], 0),
    )


def dot_table(data, table):
    high, low = table[0], table[1]
    return dot(
        jnp.concatenate([data[0], data[1], data[0]], 1),
        jnp.concatenate([high, high, low], 0),
    )


def rolled_probe(source, target, left):
    step = 64
    for start in range(0, SIDE, step):
        turned = pltpu.roll(source[start : start + step, :], left, 1)
        for side in range(2):
            lanes = slice(side * HALF, (side + 1) * HALF)
            target[side, SPILL + start : SPILL + start + step, :] = turned[:, lanes]
            if start + step == SIDE:
                target[side, 0:SPILL, :] = turned[step - SPILL :, lanes]


def patch_kernel(
    rows_s, cols_s, behind, own, halo, probe, le_h, let_h, lo_h, lot_h, amp_h,
    numer_own, numer_next, grad, weight,
    power, sorter, le, let, lo, lot, amp, table_sems, amp_sems, *scratch,
):
    group = pl.program_id(0)
    groups = amp.shape[0] // GROUP
    tables = [
        pltpu.make_async_copy(src, dst, table_sems.at[i])
        for i, (src, dst) in enumerate(((le_h, le), (let_h, let), (lo_h, lo), (lot_h, lot)))
    ]

    def amp_load(index):
        rows = pl.ds(index * GROUP, GROUP)
        return pltpu.make_async_copy(amp_h.at[0, rows], amp.at[rows], amp_sems.at[index])

    first_slot = pl.program_id(0) * GROUP
    step = 16
    row_id = lax.broadcasted_iota(jnp.int32, (step, HALF), 0)
    lane_id = lax.broadcasted_iota(jnp.int32, (step, HALF), 1)
    re_half, im_half = slice(0, HALF), slice(HALF, SIDE)

    @pl.when(group == 0)
    def _():
        for load in tables:
            load.start()
        for index in range(groups):
            amp_load(index).start()
        numer_own[...] = jnp.zeros_like(numer_own)
        numer_next[...] = jnp.zeros_like(numer_next)
        grad[...] = jnp.zeros_like(grad)
        weight[...] = jnp.full_like(weight, ridge)
        power[...] = probe[0] * probe[0] + probe[1] * probe[1]
        place = lax.broadcasted_iota(jnp.int32, (SIDE, SIDE), 0)
        target = lax.broadcasted_iota(jnp.int32, (SIDE, SIDE), 1)
        source = jnp.where(target < HALF, 2 * target, 2 * (target - HALF) + 1)
        sorter[...] = jnp.where(place == source, 1.0, 0.0).astype(jnp.bfloat16)
        for load in tables:
            load.wait()

    amp_load(group).wait()

    def stages(member):
        brow, prow, pc, piece_s, wave_s, grow, xe, xo, ze, zo, amp_s, amp_c = scratch[
            member * 12 : member * 12 + 12
        ]
        slot = first_slot + member
        top, left = rows_s[0, slot], cols_s[0, slot]
        top_b, left_b = behind[0, slot], behind[1, slot]
        row_in = row_id >= top
        lane_in = [lane_id + side * HALF >= left for side in range(2)]
        lane_behind = [lane_id + side * HALF < left_b for side in range(2)]
        kept = {}

        def turn_probe():
            rolled_probe(probe.at[0], prow.at[0], left)
            rolled_probe(probe.at[1], prow.at[1], left)
            rolled_probe(power, brow, left_b)

        def sort_amplitudes():
            for side in range(2):
                amp_c[side] = amp[slot, :, side * HALF : (side + 1) * HALF]
            for odd in range(2):
                part = jnp.concatenate(
                    [amp_c[side, pl.ds(odd, HALF, stride=2), :] for side in range(2)], 1
                )
                high = part.astype(jnp.bfloat16)
                low = (part - high.astype(jnp.float32)).astype(jnp.bfloat16)
                amp_s[odd * HALF : (odd + 1) * HALF, :] = dot(high, sorter[...]) + dot(low, sorter[...])

        def wave_rows(start, side):
            rows = slice(start, start + step)
            lanes = slice(side * HALF, (side + 1) * HALF)
            p = [prow[c, side, pl.ds(SPILL - top + start, step), :] for c in range(2)]
            piece = []
            for c in range(2):
                here = own[c, rows, lanes]
                there = halo[c, rows, lanes]
                if start == 0:
                    here = jnp.where(row_in, here, own[c, SIDE:BAND, lanes])
                    there = jnp.where(row_in, there, halo[c, SIDE:BAND, lanes])
                piece.append(jnp.where(lane_in[side], here, there))
                piece_s[c, rows, lanes] = piece[c]
                pc[c, rows, lanes] = p[c]
            wave = [p[0] * piece[0] - p[1] * piece[1], p[0] * piece[1] + p[1] * piece[0]]
            for c in range(2):
                wave_s[c, rows, lanes] = wave[c]
            mine = jnp.where(lane_in[side], p[0] * p[0] + p[1] * p[1], 0.0)
            theirs = brow[side, pl.ds(SPILL - top_b + start, step), :]
            theirs = jnp.where(lane_behind[side], theirs, 0.0)
            if start == 0:
                mine_in = jnp.where(row_in, mine, 0.0)
                theirs_in = jnp.where(row_id >= top_b, theirs, 0.0)
                weight[SIDE:BAND, lanes] += (mine - mine_in) + (theirs - theirs_in)
                mine, theirs = mine_in, theirs_in
            weight[rows, lanes] += mine + theirs
            return wave

        def waves():
            for start in range(0, HALF, step):
                for side in range(2):
                    lanes = slice(side * HALF, (side + 1) * HALF)
                    upper = wave_rows(start, side)
                    lower = wave_rows(start + HALF, side)
                    for c in range(2):
                        rows = slice(c * HALF + start, c * HALF + start + step)
                        put_split(xe, rows, lanes, upper[c] + lower[c])
                        put_split(xo, rows, lanes, upper[c] - lower[c])

        def over_rows(odd):
            mid = table_dot((le, lo)[odd], (xe, xo)[odd])
            rows = slice(odd * HALF, (odd + 1) * HALF)
            for part in (re_half, im_half):
                first, second = mid[part, re_half], mid[part, im_half]
                put_split(ze, rows, part, first + second)
                put_split(zo, rows, part, first - second)

        def over_columns(odd):
            far = dot_table((ze, zo)[odd], (let, lot)[odd])
            far_re, far_im = far[:, re_half], far[:, im_half]
            square = far_re * far_re + far_im * far_im
            factor = amp_s[:, odd * HALF : (odd + 1) * HALF] * lax.rsqrt(
                jnp.maximum(square, amp_floor * amp_floor)
            )
            put_split((xe, xo)[odd], slice(0, SIDE), re_half, far_re * factor)
            put_split((xe, xo)[odd], slice(0, SIDE), im_half, far_im * factor)

        def back_columns():
            even = dot_table(xe, le)
            odds = dot_table(xo, lo)
            for c, part in enumerate((re_half, im_half)):
                first, second = even[:, part], odds[:, part]
                for side, value in enumerate((first + second, first - second)):
                    lanes = slice(side * HALF, (side + 1) * HALF)
                    rows = slice(c * HALF, (c + 1) * HALF)
                    put_split(ze, rows, lanes, value[:HALF])
                    put_split(zo, rows, lanes, value[HALF:])

        def back_rows():
            kept["even"] = table_dot(let, ze)
            kept["odds"] = table_dot(lot, zo)

        def changes():
            even, odds = kept["even"], kept["odds"]
            for start in range(0, HALF, step):
                for side in range(2):
                    lanes = slice(side * HALF, (side + 1) * HALF)
                    spans = [slice(c * HALF + start, c * HALF + start + step) for c in range(2)]
                    first = [even[spans[c], lanes] for c in range(2)]
                    second = [odds[spans[c], lanes] for c in range(2)]
                    for lower in range(2):
                        begin = start + lower * HALF
                        rows = slice(begin, begin + step)
                        change = []
                        for c in range(2):
                            back = first[c] - second[c] if lower else first[c] + second[c]
                            change.append(back - wave_s[c, rows, lanes])
                        p = [pc[c, rows, lanes] for c in range(2)]
                        piece = [piece_s[c, rows, lanes] for c in range(2)]
                        numer = [
                            p[0] * change[0] + p[1] * change[1],
                            p[0] * change[1] - p[1] * change[0],
                        ]
                        turned = [
                            piece[0] * change[0] + piece[1] * change[1],
                            piece[0] * change[1] - piece[1] * change[0],
                        ]
                        for c in range(2):
                            grow[c, side, rows, :] = turned[c]
                            here = jnp.where(lane_in[side], numer[c], 0.0)
                            there = numer[c] - here
                            if begin == 0:
                                grow[c, side, SIDE:BAND, :] = turned[c]
                                for total, value in ((numer_own, here), (numer_next, there)):
                                    inside = jnp.where(row_in, value, 0.0)
                                    total[c, rows, lanes] += inside
                                    total[c, SIDE:BAND, lanes] += value - inside
                            else:
                                numer_own[c, rows, lanes] += here
                                numer_next[c, rows, lanes] += there

        def gradient():
            back_left = lax.rem(SIDE - left, SIDE)
            tall = 64
            for c in range(2):
                for start in range(0, SIDE, tall):
                    pair = [grow[c, side, pl.ds(top + start, tall), :] for side in range(2)]
                    value = pltpu.roll(jnp.concatenate(pair, 1), back_left, 1)
                    for side in range(2):
                        begin = (2 * c + side) * SIDE + start
                        grad[begin : begin + tall, :] += value[:, side * HALF : (side + 1) * HALF]

        return [
            turn_probe,
            waves,
            lambda: (over_rows(0), sort_amplitudes(), over_rows(1)),
            lambda: (over_columns(0), over_columns(1)),
            back_columns,
            back_rows,
            changes,
            gradient,
        ]

    ahead, after = stages(0), stages(1)
    lag = 3
    for turn in range(len(ahead) + lag):
        if turn < len(ahead):
            ahead[turn]()
        if turn >= lag:
            after[turn - lag]()

    @pl.when(pl.program_id(0) == pl.num_programs(0) - 1)
    def _():
        weight[...] = 1.0 / weight[...]


def patch_terms(rows, cols, behind, own, halo, probe, amplitudes):
    count = amplitudes.shape[1]
    tables = half_tables()
    whole = lambda *shape: pl.BlockSpec(shape, lambda k: (0,) * len(shape))
    scalars = pl.BlockSpec(memory_space=pltpu.SMEM)
    band = whole(2, BAND, SIDE)
    f32, bf16 = jnp.float32, jnp.bfloat16
    split = pltpu.VMEM((2, SIDE, SIDE), bf16)
    square = pltpu.VMEM((2, SIDE, SIDE), f32)
    member = [
        pltpu.VMEM((2, BAND, HALF), f32),
        pltpu.VMEM((2, 2, BAND, HALF), f32),
        square, square, square,
        pltpu.VMEM((2, 2, BAND, HALF), f32),
        split, split, split, split,
        pltpu.VMEM((SIDE, SIDE), f32),
        pltpu.VMEM((2, SIDE, HALF), f32),
    ]
    return pl.pallas_call(
        patch_kernel,
        grid=(count // GROUP,),
        in_specs=[scalars, scalars, scalars, band, band, whole(2, SIDE, SIDE)]
        + [pl.BlockSpec(memory_space=pltpu.HBM)] * 5,
        out_specs=[band, band, whole(GRAD_ROWS, HALF), whole(BAND, SIDE)],
        out_shape=[
            jax.ShapeDtypeStruct((2, BAND, SIDE), f32),
            jax.ShapeDtypeStruct((2, BAND, SIDE), f32),
            jax.ShapeDtypeStruct((GRAD_ROWS, HALF), f32),
            jax.ShapeDtypeStruct((BAND, SIDE), f32),
        ],
        scratch_shapes=[pltpu.VMEM((SIDE, SIDE), f32), pltpu.VMEM((SIDE, SIDE), bf16)]
        + [split] * 4
        + [
            pltpu.VMEM((count, SIDE, SIDE), f32),
            pltpu.SemaphoreType.DMA((4,)),
            pltpu.SemaphoreType.DMA((count // GROUP,)),
        ]
        + member * GROUP,
        compiler_params=pltpu.CompilerParams(
            dimension_semantics=("arbitrary",), vmem_limit_bytes=VMEM_BYTES
        ),
        cost_estimate=pl.CostEstimate(
            flops=count * 26 * 2 * SIDE**3, bytes_accessed=6 * 2**20, transcendentals=0
        ),
        name="patch_terms",
    )(rows, cols, behind, own, halo, probe, *[jnp.asarray(t) for t in tables], amplitudes)


class Place:
    def __init__(self):
        self.phase, self.space = lax.axis_index("phase"), lax.axis_index("space")
        self.core = lax.rem(self.phase, CORES)
        self.z = lax.rem(self.phase // CORES, Z_SIZE)
        x_lo = self.phase // (CORES * Z_SIZE)
        self.y = lax.rem(self.space, Y_SIZE)
        self.x_hi = self.space // Y_SIZE
        self.x = self.x_hi * X_LO + x_lo

    def device(self, core, z, x, y):
        phase = (lax.rem(x, X_LO) * Z_SIZE + z) * CORES + core
        return (phase, (x // X_LO) * Y_SIZE + y)

    def core_peer(self):
        return self.device(1 - self.core, self.z, self.x, self.y)

    def x_peer(self, k):
        return self.device(self.core, self.z, lax.rem(self.x + k, X_SIZE), self.y)

    def y_peer(self, k):
        return self.device(self.core, self.z, self.x, lax.rem(self.y + k, Y_SIZE))

    def y_mirror(self):
        return self.device(self.core, self.z, self.x, Y_SIZE - 1 - self.y)

    def near_peer(self, k):
        near = lax.rem(lax.rem(self.z, NEAR) + k, NEAR)
        return self.device(self.core, self.z // NEAR * NEAR + near, self.x, self.y)

    def far_peer(self, k):
        return self.device(self.core, lax.rem(self.z + k * NEAR, Z_SIZE), self.x, self.y)

    def bin_at(self, k):
        count = lax.axis_size("phase")
        return (lax.rem(self.phase + k + count, count), self.space)

    def tile_at(self, k):
        count = lax.axis_size("space")
        return (self.phase, lax.rem(self.space + k + count, count))


def remote(src, dst, s, v, target):
    return pltpu.make_async_remote_copy(
        src_ref=src, dst_ref=dst, send_sem=s, recv_sem=v,
        device_id=target, device_id_type=pl.DeviceIdType.MESH,
    )


def greet(target):
    pl.semaphore_signal(
        pltpu.get_barrier_semaphore(), inc=1, device_id=target, device_id_type=pl.DeviceIdType.MESH
    )


ROW_CUTS = (0, 136, 272)
CHUNKS = tuple(
    (part, slice(ROW_CUTS[i], ROW_CUTS[i + 1])) for i in range(len(ROW_CUTS) - 1) for part in range(2)
)
EDGE = Y_SIZE


def chunk_of(ref, index):
    part, rows = CHUNKS[index]
    return ref.at[part, pl.ds(rows.start, rows.stop - rows.start), :]


def by_ring(index):
    return CHUNKS[index][0] == 1


def opening_kernel(
    own, split_h, dual_h, rows_h, cols_h,
    halo, steady, behind,
    here, split, dual, start_point, following, preceding, rows, cols, offsets,
    ls, hs, hv, rs, ns, nv, ps, pv, os, ov,
):
    me = Place()
    last = TILES - 1
    count = range(len(CHUNKS))
    loads = [
        pltpu.make_async_copy(src, dst, ls.at[i])
        for i, (src, dst) in enumerate(
            ((rows_h, rows), (cols_h, cols), (own, here), (split_h, split), (dual_h, dual))
        )
    ]
    for load in loads:
        load.start()
    for target in (me.tile_at(1), me.tile_at(-1), me.tile_at(TILES // 2), me.y_mirror()):
        greet(target)
    for target in (me.bin_at(1), me.bin_at(-1)):
        greet(target)

    @pl.when(me.space == 0)
    def _():
        behind[...] = jnp.zeros_like(behind)

    pl.semaphore_wait(pltpu.get_barrier_semaphore(), 6)

    def halo_copy(index):
        target = me.y_peer(Y_SIZE - 1) if by_ring(index) else me.tile_at(-1)
        return remote(chunk_of(own, index), chunk_of(halo, index), hs.at[index], hv.at[index], target)

    def relay(index):
        place = chunk_of(halo, index)
        return remote(place, place, rs.at[index], hv.at[index], me.tile_at(TILES // 2))

    @pl.when(me.space > 0)
    def _():
        for index in count:
            halo_copy(index).start()

    to_preceding = remote(own, following, ns, nv, me.bin_at(-1))
    to_following = remote(start_point, preceding, ps, pv, me.bin_at(1))
    to_preceding.start()
    for load in loads:
        load.wait()
    start_point[...] = here[...] + split[...] - dual[...]
    to_following.start()
    offsets[...] = jnp.zeros_like(offsets)
    offsets[0:1, 0 : rows.shape[1]] = rows[...]
    offsets[1:2, 0 : cols.shape[1]] = cols[...]
    offsets_on = remote(offsets, behind, os, ov, me.tile_at(1))

    @pl.when(me.space < last)
    def _():
        offsets_on.start()

    @pl.when(me.space == last)
    def _():
        for index in count:
            if by_ring(index):
                halo_copy(index).wait_recv()
                relay(index).start()

    to_preceding.wait()
    to_following.wait()
    steady[...] = here[...] - tv_step * (
        (here[...] - preceding[...]) - (following[...] - start_point[...])
    )

    @pl.when(me.space > 0)
    def _():
        offsets_on.wait_recv()
        for index in count:
            halo_copy(index).wait_send()

    @pl.when(me.space < last)
    def _():
        offsets_on.wait_send()
        for index in count:
            halo_copy(index).wait_recv()

    @pl.when(me.space == last)
    def _():
        for index in count:
            if by_ring(index):
                relay(index).wait_send()


def opening(own, split, dual, rows, cols):
    f32, i32 = jnp.float32, jnp.int32
    dma = pltpu.SemaphoreType.DMA
    room = pltpu.VMEM((2, BAND, SIDE), f32)
    many = dma((len(CHUNKS),))
    return pl.pallas_call(
        opening_kernel,
        in_specs=[pl.BlockSpec(memory_space=pltpu.HBM)] * 5,
        out_specs=[
            pl.BlockSpec(memory_space=pltpu.HBM),
            pl.BlockSpec(memory_space=pltpu.VMEM),
            pl.BlockSpec(memory_space=pltpu.VMEM),
        ],
        out_shape=[
            jax.ShapeDtypeStruct((2, BAND, SIDE), f32),
            jax.ShapeDtypeStruct((2, BAND, SIDE), f32),
            jax.ShapeDtypeStruct((8, HALF), i32),
        ],
        scratch_shapes=[
            room, room, room, room, room, room,
            pltpu.VMEM(rows.shape, i32), pltpu.VMEM(cols.shape, i32), pltpu.VMEM((8, HALF), i32),
            dma((5,)), many, many, many, dma, dma, dma, dma, dma, dma,
        ],
        compiler_params=pltpu.CompilerParams(
            collective_id=0, has_side_effects=True, vmem_limit_bytes=VMEM_BYTES
        ),
        cost_estimate=pl.CostEstimate(flops=2**20, bytes_accessed=2**24, transcendentals=0),
        name="opening",
    )(own, split, dual, rows, cols)


def tail_kernel(
    numer_own, numer_next, inverse, term, steady_h,
    updated, next_updated, out,
    steady, inc, r1, a1, r2, a2, r3, a3, r4, r5, a5, f3, f2, f1, f0,
    ls, cs, cv, rs, us, uv,
    s1, v1, s2, v2, s3, v3, s4, v4, s5, v5, s6, v6, s7, v7, s8, v8, s9, v9,
):
    me = Place()
    core, x, y, z = me.core, me.x, me.y, me.z
    last = TILES - 1

    load = pltpu.make_async_copy(steady_h, steady, ls)
    load.start()
    peers = [me.core_peer(), me.bin_at(1), me.bin_at(-1), me.tile_at(1), me.tile_at(-1)]
    peers += [me.x_peer(k) for k in range(1, X_SIZE)]
    peers += [me.y_peer(k) for k in range(1, Y_SIZE)]
    peers += [me.near_peer(k) for k in range(1, NEAR)] + [me.far_peer(k) for k in range(1, NEAR)]
    for target in peers:
        greet(target)
    pl.semaphore_wait(pltpu.get_barrier_semaphore(), len(peers))
    count = range(len(CHUNKS))

    def correction(index):
        target = me.y_peer(1) if by_ring(index) else me.tile_at(1)
        return remote(
            chunk_of(numer_next, index), chunk_of(inc, index), cs.at[index], cv.at[index], target
        )

    def relay(index):
        place = chunk_of(inc, index)
        return remote(place, place, rs.at[index], cv.at[index], me.tile_at(TILES // 2))

    def updated_copy(index):
        return remote(
            chunk_of(updated, index), chunk_of(next_updated, index), us.at[index], uv.at[index],
            me.bin_at(-1),
        )

    for index in count:
        early = last if by_ring(index) else EDGE - 1

        @pl.when(jnp.logical_or(me.space < early, jnp.logical_and(me.space > EDGE - 1, me.space < last)))
        def _():
            correction(index).start()

    part1 = GRAD_ROWS // CORES
    part2 = part1 // X_SIZE
    part3 = part2 // NEAR
    part4 = part3 // NEAR

    def span(index, size):
        return pl.ds(pl.multiple_of(index * size, size), size)

    copy = remote(term.at[span(1 - core, part1)], r1, s1, v1, me.core_peer())
    copy.start()
    copy.wait()
    a1[...] = term[span(core, part1), :] + r1[...]

    copies = []
    for k in range(1, X_SIZE):
        target = lax.rem(x + k, X_SIZE)
        copies.append(
            remote(a1.at[span(target, part2)], r2.at[k - 1], s2.at[k - 1], v2.at[k - 1], me.x_peer(k))
        )
    for copy in copies:
        copy.start()
    for copy in copies:
        copy.wait()
    @pl.when(me.space == EDGE - 1)
    def _():
        for index in count:
            if not by_ring(index):
                correction(index).start()

    a2[...] = a1[span(x, part2), :] + r2[0] + r2[1] + r2[2]

    near, far = lax.rem(z, NEAR), z // NEAR
    copies = []
    for k in range(1, NEAR):
        target = lax.rem(near + k, NEAR)
        copies.append(
            remote(a2.at[span(target, part3)], r3.at[k - 1], s3.at[k - 1], v3.at[k - 1], me.near_peer(k))
        )
    for copy in copies:
        copy.start()

    @pl.when(me.space == 0)
    def _():
        for index in count:
            if by_ring(index):
                correction(index).wait_recv()
                relay(index).start()

    for copy in copies:
        copy.wait()
    a3[...] = a2[span(near, part3), :] + r3[0] + r3[1] + r3[2]

    copies = []
    for k in range(1, NEAR):
        target = lax.rem(far + k, NEAR)
        copies.append(
            remote(a3.at[span(target, part4)], r4.at[k - 1], s4.at[k - 1], v4.at[k - 1], me.far_peer(k))
        )
    for copy in copies:
        copy.start()
    for copy in copies:
        copy.wait()

    r5[y] = a3[span(far, part4), :] + r4[0] + r4[1] + r4[2]
    copies = [
        remote(r5.at[y], r5.at[y], s5.at[k - 1], v5.at[k - 1], me.y_peer(k)) for k in range(1, Y_SIZE)
    ]
    for copy in copies:
        copy.start()
    for copy in copies:
        copy.wait()
    terms = PATCHES * lax.axis_size("phase") * lax.axis_size("space")
    a5[...] = ((r5[0] + r5[1]) + (r5[2] + r5[3])) * (1.0 / math.sqrt(terms))

    copies = [
        remote(a5, f3.at[span(far, part4)], s6.at[k - 1], v6.at[k - 1], me.far_peer(k))
        for k in range(1, NEAR)
    ]
    for copy in copies:
        copy.start()
    f3[span(far, part4), :] = a5[...]
    for copy in copies:
        copy.wait()

    copies = [
        remote(f3, f2.at[span(near, part3)], s7.at[k - 1], v7.at[k - 1], me.near_peer(k))
        for k in range(1, NEAR)
    ]
    for copy in copies:
        copy.start()
    f2[span(near, part3), :] = f3[...]
    for copy in copies:
        copy.wait()

    copies = [
        remote(f2, f1.at[span(x, part2)], s8.at[k - 1], v8.at[k - 1], me.x_peer(k))
        for k in range(1, X_SIZE)
    ]
    for copy in copies:
        copy.start()
    f1[span(x, part2), :] = f2[...]

    def send_updated(index, corrected):
        part, rows = CHUNKS[index]
        numer = numer_own[part, rows, :]
        if corrected:
            correction(index).wait_recv()
            numer = numer + inc[part, rows, :]
        updated[part, rows, :] = steady[part, rows, :] + numer * inverse[rows, :]
        updated_copy(index).start()

    load.wait()

    @pl.when(me.space == 0)
    def _():
        for index in count:
            send_updated(index, False)

    @pl.when(me.space > 0)
    def _():
        for index in count:
            send_updated(index, True)

    for copy in copies:
        copy.wait()

    copy = remote(f1, f0.at[span(core, part1)], s9, v9, me.core_peer())
    copy.start()
    f0[span(core, part1), :] = f1[...]
    copy.wait()
    for c in range(2):
        for side in range(2):
            begin = (2 * c + side) * SIDE
            out[c, :, side * HALF : (side + 1) * HALF] = f0[begin : begin + SIDE, :]

    for index in count:
        updated_copy(index).wait()

    @pl.when(me.space < last)
    def _():
        for index in count:
            correction(index).wait_send()

    @pl.when(me.space == 0)
    def _():
        for index in count:
            if by_ring(index):
                relay(index).wait_send()


def tail(numer_own, numer_next, inverse, term, steady):
    part1 = GRAD_ROWS // CORES
    part2 = part1 // X_SIZE
    part3 = part2 // NEAR
    part4 = part3 // NEAR
    f32 = jnp.float32
    dma = pltpu.SemaphoreType.DMA
    vmem = pl.BlockSpec(memory_space=pltpu.VMEM)
    hbm = pl.BlockSpec(memory_space=pltpu.HBM)
    room = pltpu.VMEM((2, BAND, SIDE), f32)
    many = dma((len(CHUNKS),))
    band = jax.ShapeDtypeStruct((2, BAND, SIDE), f32)
    sems = []
    steps = (1, X_SIZE - 1, NEAR - 1, NEAR - 1, Y_SIZE - 1, NEAR - 1, NEAR - 1, X_SIZE - 1, 1)
    for count in steps:
        sems += [dma if count == 1 else dma((count,))] * 2
    return pl.pallas_call(
        tail_kernel,
        in_specs=[vmem, hbm, vmem, vmem, hbm],
        out_specs=[vmem] * 3,
        out_shape=[band, band, jax.ShapeDtypeStruct((2, SIDE, SIDE), f32)],
        scratch_shapes=[
            room, room,
            pltpu.VMEM((part1, HALF), f32),
            pltpu.VMEM((part1, HALF), f32),
            pltpu.VMEM((X_SIZE - 1, part2, HALF), f32),
            pltpu.VMEM((part2, HALF), f32),
            pltpu.VMEM((NEAR - 1, part3, HALF), f32),
            pltpu.VMEM((part3, HALF), f32),
            pltpu.VMEM((NEAR - 1, part4, HALF), f32),
            pltpu.VMEM((Y_SIZE, part4, HALF), f32),
            pltpu.VMEM((part4, HALF), f32),
            pltpu.VMEM((part3, HALF), f32),
            pltpu.VMEM((part2, HALF), f32),
            pltpu.VMEM((part1, HALF), f32),
            pltpu.VMEM((GRAD_ROWS, HALF), f32),
            dma, many, many, many, many, many,
            *sems,
        ],
        compiler_params=pltpu.CompilerParams(
            collective_id=1, has_side_effects=True, vmem_limit_bytes=VMEM_BYTES
        ),
        cost_estimate=pl.CostEstimate(flops=2**20, bytes_accessed=2**24, transcendentals=0),
        name="tail",
    )(numer_own, numer_next, inverse, term, steady)


def finish_kernel(updated, next_updated, dual, summed, out_object, out_split, out_dual, out_sum):
    out_object[...] = updated[...]
    out_sum[...] = summed[...]
    joint = [next_updated[c] - updated[c] + dual[c] for c in range(2)]
    size_abs = jnp.sqrt(joint[0] * joint[0] + joint[1] * joint[1])
    shrink = jnp.maximum(size_abs - shrink_level, 0.0) / jnp.maximum(size_abs, shrink_level)
    for c in range(2):
        new_split = joint[c] * shrink
        out_split[c] = new_split
        out_dual[c] = joint[c] - new_split


def finish(updated, next_updated, dual, summed):
    steps = 2
    f32 = jnp.float32
    band = pl.BlockSpec((2, BAND // steps, SIDE), lambda i: (0, i, 0))
    grad = pl.BlockSpec((2, SIDE // steps, SIDE), lambda i: (0, i, 0))
    band_shape = jax.ShapeDtypeStruct((2, BAND, SIDE), f32)
    return pl.pallas_call(
        finish_kernel,
        grid=(steps,),
        in_specs=[band, band, band, grad],
        out_specs=[band, band, band, grad],
        out_shape=[band_shape] * 3 + [jax.ShapeDtypeStruct((2, SIDE, SIDE), f32)],
        compiler_params=pltpu.CompilerParams(
            dimension_semantics=("arbitrary",), vmem_limit_bytes=VMEM_BYTES
        ),
        cost_estimate=pl.CostEstimate(flops=2**20, bytes_accessed=2**22, transcendentals=0),
        name="finish",
    )(updated, next_updated, dual, summed)


def shards(object_field, split_field, scaled_dual, probe, amplitudes, row_offsets, col_offsets):
    own = object_field[:, 0]
    split_own = split_field[:, 0]
    dual_own = scaled_dual[:, 0]
    halo, steady, behind = opening(own, split_own, dual_own, row_offsets, col_offsets)
    numer_own, numer_next, grad, inverse = patch_terms(
        row_offsets, col_offsets, behind, own, halo, probe, amplitudes
    )
    updated, next_updated, summed = tail(numer_own, numer_next, inverse, grad, steady)
    updated, new_split, new_dual, probe_gradient = finish(updated, next_updated, dual_own, summed)
    return (updated[:, None], new_split[:, None], new_dual[:, None], probe_gradient)


def solution(mesh):
    in_specs = (
        P(None, "phase", None, "space"),
        P(None, "phase", None, "space"),
        P(None, "phase", None, "space"),
        P(),
        P("phase", "space", None, None),
        P("phase", "space"),
        P("phase", "space"),
    )
    out_specs = (
        P(None, "phase", None, "space"),
        P(None, "phase", None, "space"),
        P(None, "phase", None, "space"),
        P(),
    )
    return jax.shard_map(shards, mesh=mesh, in_specs=in_specs, out_specs=out_specs, check_vma=False)
```

```python
import math

import jax
import jax.numpy as jnp
import ml_dtypes
import numpy as np
from jax import lax
from jax.experimental import pallas as pl
from jax.experimental.pallas import tpu as pltpu
from jax.sharding import PartitionSpec as P

amp_floor = 0.25
ridge = 1.0
tv_step = 0.25
shrink_level = 0.5

SIDE = 256
HALF = 128
BAND = 272
SPILL = BAND - SIDE
CORES, Z_SIZE, X_LO, Y_SIZE, X_SIZE = 2, 16, 2, 4, 4
GRAD_ROWS = 1024
TILES = X_SIZE // X_LO * Y_SIZE
PATCHES = 6
VMEM_BYTES = 58 * 1024 * 1024
SETS = 3
LAG = 3


def two_parts(table):
    high = table.astype(ml_dtypes.bfloat16)
    low = (table - high.astype(np.float64)).astype(ml_dtypes.bfloat16)
    return np.stack([high, low])


def half_tables():
    place = np.arange(HALF)
    tables = []
    for odd in (0, 1):
        turns = ((2 * place[:, None] + odd) * place[None, :]) % SIDE
        angle = -2.0 * np.pi * turns / SIDE
        re = np.cos(angle) / math.sqrt(SIDE)
        im = np.sin(angle) / math.sqrt(SIDE)
        real_form = np.block([[re, -im], [im, re]])
        tables.append(two_parts(real_form))
        tables.append(two_parts(real_form.T))
    return tables


def put_split(ref, rows, lanes, value):
    high = value.astype(jnp.bfloat16)
    ref[0, rows, lanes] = high
    ref[1, rows, lanes] = (value - high.astype(jnp.float32)).astype(jnp.bfloat16)


def dot(a, b):
    return jnp.dot(a, b, preferred_element_type=jnp.float32)


def table_dot(table, data):
    high, low = table[0], table[1]
    return dot(
        jnp.concatenate([high, high, low], 1),
        jnp.concatenate([data[0], data[1], data[0]], 0),
    )


def dot_table(data, table):
    high, low = table[0], table[1]
    return dot(
        jnp.concatenate([data[0], data[1], data[0]], 1),
        jnp.concatenate([high, high, low], 0),
    )


def rolled_probe(source, target, left):
    step = 64
    for start in range(0, SIDE, step):
        turned = pltpu.roll(source[start : start + step, :], left, 1)
        for side in range(2):
            lanes = slice(side * HALF, (side + 1) * HALF)
            target[side, SPILL + start : SPILL + start + step, :] = turned[:, lanes]
            if start + step == SIDE:
                target[side, 0:SPILL, :] = turned[step - SPILL :, lanes]


def patch_kernel(
    rows_s, cols_s, behind, own, halo, probe, le_h, let_h, lo_h, lot_h, amp_h,
    numer_own, numer_next, grad, weight,
    power, sorter, le, let, lo, lot, amp, table_sems, amp_sems, *scratch,
):
    loads = [
        pltpu.make_async_copy(src, dst, table_sems.at[i])
        for i, (src, dst) in enumerate(((le_h, le), (let_h, let), (lo_h, lo), (lot_h, lot)))
    ]
    count = amp.shape[0]
    amp_loads = [
        pltpu.make_async_copy(amp_h.at[0, slot], amp.at[slot], amp_sems.at[slot])
        for slot in range(count)
    ]
    for load in loads + amp_loads:
        load.start()
    step = 16
    row_id = lax.broadcasted_iota(jnp.int32, (step, HALF), 0)
    lane_id = lax.broadcasted_iota(jnp.int32, (step, HALF), 1)
    re_half, im_half = slice(0, HALF), slice(HALF, SIDE)

    numer_own[...] = jnp.zeros_like(numer_own)
    numer_next[...] = jnp.zeros_like(numer_next)
    grad[...] = jnp.zeros_like(grad)
    weight[...] = jnp.full_like(weight, ridge)
    power[...] = probe[0] * probe[0] + probe[1] * probe[1]
    place = lax.broadcasted_iota(jnp.int32, (SIDE, SIDE), 0)
    target = lax.broadcasted_iota(jnp.int32, (SIDE, SIDE), 1)
    source = jnp.where(target < HALF, 2 * target, 2 * (target - HALF) + 1)
    sorter[...] = jnp.where(place == source, 1.0, 0.0).astype(jnp.bfloat16)

    def stages(slot):
        brow, prow, pc, piece_s, wave_s, grow, xe, xo, ze, zo, amp_s, amp_c = scratch[
            slot % SETS * 12 : slot % SETS * 12 + 12
        ]
        top, left = rows_s[0, slot], cols_s[0, slot]
        top_b, left_b = behind[0, slot], behind[1, slot]
        row_in = row_id >= top
        lane_in = [lane_id + side * HALF >= left for side in range(2)]
        lane_behind = [lane_id + side * HALF < left_b for side in range(2)]
        kept = {}

        def turn_probe():
            rolled_probe(probe.at[0], prow.at[0], left)
            rolled_probe(probe.at[1], prow.at[1], left)
            rolled_probe(power, brow, left_b)

        def sort_amplitudes():
            if slot == 0:
                for load in loads:
                    load.wait()
            amp_loads[slot].wait()
            for side in range(2):
                amp_c[side] = amp[slot, :, side * HALF : (side + 1) * HALF]
            for odd in range(2):
                part = jnp.concatenate(
                    [amp_c[side, pl.ds(odd, HALF, stride=2), :] for side in range(2)], 1
                )
                high = part.astype(jnp.bfloat16)
                low = (part - high.astype(jnp.float32)).astype(jnp.bfloat16)
                amp_s[odd * HALF : (odd + 1) * HALF, :] = dot(high, sorter[...]) + dot(low, sorter[...])

        def wave_rows(start, side):
            rows = slice(start, start + step)
            lanes = slice(side * HALF, (side + 1) * HALF)
            p = [prow[c, side, pl.ds(SPILL - top + start, step), :] for c in range(2)]
            piece = []
            for c in range(2):
                here = own[c, rows, lanes]
                there = halo[c, rows, lanes]
                if start == 0:
                    here = jnp.where(row_in, here, own[c, SIDE:BAND, lanes])
                    there = jnp.where(row_in, there, halo[c, SIDE:BAND, lanes])
                piece.append(jnp.where(lane_in[side], here, there))
                piece_s[c, rows, lanes] = piece[c]
                pc[c, rows, lanes] = p[c]
            wave = [p[0] * piece[0] - p[1] * piece[1], p[0] * piece[1] + p[1] * piece[0]]
            for c in range(2):
                wave_s[c, rows, lanes] = wave[c]
            mine = jnp.where(lane_in[side], p[0] * p[0] + p[1] * p[1], 0.0)
            theirs = brow[side, pl.ds(SPILL - top_b + start, step), :]
            theirs = jnp.where(lane_behind[side], theirs, 0.0)
            if start == 0:
                mine_in = jnp.where(row_in, mine, 0.0)
                theirs_in = jnp.where(row_id >= top_b, theirs, 0.0)
                weight[SIDE:BAND, lanes] += (mine - mine_in) + (theirs - theirs_in)
                mine, theirs = mine_in, theirs_in
            weight[rows, lanes] += mine + theirs
            return wave

        def waves():
            for start in range(0, HALF, step):
                for side in range(2):
                    lanes = slice(side * HALF, (side + 1) * HALF)
                    upper = wave_rows(start, side)
                    lower = wave_rows(start + HALF, side)
                    for c in range(2):
                        rows = slice(c * HALF + start, c * HALF + start + step)
                        put_split(xe, rows, lanes, upper[c] + lower[c])
                        put_split(xo, rows, lanes, upper[c] - lower[c])

        def over_rows(odd):
            mid = table_dot((le, lo)[odd], (xe, xo)[odd])
            rows = slice(odd * HALF, (odd + 1) * HALF)
            for part in (re_half, im_half):
                first, second = mid[part, re_half], mid[part, im_half]
                put_split(ze, rows, part, first + second)
                put_split(zo, rows, part, first - second)

        def over_columns(odd):
            far = dot_table((ze, zo)[odd], (let, lot)[odd])
            far_re, far_im = far[:, re_half], far[:, im_half]
            square = far_re * far_re + far_im * far_im
            factor = amp_s[:, odd * HALF : (odd + 1) * HALF] * lax.rsqrt(
                jnp.maximum(square, amp_floor * amp_floor)
            )
            put_split((xe, xo)[odd], slice(0, SIDE), re_half, far_re * factor)
            put_split((xe, xo)[odd], slice(0, SIDE), im_half, far_im * factor)

        def back_columns():
            even = dot_table(xe, le)
            odds = dot_table(xo, lo)
            for c, part in enumerate((re_half, im_half)):
                first, second = even[:, part], odds[:, part]
                for side, value in enumerate((first + second, first - second)):
                    lanes = slice(side * HALF, (side + 1) * HALF)
                    rows = slice(c * HALF, (c + 1) * HALF)
                    put_split(ze, rows, lanes, value[:HALF])
                    put_split(zo, rows, lanes, value[HALF:])

        def back_rows():
            kept["even"] = table_dot(let, ze)
            kept["odds"] = table_dot(lot, zo)

        def changes():
            even, odds = kept["even"], kept["odds"]
            for start in range(0, HALF, step):
                for side in range(2):
                    lanes = slice(side * HALF, (side + 1) * HALF)
                    spans = [slice(c * HALF + start, c * HALF + start + step) for c in range(2)]
                    first = [even[spans[c], lanes] for c in range(2)]
                    second = [odds[spans[c], lanes] for c in range(2)]
                    for lower in range(2):
                        begin = start + lower * HALF
                        rows = slice(begin, begin + step)
                        change = []
                        for c in range(2):
                            back = first[c] - second[c] if lower else first[c] + second[c]
                            change.append(back - wave_s[c, rows, lanes])
                        p = [pc[c, rows, lanes] for c in range(2)]
                        piece = [piece_s[c, rows, lanes] for c in range(2)]
                        numer = [
                            p[0] * change[0] + p[1] * change[1],
                            p[0] * change[1] - p[1] * change[0],
                        ]
                        turned = [
                            piece[0] * change[0] + piece[1] * change[1],
                            piece[0] * change[1] - piece[1] * change[0],
                        ]
                        for c in range(2):
                            grow[c, side, rows, :] = turned[c]
                            here = jnp.where(lane_in[side], numer[c], 0.0)
                            there = numer[c] - here
                            if begin == 0:
                                grow[c, side, SIDE:BAND, :] = turned[c]
                                for total, value in ((numer_own, here), (numer_next, there)):
                                    inside = jnp.where(row_in, value, 0.0)
                                    total[c, rows, lanes] += inside
                                    total[c, SIDE:BAND, lanes] += value - inside
                            else:
                                numer_own[c, rows, lanes] += here
                                numer_next[c, rows, lanes] += there

        def gradient():
            back_left = lax.rem(SIDE - left, SIDE)
            tall = 64
            for c in range(2):
                for start in range(0, SIDE, tall):
                    pair = [grow[c, side, pl.ds(top + start, tall), :] for side in range(2)]
                    value = pltpu.roll(jnp.concatenate(pair, 1), back_left, 1)
                    for side in range(2):
                        begin = (2 * c + side) * SIDE + start
                        grad[begin : begin + tall, :] += value[:, side * HALF : (side + 1) * HALF]

        return [
            turn_probe,
            waves,
            lambda: (sort_amplitudes(), over_rows(0), over_rows(1)),
            lambda: (over_columns(0), over_columns(1)),
            back_columns,
            back_rows,
            changes,
            gradient,
        ]

    lines = [stages(slot) for slot in range(count)]
    for turn in range(len(lines[0]) + LAG * (count - 1)):
        for slot, line in enumerate(lines):
            if 0 <= turn - LAG * slot < len(line):
                line[turn - LAG * slot]()

    weight[...] = 1.0 / weight[...]


def patch_terms(rows, cols, behind, own, halo, probe, amplitudes):
    count = amplitudes.shape[1]
    tables = half_tables()
    vmem = pl.BlockSpec(memory_space=pltpu.VMEM)
    scalars = pl.BlockSpec(memory_space=pltpu.SMEM)
    f32, bf16 = jnp.float32, jnp.bfloat16
    split = pltpu.VMEM((2, SIDE, SIDE), bf16)
    square = pltpu.VMEM((2, SIDE, SIDE), f32)
    member = [
        pltpu.VMEM((2, BAND, HALF), f32),
        pltpu.VMEM((2, 2, BAND, HALF), f32),
        square, square, square,
        pltpu.VMEM((2, 2, BAND, HALF), f32),
        split, split, split, split,
        pltpu.VMEM((SIDE, SIDE), f32),
        pltpu.VMEM((2, SIDE, HALF), f32),
    ]
    return pl.pallas_call(
        patch_kernel,
        in_specs=[scalars, scalars, scalars, vmem, vmem, vmem]
        + [pl.BlockSpec(memory_space=pltpu.HBM)] * 5,
        out_specs=[vmem] * 4,
        out_shape=[
            jax.ShapeDtypeStruct((2, BAND, SIDE), f32),
            jax.ShapeDtypeStruct((2, BAND, SIDE), f32),
            jax.ShapeDtypeStruct((GRAD_ROWS, HALF), f32),
            jax.ShapeDtypeStruct((BAND, SIDE), f32),
        ],
        scratch_shapes=[pltpu.VMEM((SIDE, SIDE), f32), pltpu.VMEM((SIDE, SIDE), bf16)]
        + [split] * 4
        + [
            pltpu.VMEM((count, SIDE, SIDE), f32),
            pltpu.SemaphoreType.DMA((4,)),
            pltpu.SemaphoreType.DMA((count,)),
        ]
        + member * SETS,
        compiler_params=pltpu.CompilerParams(vmem_limit_bytes=VMEM_BYTES),
        cost_estimate=pl.CostEstimate(
            flops=count * 26 * 2 * SIDE**3, bytes_accessed=6 * 2**20, transcendentals=0
        ),
        name="patch_terms",
    )(rows, cols, behind, own, halo, probe, *[jnp.asarray(t) for t in tables], amplitudes)


class Place:
    def __init__(self):
        self.phase, self.space = lax.axis_index("phase"), lax.axis_index("space")
        self.core = lax.rem(self.phase, CORES)
        self.z = lax.rem(self.phase // CORES, Z_SIZE)
        x_lo = self.phase // (CORES * Z_SIZE)
        self.y = lax.rem(self.space, Y_SIZE)
        self.x_hi = self.space // Y_SIZE
        self.x = self.x_hi * X_LO + x_lo

    def device(self, core, z, x, y):
        phase = (lax.rem(x, X_LO) * Z_SIZE + z) * CORES + core
        return (phase, (x // X_LO) * Y_SIZE + y)

    def core_peer(self):
        return self.device(1 - self.core, self.z, self.x, self.y)

    def x_peer(self, k):
        return self.device(self.core, self.z, lax.rem(self.x + k, X_SIZE), self.y)

    def y_peer(self, k):
        return self.device(self.core, self.z, self.x, lax.rem(self.y + k, Y_SIZE))

    def y_mirror(self):
        return self.device(self.core, self.z, self.x, Y_SIZE - 1 - self.y)

    def z_peer(self, k):
        return self.device(self.core, lax.rem(self.z + k, Z_SIZE), self.x, self.y)

    def bin_at(self, k):
        count = lax.axis_size("phase")
        return (lax.rem(self.phase + k + count, count), self.space)

    def tile_at(self, k):
        count = lax.axis_size("space")
        return (self.phase, lax.rem(self.space + k + count, count))


def remote(src, dst, s, v, target):
    return pltpu.make_async_remote_copy(
        src_ref=src, dst_ref=dst, send_sem=s, recv_sem=v,
        device_id=target, device_id_type=pl.DeviceIdType.MESH,
    )


def greet(target):
    pl.semaphore_signal(
        pltpu.get_barrier_semaphore(), inc=1, device_id=target, device_id_type=pl.DeviceIdType.MESH
    )


ROW_CUTS = (0, 136, 272)
CHUNKS = tuple(
    (part, slice(ROW_CUTS[i], ROW_CUTS[i + 1])) for i in range(len(ROW_CUTS) - 1) for part in range(2)
)
EDGE = Y_SIZE


def chunk_of(ref, index):
    part, rows = CHUNKS[index]
    return ref.at[part, pl.ds(rows.start, rows.stop - rows.start), :]


def by_ring(index):
    return CHUNKS[index][0] == 1


def opening_kernel(
    own, split_h, dual_h, rows_h, cols_h,
    halo, steady, behind,
    here, split, dual, start_point, following, preceding, rows, cols, offsets,
    ls, hs, hv, rs, ns, nv, ps, pv, os, ov,
):
    me = Place()
    last = TILES - 1
    count = range(len(CHUNKS))
    loads = [
        pltpu.make_async_copy(src, dst, ls.at[i])
        for i, (src, dst) in enumerate(
            ((rows_h, rows), (cols_h, cols), (own, here), (split_h, split), (dual_h, dual))
        )
    ]
    for load in loads:
        load.start()
    for target in (me.tile_at(1), me.tile_at(-1), me.tile_at(TILES // 2), me.y_mirror()):
        greet(target)
    for target in (me.bin_at(1), me.bin_at(-1)):
        greet(target)

    @pl.when(me.space == 0)
    def _():
        behind[...] = jnp.zeros_like(behind)

    pl.semaphore_wait(pltpu.get_barrier_semaphore(), 6)

    def halo_copy(index):
        target = me.y_peer(Y_SIZE - 1) if by_ring(index) else me.tile_at(-1)
        return remote(chunk_of(own, index), chunk_of(halo, index), hs.at[index], hv.at[index], target)

    def relay(index):
        place = chunk_of(halo, index)
        return remote(place, place, rs.at[index], hv.at[index], me.tile_at(TILES // 2))

    @pl.when(me.space > 0)
    def _():
        for index in count:
            halo_copy(index).start()

    to_preceding = remote(own, following, ns, nv, me.bin_at(-1))
    to_following = remote(start_point, preceding, ps, pv, me.bin_at(1))
    to_preceding.start()
    for load in loads:
        load.wait()
    start_point[...] = here[...] + split[...] - dual[...]
    to_following.start()
    offsets[...] = jnp.zeros_like(offsets)
    offsets[0:1, 0 : rows.shape[1]] = rows[...]
    offsets[1:2, 0 : cols.shape[1]] = cols[...]
    offsets_on = remote(offsets, behind, os, ov, me.tile_at(1))

    @pl.when(me.space < last)
    def _():
        offsets_on.start()

    @pl.when(me.space == last)
    def _():
        for index in count:
            if by_ring(index):
                halo_copy(index).wait_recv()
                relay(index).start()

    to_preceding.wait()
    to_following.wait()
    steady[...] = here[...] - tv_step * (
        (here[...] - preceding[...]) - (following[...] - start_point[...])
    )

    @pl.when(me.space > 0)
    def _():
        offsets_on.wait_recv()
        for index in count:
            halo_copy(index).wait_send()

    @pl.when(me.space < last)
    def _():
        offsets_on.wait_send()
        for index in count:
            halo_copy(index).wait_recv()

    @pl.when(me.space == last)
    def _():
        for index in count:
            if by_ring(index):
                relay(index).wait_send()


def opening(own, split, dual, rows, cols):
    f32, i32 = jnp.float32, jnp.int32
    dma = pltpu.SemaphoreType.DMA
    room = pltpu.VMEM((2, BAND, SIDE), f32)
    many = dma((len(CHUNKS),))
    return pl.pallas_call(
        opening_kernel,
        in_specs=[pl.BlockSpec(memory_space=pltpu.HBM)] * 5,
        out_specs=[
            pl.BlockSpec(memory_space=pltpu.HBM),
            pl.BlockSpec(memory_space=pltpu.VMEM),
            pl.BlockSpec(memory_space=pltpu.VMEM),
        ],
        out_shape=[
            jax.ShapeDtypeStruct((2, BAND, SIDE), f32),
            jax.ShapeDtypeStruct((2, BAND, SIDE), f32),
            jax.ShapeDtypeStruct((8, HALF), i32),
        ],
        scratch_shapes=[
            room, room, room, room, room, room,
            pltpu.VMEM(rows.shape, i32), pltpu.VMEM(cols.shape, i32), pltpu.VMEM((8, HALF), i32),
            dma((5,)), many, many, many, dma, dma, dma, dma, dma, dma,
        ],
        compiler_params=pltpu.CompilerParams(
            collective_id=0, has_side_effects=True, vmem_limit_bytes=VMEM_BYTES
        ),
        cost_estimate=pl.CostEstimate(flops=2**20, bytes_accessed=2**24, transcendentals=0),
        name="opening",
    )(own, split, dual, rows, cols)


def tail_kernel(
    numer_own, numer_next, inverse, term, steady_h,
    updated, next_updated, out,
    steady, inc, r1, a1, r2, a2, r3, r4, a4, f2, f1, f0,
    ls, cs, cv, rs, us, uv,
    s1, v1, s2, v2, s3, v3, s4, v4, s5, v5, s6, v6, s7, v7,
):
    me = Place()
    core, x, y, z = me.core, me.x, me.y, me.z
    last = TILES - 1

    load = pltpu.make_async_copy(steady_h, steady, ls)
    load.start()
    greet(me.core_peer())
    for k in range(1, X_SIZE):
        greet(me.x_peer(k))
    for k in range(1, Y_SIZE):
        greet(me.y_peer(k))
    for target in (me.tile_at(1), me.tile_at(-1), me.bin_at(1), me.bin_at(-1)):
        greet(target)

    def greet_z(k, carry):
        greet(me.z_peer(k))
        return carry

    lax.fori_loop(1, Z_SIZE, greet_z, 0)
    pl.semaphore_wait(
        pltpu.get_barrier_semaphore(), 1 + (X_SIZE - 1) + (Y_SIZE - 1) + 4 + (Z_SIZE - 1)
    )

    def correction(index):
        target = me.y_peer(1) if by_ring(index) else me.tile_at(1)
        return remote(
            chunk_of(numer_next, index), chunk_of(inc, index), cs.at[index], cv.at[index], target
        )

    def relay(index):
        place = chunk_of(inc, index)
        return remote(place, place, rs.at[index], cv.at[index], me.tile_at(TILES // 2))

    def updated_copy(index):
        return remote(
            chunk_of(updated, index), chunk_of(next_updated, index), us.at[index], uv.at[index],
            me.bin_at(-1),
        )

    order = range(len(CHUNKS))
    ringed = [index for index in order if by_ring(index)]

    @pl.when(me.space < last)
    def _():
        for index in order:
            correction(index).start()

    def relay_on(index):
        @pl.when(me.space == 0)
        def _():
            correction(index).wait_recv()
            relay(index).start()

    part1 = GRAD_ROWS // CORES
    part2 = part1 // X_SIZE
    part3 = part2 // Z_SIZE

    def span(index, size):
        return pl.ds(pl.multiple_of(index * size, size), size)

    copy = remote(term.at[span(1 - core, part1)], r1, s1, v1, me.core_peer())
    copy.start()
    copy.wait()
    a1[...] = term[span(core, part1), :] + r1[...]

    copies = []
    for k in range(1, X_SIZE):
        target = lax.rem(x + k, X_SIZE)
        copies.append(
            remote(a1.at[span(target, part2)], r2.at[k - 1], s2.at[k - 1], v2.at[k - 1], me.x_peer(k))
        )
    for copy in copies:
        copy.start()
    relay_on(ringed[0])
    for copy in copies:
        copy.wait()
    a2[...] = a1[span(x, part2), :] + r2[0] + r2[1] + r2[2]

    def z_sum(k):
        target = lax.rem(z + k, Z_SIZE)
        return remote(a2.at[span(target, part3)], r3.at[k - 1], s3.at[k - 1], v3.at[k - 1], me.z_peer(k))

    def start_z_sum(k, carry):
        z_sum(k).start()
        return carry

    def wait_z_sum(k, carry):
        z_sum(k).wait()
        return carry

    lax.fori_loop(1, Z_SIZE, start_z_sum, 0)
    relay_on(ringed[1])
    lax.fori_loop(1, Z_SIZE, wait_z_sum, 0)
    total = a2[span(z, part3), :]
    for k in range(Z_SIZE - 1):
        total = total + r3[k]

    r4[y] = total
    copies = [
        remote(r4.at[y], r4.at[y], s4.at[k - 1], v4.at[k - 1], me.y_peer(k)) for k in range(1, Y_SIZE)
    ]
    for copy in copies:
        copy.start()
    for copy in copies:
        copy.wait()
    count = PATCHES * lax.axis_size("phase") * lax.axis_size("space")
    a4[...] = ((r4[0] + r4[1]) + (r4[2] + r4[3])) * (1.0 / math.sqrt(count))

    f2[span(z, part3), :] = a4[...]

    def z_spread(k):
        return remote(a4, f2.at[span(z, part3)], s5.at[k - 1], v5.at[k - 1], me.z_peer(k))

    def start_z_spread(k, carry):
        z_spread(k).start()
        return carry

    def wait_z_spread(k, carry):
        z_spread(k).wait()
        return carry

    lax.fori_loop(1, Z_SIZE, start_z_spread, 0)
    load.wait()

    for index in order:
        part, rows = CHUNKS[index]

        @pl.when(me.space > 0)
        def _():
            correction(index).wait_recv()
            numer = numer_own[part, rows, :] + inc[part, rows, :]
            updated[part, rows, :] = steady[part, rows, :] + numer * inverse[rows, :]

        @pl.when(me.space == 0)
        def _():
            updated[part, rows, :] = steady[part, rows, :] + numer_own[part, rows, :] * inverse[rows, :]

        updated_copy(index).start()

    lax.fori_loop(1, Z_SIZE, wait_z_spread, 0)

    copies = [
        remote(f2, f1.at[span(x, part2)], s6.at[k - 1], v6.at[k - 1], me.x_peer(k))
        for k in range(1, X_SIZE)
    ]
    for copy in copies:
        copy.start()
    f1[span(x, part2), :] = f2[...]
    for copy in copies:
        copy.wait()

    copy = remote(f1, f0.at[span(core, part1)], s7, v7, me.core_peer())
    copy.start()
    f0[span(core, part1), :] = f1[...]
    copy.wait()
    for c in range(2):
        for side in range(2):
            begin = (2 * c + side) * SIDE
            out[c, :, side * HALF : (side + 1) * HALF] = f0[begin : begin + SIDE, :]

    for index in order:
        updated_copy(index).wait()

    @pl.when(me.space < last)
    def _():
        for index in order:
            correction(index).wait_send()

    @pl.when(me.space == 0)
    def _():
        for index in ringed:
            relay(index).wait_send()


def tail(numer_own, numer_next, inverse, term, steady):
    part1 = GRAD_ROWS // CORES
    part2 = part1 // X_SIZE
    part3 = part2 // Z_SIZE
    f32 = jnp.float32
    dma = pltpu.SemaphoreType.DMA
    vmem = pl.BlockSpec(memory_space=pltpu.VMEM)
    hbm = pl.BlockSpec(memory_space=pltpu.HBM)
    room = pltpu.VMEM((2, BAND, SIDE), f32)
    many = dma((len(CHUNKS),))
    band = jax.ShapeDtypeStruct((2, BAND, SIDE), f32)
    sems = []
    for count in (1, X_SIZE - 1, Z_SIZE - 1, Y_SIZE - 1, Z_SIZE - 1, X_SIZE - 1, 1):
        sems += [dma if count == 1 else dma((count,))] * 2
    return pl.pallas_call(
        tail_kernel,
        in_specs=[vmem, hbm, vmem, vmem, hbm],
        out_specs=[vmem] * 3,
        out_shape=[band, band, jax.ShapeDtypeStruct((2, SIDE, SIDE), f32)],
        scratch_shapes=[
            room, room,
            pltpu.VMEM((part1, HALF), f32),
            pltpu.VMEM((part1, HALF), f32),
            pltpu.VMEM((X_SIZE - 1, part2, HALF), f32),
            pltpu.VMEM((part2, HALF), f32),
            pltpu.VMEM((Z_SIZE - 1, part3, HALF), f32),
            pltpu.VMEM((Y_SIZE, part3, HALF), f32),
            pltpu.VMEM((part3, HALF), f32),
            pltpu.VMEM((part2, HALF), f32),
            pltpu.VMEM((part1, HALF), f32),
            pltpu.VMEM((GRAD_ROWS, HALF), f32),
            dma, many, many, many, many, many,
            *sems,
        ],
        compiler_params=pltpu.CompilerParams(
            collective_id=1, has_side_effects=True, vmem_limit_bytes=VMEM_BYTES
        ),
        cost_estimate=pl.CostEstimate(flops=2**20, bytes_accessed=2**24, transcendentals=0),
        name="tail",
    )(numer_own, numer_next, inverse, term, steady)


def finish_kernel(updated, next_updated, dual, summed, out_object, out_split, out_dual, out_sum):
    out_object[...] = updated[...]
    out_sum[...] = summed[...]
    joint = [next_updated[c] - updated[c] + dual[c] for c in range(2)]
    size_abs = jnp.sqrt(joint[0] * joint[0] + joint[1] * joint[1])
    shrink = jnp.maximum(size_abs - shrink_level, 0.0) / jnp.maximum(size_abs, shrink_level)
    for c in range(2):
        new_split = joint[c] * shrink
        out_split[c] = new_split
        out_dual[c] = joint[c] - new_split


def finish(updated, next_updated, dual, summed):
    steps = 2
    f32 = jnp.float32
    band = pl.BlockSpec((2, BAND // steps, SIDE), lambda i: (0, i, 0))
    grad = pl.BlockSpec((2, SIDE // steps, SIDE), lambda i: (0, i, 0))
    band_shape = jax.ShapeDtypeStruct((2, BAND, SIDE), f32)
    return pl.pallas_call(
        finish_kernel,
        grid=(steps,),
        in_specs=[band, band, band, grad],
        out_specs=[band, band, band, grad],
        out_shape=[band_shape] * 3 + [jax.ShapeDtypeStruct((2, SIDE, SIDE), f32)],
        compiler_params=pltpu.CompilerParams(
            dimension_semantics=("arbitrary",), vmem_limit_bytes=VMEM_BYTES
        ),
        cost_estimate=pl.CostEstimate(flops=2**20, bytes_accessed=2**22, transcendentals=0),
        name="finish",
    )(updated, next_updated, dual, summed)


def shards(object_field, split_field, scaled_dual, probe, amplitudes, row_offsets, col_offsets):
    own = object_field[:, 0]
    split_own = split_field[:, 0]
    dual_own = scaled_dual[:, 0]
    halo, steady, behind = opening(own, split_own, dual_own, row_offsets, col_offsets)
    numer_own, numer_next, grad, inverse = patch_terms(
        row_offsets, col_offsets, behind, own, halo, probe, amplitudes
    )
    updated, next_updated, summed = tail(numer_own, numer_next, inverse, grad, steady)
    updated, new_split, new_dual, probe_gradient = finish(updated, next_updated, dual_own, summed)
    return (updated[:, None], new_split[:, None], new_dual[:, None], probe_gradient)


def solution(mesh):
    in_specs = (
        P(None, "phase", None, "space"),
        P(None, "phase", None, "space"),
        P(None, "phase", None, "space"),
        P(),
        P("phase", "space", None, None),
        P("phase", "space"),
        P("phase", "space"),
    )
    out_specs = (
        P(None, "phase", None, "space"),
        P(None, "phase", None, "space"),
        P(None, "phase", None, "space"),
        P(),
    )
    return jax.shard_map(shards, mesh=mesh, in_specs=in_specs, out_specs=out_specs, check_vma=False)
```
